32 devices in a mesh: gx: 8 (over z, x), gy: 2 (over y), gz: 2 (over core).
Axes of the slice: x: 2, y: 2, z: 4, core: 2. Of those that a mesh axis runs over, the one named last changes fastest.
Arguments:
- source: float32 [256, 64, 1024], P('gx', 'gz', 'gy'), may hold values from -24 to 24
- coef: float32 [256, 64, 32], P('gx', 'gz', 'gy'), may hold values from 0.01 to 0.05
- face_trace: int32 [256, 2, 32], P('gx', 'gz'), may hold values from 0 to 1023, as said below
- near_col: int32 [8, 2, 2], P('gx', 'gz', 'gy'), may hold values from 0 to 15, as said below
- far_col: int32 [8, 2, 2, 7], P('gx', 'gz', 'gy'), may hold values from 0 to 15, as said below
- near_tile: bfloat16 [8, 2, 2, 1024, 1024], P('gx', 'gz', 'gy'), may hold values from -0.1875 to 0.1875
- far_u: bfloat16 [8, 2, 2, 7, 16, 1024], P('gx', 'gz', 'gy'), may hold values from -0.375 to 0.375
- far_v: bfloat16 [8, 2, 2, 7, 16, 1024], P('gx', 'gz', 'gy'), may hold values from -0.1875 to 0.1875
Outputs:
- solution: float32 [256, 64, 1024], P('gx', 'gz', 'gy')
- flux: float32 [256, 2, 1024], P('gx', 'gz', 'gy')
The draws below stay inside these ranges and needn't reach their ends.
Inputs may be any that keep to these rules, and one draw needn't show every extreme that they name: For every block of 32 rows of x and each face s, the entries face_trace(x, s, y) of that block are a permutation of 0 to 1023. For every row block, near_col over the slots j together with far_col over j and k name each column block 0 to 15 exactly once. `far_col`: see near_col: near and far column blocks of a row block together name every column block exactly once.
All inputs are finite; a program needn't handle non-finite values.
Results may differ from the reference program's by a relative error of at most 0.003.
Values may be sent and summed in bfloat16 or wider, within the bound.
No kernel may reach another device: no remote copies, remote signals or barrier semaphores. Data moves between devices by JAX's collectives and lax.ppermute only.
A program may use at most 64 MiB of HBM per device.

```python
import math
import jax
import jax.numpy as jnp
from jax import lax

E = 32
TILE = 1024
RANK = 16
SWEEPS = 3
CX = 32
NX = 256
NY = 32
NZ = 64
NBLK = 16
COLS = 8
FAR = 7
N_GX = 8
N_GY = 2


def column_lists(key):
    keys = jax.random.split(jax.random.fold_in(key, 17), NBLK)
    perms = jax.vmap(lambda k: jax.random.permutation(k, NBLK))(keys).astype(jnp.int32)
    return perms.reshape(NBLK // 2, 2, NBLK // COLS, COLS)


def draw_near_col(key, part):
    return column_lists(key)[..., 0]


def draw_far_col(key, part):
    return column_lists(key)[..., 1:]


def draw_face_trace(key, part):
    keys = jax.random.split(jax.random.fold_in(key, 29), NBLK)
    perms = jax.vmap(lambda k: jax.random.permutation(k, TILE))(keys).astype(jnp.int32)
    return perms.reshape(NBLK // 2, 2, CX, NY).transpose(0, 2, 1, 3).reshape(NX, 2, NY)


def draw_source(key, part):
    subkeys = jax.random.split(jax.random.fold_in(key, 41), 2)
    x_index = jnp.arange(NX, dtype=jnp.int32)[:, None, None, None]
    z_index = jnp.arange(NZ, dtype=jnp.int32)[None, :, None, None]
    y_index = jnp.arange(NY, dtype=jnp.int32)[None, None, :, None]
    parity = (1 - 2 * ((x_index + y_index + z_index) % 2)).astype(jnp.float32)
    envelope = jnp.sin(math.pi * (x_index.astype(jnp.float32) + 0.5) / NX)
    envelope = envelope * jnp.sin(math.pi * (z_index.astype(jnp.float32) + 0.5) / NZ)
    envelope = envelope * jnp.sin(math.pi * (y_index.astype(jnp.float32) + 0.5) / NY)
    polarity = (1 - 2 * jax.random.randint(subkeys[0], (E,), 0, 2)).astype(jnp.float32)
    amplitude = 20.0
    jitter = 0.15 * jnp.clip(jax.random.normal(subkeys[1], (NX, NZ, NY, E), jnp.float32), -3.0, 3.0)
    drawn = amplitude * envelope * parity * polarity + jitter
    return drawn.reshape(NX, NZ, NY * E).astype(jnp.float32)


def steps_of(key, extent, shards, smallest, top_value):
    factor_of = 1.0
    for dim, blocks in shards:
        draws = jax.random.uniform(jax.random.fold_in(jax.random.fold_in(key, 6), dim), (blocks,), jnp.float32, smallest / len(shards), top_value / len(shards))
        factor_of = factor_of * jnp.repeat(jnp.exp(draws), extent[dim] // blocks).reshape((-1,) + (1,) * (len(extent) - 1 - dim))
    return factor_of


def gaussian(own_key, shape, scale, limit, shards=(), held_as=jnp.bfloat16):
    values = jax.random.normal(own_key, shape, jnp.float32) * scale
    if len(shards) > 0:
        values = steps_of(own_key, shape, shards, -0.22, 0.18) * values
    return jnp.clip(values, min=-limit, max=limit).astype(held_as)


def setup_inputs(seed: int = 0) -> dict:
    seeds = jax.random.split(jax.random.key(seed), 9)
    source = draw_source(jax.random.fold_in(seeds[8], 71), 0)
    coef = jnp.clip(jnp.exp(math.log(0.05) - 1.609438 * jax.random.uniform(seeds[1], (NX, NZ, NY), jnp.float32) ** steps_of(seeds[1], (NX, NZ, NY), ((0, 8), (1, 2), (2, 2)), -0.2, 0.2)), 0.01, 0.05)
    face_trace = draw_face_trace(jax.random.fold_in(seeds[8], 71), 0)
    near_col = draw_near_col(jax.random.fold_in(seeds[8], 71), 0)
    far_col = draw_far_col(jax.random.fold_in(seeds[8], 71), 0)
    near_tile = gaussian(seeds[5], (N_GX, 2, N_GY, TILE, TILE), TILE ** -0.5, 0.1875, ((0, 8), (1, 2), (2, 2)))
    far_u = gaussian(seeds[6], (N_GX, 2, N_GY, FAR, RANK, TILE), (RANK * NBLK) ** -0.5, 0.375, ((0, 8), (1, 2), (2, 2)))
    far_v = gaussian(seeds[7], (N_GX, 2, N_GY, FAR, RANK, TILE), TILE ** -0.5, 0.1875, ((0, 8), (1, 2), (2, 2)))
    return {"source": source, "coef": coef, "face_trace": face_trace, "near_col": near_col, "far_col": far_col, "near_tile": near_tile, "far_u": far_u, "far_v": far_v}


def sweep(field, rhs, diag):
    padded = jnp.pad(field, ((1, 1), (1, 1), (0, 0)))
    zeros_rim = jnp.zeros((field.shape[0], field.shape[1], E), field.dtype)
    yplus = jnp.concatenate([field[:, :, E:], zeros_rim], axis=2)
    yminus = jnp.concatenate([zeros_rim, field[:, :, :-E]], axis=2)
    beside = padded[2:, 1:-1] + padded[:-2, 1:-1] + padded[1:-1, 2:] + padded[1:-1, :-2]
    beside = beside + yplus + yminus
    return (rhs + beside) / diag


def reference(source, coef, face_trace, near_col, far_col, near_tile, far_u, far_v):
    diag = jnp.repeat(6.0 + coef, E, axis=2)
    field = jnp.zeros(source.shape, source.dtype)
    for step in range(SWEEPS):
        field = sweep(field, source, diag)
    facevalue = jnp.stack([field[:, 0, :], field[:, NZ - 1, :]], axis=1).astype(jnp.bfloat16)
    blocks = facevalue.reshape(NBLK // 2, CX, 2, NY, E).transpose(0, 2, 1, 3, 4).reshape(NBLK, TILE, E)
    perms = face_trace.reshape(NBLK // 2, CX, 2, NY).transpose(0, 2, 1, 3).reshape(NBLK, TILE).astype(jnp.int32)
    rowids = jnp.arange(NBLK, dtype=jnp.int32)[:, None]
    traces = jnp.zeros((NBLK, TILE, E), jnp.bfloat16).at[rowids, perms].set(blocks)

    near_all = near_tile.reshape(NBLK, N_GY, TILE, TILE)
    u_all = far_u.reshape(NBLK, N_GY, FAR, RANK, TILE)
    v_all = far_v.reshape(NBLK, N_GY, FAR, RANK, TILE)
    ncol_all = near_col.reshape(NBLK, N_GY).astype(jnp.int32)
    fcol_all = far_col.reshape(NBLK, N_GY, FAR).astype(jnp.int32)

    def one_row(items):
        tiles, ufac, vfac, ncol, fcol = items
        near_traces = traces[ncol]
        nearpart = jnp.einsum('gij,gje->ie', tiles.astype(jnp.float32), near_traces.astype(jnp.float32))
        far_traces = traces[fcol]
        weights = jnp.einsum('gfrt,gfte->gfre', vfac.astype(jnp.float32), far_traces.astype(jnp.float32)).astype(jnp.bfloat16)
        farpart = jnp.einsum('gfrt,gfre->te', ufac.astype(jnp.float32), weights.astype(jnp.float32))
        return nearpart + farpart

    rows = lax.map(one_row, (near_all, u_all, v_all, ncol_all, fcol_all))
    picked = jnp.take_along_axis(rows, perms[:, :, None], axis=1)
    flux = picked.reshape(NBLK // 2, 2, CX, NY, E).transpose(0, 2, 1, 3, 4).reshape(NX, 2, NY * E)
    rhs = source.at[:, 0, :].add(flux[:, 0, :]).at[:, NZ - 1, :].add(flux[:, 1, :])
    solution = sweep(field, rhs, diag)
    return solution, flux
```

```python
import functools

import jax
import jax.numpy as jnp
from jax import lax
from jax.experimental import pallas as pl
from jax.experimental.pallas import tpu as pltpu
from jax.sharding import PartitionSpec as P

E = 32
LANES = 128
ROWS = 8
HALO = 3
VMEM_BYTES = 56 * 1024 * 1024


def roll(value, shift, axis):
    return pltpu.roll(value, shift % value.shape[axis], axis)


def lane_ids(value):
    return lax.broadcasted_iota(jnp.int32, value.shape, value.ndim - 1)


def call(kernel, ids, operands, out_shape, in_specs=None, out_specs=None, scratch=(), flops=0, **kw):
    whole = lambda a: pl.BlockSpec(a.shape, lambda i, ids, n=len(a.shape): (0,) * n)
    if in_specs is None:
        in_specs = [None] * len(operands)
    in_specs = [whole(a) if spec is None else spec for a, spec in zip(operands, in_specs)]
    if out_specs is None:
        out_specs = [whole(a) for a in out_shape]
    moved = sum(a.size * a.dtype.itemsize for a in (*operands, *out_shape))
    return pl.pallas_call(
        kernel,
        out_shape=out_shape,
        grid_spec=pltpu.PrefetchScalarGridSpec(
            num_scalar_prefetch=1,
            grid=(1,),
            in_specs=in_specs,
            out_specs=out_specs,
            scratch_shapes=list(scratch),
        ),
        compiler_params=pltpu.CompilerParams(vmem_limit_bytes=VMEM_BYTES),
        cost_estimate=pl.CostEstimate(flops=flops, bytes_accessed=moved, transcendentals=0),
        **kw,
    )(ids, *operands)


def pairs(count):
    first = [(i, i ^ 1) for i in range(count)]
    second = [(i, i + 1) for i in range(1, count - 1, 2)]
    return first, second + [(b, a) for a, b in second]


def swap(messages, axis):
    count = lax.axis_size(axis)
    return [lax.ppermute(m, axis, p) for m, p in zip(messages, pairs(count))]


def message_count(axis):
    return 1 if lax.axis_size(axis) == 2 else 2


def choose(odd, low, high, number):
    return jnp.where(odd == number, high, low)


def from_low(odd, received):
    other = received[1] if len(received) == 2 else jnp.zeros_like(received[0])
    return jnp.where(odd == 1, received[0], other)


def from_high(odd, received):
    other = received[1] if len(received) == 2 else jnp.zeros_like(received[0])
    return jnp.where(odd == 1, other, received[0])


def spread_matrix(cells, width):
    k = lax.broadcasted_iota(jnp.int32, (LANES, width), 0)
    cell = lax.broadcasted_iota(jnp.int32, (LANES, width), 1) // E
    part = k // 32
    hit = (k - part * 32 == cell) & (part < 3) & (cell < cells)
    return jnp.where(hit, 1.0, 0.0).astype(jnp.bfloat16)


def spread(compact, width, cells):
    compact = jnp.where(lane_ids(compact) < cells, compact, 0.0)
    high = compact.astype(jnp.bfloat16).astype(jnp.float32)
    rest = compact - high
    middle = rest.astype(jnp.bfloat16).astype(jnp.float32)
    low = (rest - middle).astype(jnp.bfloat16).astype(jnp.float32)
    packed = high + roll(middle, 32, 1) + roll(low, 64, 1)
    return jnp.dot(
        packed.astype(jnp.bfloat16), spread_matrix(cells, width), preferred_element_type=jnp.float32
    )


def face_start_kernel(ids, src, inv, s_out, i_out, *messages):
    odd, side = ids[0] % 2, ids[2]
    rows_x, _, width = src.shape
    cells = width // E
    planes = []
    for d in range(3):
        s = jnp.where(side == 0, src[:, d, :], src[:, ROWS - 1 - d, :])
        c = jnp.where(side == 0, inv[:, d, :], inv[:, ROWS - 1 - d, :])
        i = spread(c, width, cells)
        s_out[d], i_out[d] = s, i
        planes.append((s, i))
    for number, message in enumerate(messages):
        for d in range(2):
            for k in range(2):
                v = planes[d][k]
                row = 4 * k + 2 * d
                message[row : row + 2, :] = choose(odd, v[:2], v[rows_x - 2 :], number)


def edge_pair(s, i):
    lane = lane_ids(s[:, :LANES])
    low = jnp.where(lane < 2 * E, s[:, :LANES], roll(i[:, :LANES], 64, 1))
    high = jnp.where(lane < 2 * E, roll(s[:, -LANES:], 64, 1), i[:, -LANES:])
    return low, high


def face_side_kernel(nx, ids, s_in, i_in, *refs):
    odd_x, odd_y = ids[0] % 2, ids[1] % 2
    got, messages = [r[...] for r in refs[:nx]], refs[nx:]
    rows_x = s_in.shape[1]
    below, above = from_low(odd_x, got), from_high(odd_x, got)
    pick = lax.broadcasted_iota(jnp.int32, below.shape, 0)
    s = jnp.where(pick == 0, roll(below, -1, 0), roll(above, 1, 0))
    i = jnp.where(pick == 0, roll(below, -5, 0), roll(above, -3, 0))
    s, i = (jnp.where(pick < 2, v, 0.0) for v in (s, i))
    parts = [edge_pair(s_in[0], i_in[0]), edge_pair(s_in[1], i_in[1]), edge_pair(s, i)]
    for number, message in enumerate(messages):
        row = 0
        for low, high in parts:
            message[row : row + low.shape[0], :] = choose(odd_y, low, high, number)
            row += low.shape[0]


def face_sweep_kernel(nx, ny, ids, s_in, i_in, *refs):
    odd_x, odd_y = ids[0] % 2, ids[1] % 2
    got_x = [r[...] for r in refs[:nx]]
    got_y = [r[...] for r in refs[nx : nx + ny]]
    out, ext_s, ext_i = refs[nx + ny :]
    _, rows_x, width = s_in.shape
    below, above = from_low(odd_x, got_x), from_high(odd_x, got_x)
    left, right = from_low(odd_y, got_y), from_high(odd_y, got_y)
    lane = lane_ids(left)
    pad_s = jnp.where(lane < 2 * E, right, roll(left, 64, 1))
    pad_i = jnp.where(lane < 2 * E, roll(right, 64, 1), left)
    ext_s[...] = jnp.zeros(ext_s.shape, jnp.float32)
    ext_i[...] = jnp.zeros(ext_i.shape, jnp.float32)
    first, last = ROWS, ROWS + rows_x
    for ext, own, pad, k in ((ext_s, s_in, pad_s, 0), (ext_i, i_in, pad_i, 1)):
        for d in range(2):
            row = 4 * k + 2 * d
            ext[d, first:last, :width] = own[d]
            ext[d, first - 2 : first, :width] = below[row : row + 2]
            ext[d, last : last + 2, :width] = above[row : row + 2]
            ext[d, first:last, width:] = pad[d * rows_x : (d + 1) * rows_x]
        ext[0, first - 1 : first, width:] = pad[2 * rows_x : 2 * rows_x + 1]
        ext[0, last : last + 1, width:] = pad[2 * rows_x + 1 : 2 * rows_x + 2]

    def around(u):
        return roll(u, 1, 0) + roll(u, -1, 0) + roll(u, E, 1) + roll(u, -E, 1)

    s0, s1, i0, i1 = ext_s[0], ext_s[1], ext_i[0], ext_i[1]
    u0, u1 = s0 * i0, s1 * i1
    deep = s_in[2] * i_in[2]
    v0 = (s0 + (around(u0) + u1)) * i0
    own = (around(u1) + u0)[first:last, :width]
    v1 = (s_in[1] + (own + deep)) * i_in[1]
    face = (s_in[0] + (around(v0)[first:last, :width] + v1)) * i_in[0]
    pieces = []
    for cell in range(width // E):
        start = cell * E // LANES * LANES
        pieces.append(roll(face[:, start : start + LANES], -(cell * E - start), 1))
    stacked = jnp.concatenate(pieces, axis=0)
    out[...] = stacked.T[:E].astype(jnp.bfloat16)


def order_kernel(ids, place, out):
    trace = lax.broadcasted_iota(jnp.int32, out.shape, 1)
    out[...] = jnp.where(place[...] == trace, 1.0, 0.0).astype(jnp.bfloat16)


def trace_kernel(ids, *refs):
    order, out = refs[-2:]
    if len(refs) == 3:
        face = refs[0][...]
    else:
        own, other = refs[0][...], refs[1][...]
        first = ids[1] == 0
        face = jnp.concatenate(
            [jnp.where(first, own, other), jnp.where(first, other, own)], axis=1
        )
    out[...] = jnp.dot(face, order[...], preferred_element_type=jnp.float32).astype(jnp.bfloat16)


ACROSS = (((1,), (1,)), ((), ()))


def operator_kernel(halves, ids, wanted, traces, near, far_v, far_u, order, *outs):
    count = wanted.shape[0] - 1
    rank = far_v.shape[0] // count
    across = functools.partial(
        lax.dot_general, dimension_numbers=ACROSS, preferred_element_type=jnp.float32
    )
    rows = across(traces[wanted[0]], near[...])
    far = jnp.concatenate([traces[wanted[1 + k]] for k in range(count)], axis=0)
    products = across(far, far_v[...])
    group = lax.broadcasted_iota(jnp.int32, (E, count * rank), 1) // rank
    weights = jnp.zeros((E, count * rank), jnp.float32)
    for k in range(count):
        weights = jnp.where(group == k, products[k * E : (k + 1) * E], weights)
    rows = rows + jnp.dot(
        weights.astype(jnp.bfloat16), far_u[...], preferred_element_type=jnp.float32
    )
    high = rows.astype(jnp.bfloat16)
    rest = rows - high.astype(jnp.float32)
    middle = rest.astype(jnp.bfloat16)
    low = (rest - middle.astype(jnp.float32)).astype(jnp.bfloat16)
    placed = across(jnp.concatenate([high, middle, low], axis=0), order[...])
    placed = placed[:E] + (placed[E : 2 * E] + placed[2 * E :])
    if halves:
        half = placed.shape[1] // 2
        first = ids[1] == 0
        outs[0][...] = jnp.where(first, placed[:, :half], placed[:, half:])
        outs[1][...] = jnp.where(first, placed[:, half:], placed[:, :half])
    else:
        outs[0][...] = placed


def finish_kernel(count, ids, *refs):
    parts, (inv, field, flux_out, out) = refs[:count], refs[count:]
    side = ids[2]
    rows_x, _, width = out.shape
    total = parts[0][...]
    if count == 2:
        total = total + parts[1][...]
    wide = jnp.concatenate([total, jnp.zeros((LANES - E, total.shape[1]), jnp.float32)], axis=0).T
    columns = []
    for start in range(0, width // E, LANES // E):
        column = wide[start * rows_x : (start + 1) * rows_x]
        for k in range(1, LANES // E):
            column = column + roll(wide[(start + k) * rows_x : (start + k + 1) * rows_x], k * E, 1)
        columns.append(column)
    flux = jnp.concatenate(columns, axis=1)
    flux_out[...] = flux
    added = (flux * inv[0])[:, None, :]
    row = lax.broadcasted_iota(jnp.int32, out.shape, 1)
    out[...] = field[...] + jnp.where(row == side * (ROWS - 1), added, 0.0)


def side_edge_kernel(ids, *refs):
    ny = len(refs) // 3
    odd = ids[1] % 2
    cells = 16
    inv = refs[ny]
    for number in range(ny):
        edge, message = refs[number], refs[ny + 1 + number]
        s, c = edge[...], inv[...]
        lane = lane_ids(s)
        width = HALO * E
        low = jnp.where(lane < width, s, roll(c, width, 2))
        high = jnp.where(lane < width, roll(s, width, 2), roll(c, width - (cells - HALO), 2))
        message[...] = choose(odd, low, high, number)


def widen(cells, ring, s, c, left, right):
    lane = lane_ids(right)
    width = HALO * E
    axis = right.ndim - 1
    zero = jnp.zeros_like(right)
    after = jnp.where(lane < width, right, zero)
    before = jnp.where(lane >= LANES - width, roll(left, LANES - width, axis), zero)
    pads = [after + before] if ring - cells == LANES // E else [after, before]
    own = jnp.where(lane < cells, c, zero)
    c_after = jnp.where((lane >= cells) & (lane < cells + HALO), roll(right, cells - width, axis), zero)
    c_before = jnp.where(
        (lane >= ring - HALO) & (lane < ring), roll(left, ring - HALO - width, axis), zero
    )
    return [s, *pads], own + c_after + c_before


def row_edge_kernel(cells, ring, ny, nx, ids, *refs):
    odd_x, odd_y = ids[0] % 2, ids[1] % 2
    s_low, s_high, c_low, c_high = refs[:4]
    y_low, y_high = refs[4 : 4 + ny], refs[4 + ny : 4 + 2 * ny]
    messages = refs[4 + 2 * ny :]
    block = s_low.shape[0]
    for k in range(HALO):
        sides = []
        for s, c, y, row in ((s_low, c_low, y_low, k), (s_high, c_high, y_high, block - HALO + k)):
            got = [r[row] for r in y]
            parts, compact = widen(
                cells, ring, s[row], c[row], from_low(odd_y, got), from_high(odd_y, got)
            )
            sides.append(jnp.concatenate([*parts, compact], axis=1))
        for number, message in enumerate(messages):
            message[k] = choose(odd_x, sides[0], sides[1], number)


def depth_edge_kernel(cells, ring, ny, nx, ids, s, c, *refs):
    odd_x, odd_y = ids[0] % 2, ids[1] % 2
    got_y, got_x, out = refs[:ny], refs[ny : ny + nx], refs[-1]
    rows_x = s.shape[0]
    got = [r[...] for r in got_y]
    parts, compact = widen(cells, ring, s[...], c[...], from_low(odd_y, got), from_high(odd_y, got))
    out[HALO : HALO + rows_x] = jnp.concatenate([*parts, compact], axis=2)
    got = [r[...] for r in got_x]
    out[:HALO] = from_low(odd_x, got)
    out[HALO + rows_x :] = from_high(odd_x, got)


def volume_kernel(cells, ring, ny, nx, ids, s, c, *refs):
    odd_x, odd_y, side = ids[0] % 2, ids[1] % 2, ids[2]
    got_y, got_x, got_z = refs[:ny], refs[ny : ny + nx], refs[ny + nx]
    out, ext_s, ext_i, one, two = refs[ny + nx + 1 :]
    rows_x, depth, width = s.shape
    wide = ring * E
    all_x = rows_x + 2 * HALO

    def place(x, parts, compact):
        row = lax.broadcasted_iota(jnp.int32, (ROWS, LANES), 0)
        zone = got_z[x]
        start = side * (ROWS - HALO)
        near = (row >= start) & (row < start + HALO)
        lanes = jnp.where(near, zone[:, wide:], 0.0)
        inverse = spread(jnp.concatenate([compact, lanes], axis=0), wide, ring)
        body = jnp.concatenate([jnp.concatenate(parts, axis=1), zone[:, :wide]], axis=0)
        ext_s[x] = body
        ext_i[x] = inverse
        one[x] = body * inverse

    def own(x, _):
        got = [r[x] for r in got_y]
        parts, compact = widen(cells, ring, s[x], c[x], from_low(odd_y, got), from_high(odd_y, got))
        place(x + HALO, parts, compact)
        return 0

    lax.fori_loop(0, rows_x, own, 0)
    for k in range(HALO):
        got = [r[k] for r in got_x]
        below, above = from_low(odd_x, got), from_high(odd_x, got)
        place(k, [below[:, :wide]], below[:, wide:])
        place(rows_x + HALO + k, [above[:, :wide]], above[:, wide:])

    def swept(old, x):
        u = old[x]
        beside = old[x - 1] + old[x + 1]
        beside = beside + (roll(u, 1, 0) + roll(u, -1, 0)) + (roll(u, E, 1) + roll(u, -E, 1))
        return (ext_s[x] + beside) * ext_i[x]

    def second(x, _):
        two[x] = swept(one, x)
        return 0

    def third(x, _):
        one[x] = swept(two, x)
        return 0

    def last(x, _):
        out[x - HALO] = swept(one, x)[:depth, :width]
        return 0

    lax.fori_loop(1, all_x - 1, second, 0)
    lax.fori_loop(2, all_x - 2, third, 0)
    lax.fori_loop(3, all_x - 3, last, 0)


def float_like(shape, dtype=jnp.float32):
    return jax.ShapeDtypeStruct(shape, dtype)


def body(source, coef, face_trace, near_col, far_col, near_tile, far_u, far_v):
    rows_x, depth, width = source.shape
    cells = coef.shape[2]
    groups = lax.axis_size("gy")
    size_x = lax.axis_size("gx")
    tile = near_tile.shape[3]
    count = far_u.shape[3]
    rank = far_u.shape[4]
    nx, ny = message_count("gx"), message_count("gy")
    at_x, at_y, at_z = (lax.axis_index(a).astype(jnp.int32) for a in ("gx", "gy", "gz"))
    ids = jnp.stack([at_x, at_y, at_z])
    slabs = depth // ROWS
    f32, bf16 = jnp.float32, jnp.bfloat16
    inv = jnp.pad(1.0 / (6.0 + coef), ((0, 0), (0, 0), (0, LANES - cells)))

    slab = lambda n: pl.BlockSpec((rows_x, ROWS, n), lambda i, ids: (0, ids[2] * (slabs - 1), 0))
    planes = float_like((3, rows_x, width))
    s_face, i_face, *out_x = call(
        face_start_kernel, ids, (source, inv),
        [planes, planes] + [float_like((ROWS, width))] * nx,
        in_specs=[slab(width), slab(LANES)],
    )
    got_x = swap(out_x, "gx")
    out_y = call(
        functools.partial(face_side_kernel, nx), ids, (s_face, i_face, *got_x),
        [float_like((2 * rows_x + ROWS, LANES))] * ny,
    )
    got_y = swap(out_y, "gy")
    ext = pltpu.VMEM((2, rows_x + 2 * ROWS, width + LANES), f32)
    part = rows_x * cells
    (face,) = call(
        functools.partial(face_sweep_kernel, nx, ny), ids, (s_face, i_face, *got_x, *got_y),
        [float_like((E, part), bf16)], scratch=(ext, ext),
    )

    place = face_trace.reshape(rows_x, cells * groups).T.reshape(tile, 1)
    (order,) = call(order_kernel, ids, (place,), [float_like((tile, tile), bf16)])
    if groups == 2:
        faces = (face, lax.ppermute(face, "gy", [(0, 1), (1, 0)]))
    else:
        faces = (lax.all_gather(face, "gy", axis=1, tiled=True),)
    (traces,) = call(
        trace_kernel, ids, (*faces, order), [float_like((E, tile), bf16)], flops=2 * E * tile * tile
    )
    traces = traces[None]
    steps = []
    step = size_x // 2
    while step:
        other = lax.ppermute(traces, "gx", [(i, i ^ step) for i in range(size_x)])
        traces = jnp.concatenate([traces, other], axis=0)
        steps.append(step)
        step //= 2
    other = lax.ppermute(traces, "gz", [(0, 1), (1, 0)])
    traces = jnp.concatenate([traces, other], axis=0)
    wanted = jnp.concatenate([near_col.reshape(1), far_col.reshape(count)])
    apart = (wanted // 2) ^ at_x
    spot = ((wanted % 2) ^ at_z) * size_x
    for n, step in enumerate(steps):
        spot = spot + jnp.where(apart & step > 0, 1 << n, 0)

    halves = groups == 2
    smem = pl.BlockSpec(memory_space=pltpu.SMEM)
    rows = call(
        functools.partial(operator_kernel, halves), ids,
        (spot, traces, near_tile.reshape(tile, tile), far_v.reshape(count * rank, tile),
         far_u.reshape(count * rank, tile), order),
        [float_like((E, part))] * 2 if halves else [float_like((E, tile))],
        in_specs=[smem] + [None] * 5, flops=8 * E * tile * tile,
    )
    if halves:
        rows = (rows[0], lax.ppermute(rows[1], "gy", [(0, 1), (1, 0)]))
    else:
        rows = (lax.psum_scatter(rows[0], "gy", scatter_dimension=1, tiled=True),)

    pad = LANES if groups == 2 else 2 * LANES
    ring = (width + pad) // E
    wide = width + pad
    blocks = width // LANES
    edge_at = lambda n: lambda i, ids: (0, 0, jnp.where(ids[1] % 2 == n, blocks - 1, 0))
    out_y = call(
        side_edge_kernel, ids, (*[source] * ny, inv), [float_like((rows_x, depth, LANES))] * ny,
        in_specs=[pl.BlockSpec((rows_x, depth, LANES), edge_at(n)) for n in range(ny)] + [None],
    )
    vol_y = swap(out_y, "gy")
    quad = lambda n, at: pl.BlockSpec((4, depth, n), lambda i, ids: (at, 0, 0))
    top = rows_x // 4 - 1
    out_x = call(
        functools.partial(row_edge_kernel, cells, ring, ny, nx), ids,
        (source, source, inv, inv, *vol_y, *vol_y),
        [float_like((HALO, depth, wide + LANES))] * nx,
        in_specs=[quad(width, 0), quad(width, top), quad(LANES, 0), quad(LANES, top)]
        + [quad(LANES, 0)] * ny + [quad(LANES, top)] * ny,
    )
    vol_x = swap(out_x, "gx")
    all_x = rows_x + 2 * HALO
    inner = lambda x, n: pl.BlockSpec(
        (x, ROWS, n), lambda i, ids: (0, (1 - ids[2]) * (slabs - 1), 0)
    )
    (out_z,) = call(
        functools.partial(depth_edge_kernel, cells, ring, ny, nx), ids,
        (source, inv, *vol_y, *vol_x), [float_like((all_x, ROWS, wide + LANES))],
        in_specs=[inner(rows_x, width), inner(rows_x, LANES)] + [inner(rows_x, LANES)] * ny
        + [inner(HALO, wide + LANES)] * nx,
    )
    vol_z = lax.ppermute(out_z, "gz", [(0, 1), (1, 0)])
    ext = pltpu.VMEM((all_x, depth + ROWS, wide), f32)
    (field,) = call(
        functools.partial(volume_kernel, cells, ring, ny, nx), ids,
        (source, inv, *vol_y, *vol_x, vol_z), [float_like(source.shape)], scratch=(ext,) * 4,
    )

    plane = pl.BlockSpec((1, rows_x, width), lambda i, ids: (0, 0, 0))
    flux, result = call(
        functools.partial(finish_kernel, len(rows)), ids, (*rows, i_face, field),
        [float_like((rows_x, width)), float_like(source.shape)],
        in_specs=[None] * len(rows) + [plane, slab(width)],
        out_specs=[pl.BlockSpec((rows_x, width), lambda i, ids: (0, 0)), slab(width)],
        input_output_aliases={len(rows) + 2: 1},
    )
    return (result, flux[:, None, :])


def solution(mesh):
    return jax.shard_map(
        body,
        mesh=mesh,
        in_specs=(
            P("gx", "gz", "gy"),
            P("gx", "gz", "gy"),
            P("gx", "gz", None),
            P("gx", "gz", "gy"),
            P("gx", "gz", "gy", None),
            P("gx", "gz", "gy", None, None),
            P("gx", "gz", "gy", None, None, None),
            P("gx", "gz", "gy", None, None, None),
        ),
        out_specs=(P("gx", "gz", "gy"), P("gx", "gz", "gy")),
        check_vma=False,
    )
```

```python
import functools
import math

import jax
import jax.numpy as jnp
from jax import lax
from jax.experimental import pallas as pl
from jax.experimental.pallas import tpu as pltpu
from jax.sharding import PartitionSpec as P

E = 32
LANES = 128
ROWS = 8
HALO = 3


def roll(value, shift, axis):
    return pltpu.roll(value, shift % value.shape[axis], axis)


def lane_ids(value):
    return lax.broadcasted_iota(jnp.int32, value.shape, value.ndim - 1)


def held(value):
    return pltpu.with_memory_space_constraint(value, pltpu.VMEM)


VECTOR = pl.BlockSpec(memory_space=pltpu.VMEM)
SCALAR = pl.BlockSpec(memory_space=pltpu.SMEM)
PLACED = pl.BlockSpec(memory_space=pl.ANY)


def vector(shape, dtype=jnp.float32):
    return pltpu.VMEM(shape, dtype)


def plain(shape, dtype=jnp.float32):
    return jax.ShapeDtypeStruct(shape, dtype)


def size_of(a):
    return math.prod(a.shape) * jnp.dtype(a.dtype).itemsize


def call(kernel, operands, out_shape, in_specs=None, out_specs=None, scratch=(), room=8, work=1000, **kw):
    return pl.pallas_call(
        kernel,
        out_shape=out_shape,
        in_specs=in_specs or [VECTOR] * len(operands),
        out_specs=out_specs or [VECTOR] * len(out_shape),
        scratch_shapes=list(scratch),
        compiler_params=pltpu.CompilerParams(vmem_limit_bytes=room * 1024 * 1024),
        cost_estimate=pl.CostEstimate(flops=0, bytes_accessed=work * 3000, transcendentals=0),
        **kw,
    )(*operands)


def index(axis):
    return lax.axis_index(axis).astype(jnp.int32)


def pairs(count):
    first = [(i, i ^ 1) for i in range(count)]
    second = [(i, i + 1) for i in range(1, count - 1, 2)]
    return first, second + [(b, a) for a, b in second]


def swap(messages, axis):
    count = lax.axis_size(axis)
    return [held(lax.ppermute(m, axis, p)) for m, p in zip(messages, pairs(count))]


def doubling(count):
    steps = []
    while count > 1:
        count //= 2
        steps.append(count)
    return steps


def message_count(axis):
    return 1 if lax.axis_size(axis) == 2 else 2


def choose(odd, low, high, number):
    return jnp.where(odd == number, high, low)


def from_low(odd, received):
    other = received[1] if len(received) == 2 else jnp.zeros_like(received[0])
    return jnp.where(odd == 1, received[0], other)


def from_high(odd, received):
    other = received[1] if len(received) == 2 else jnp.zeros_like(received[0])
    return jnp.where(odd == 1, other, received[0])


def spread_matrix(cells, width):
    k = lax.broadcasted_iota(jnp.int32, (LANES, width), 0)
    cell = lax.broadcasted_iota(jnp.int32, (LANES, width), 1) // E
    part = k // 32
    hit = (k - part * 32 == cell) & (part < 3) & (cell < cells)
    return jnp.where(hit, 1.0, 0.0).astype(jnp.bfloat16)


def packed(compact, cells):
    compact = jnp.where(lane_ids(compact) < cells, compact, 0.0)
    high = compact.astype(jnp.bfloat16).astype(jnp.float32)
    rest = compact - high
    middle = rest.astype(jnp.bfloat16).astype(jnp.float32)
    low = (rest - middle).astype(jnp.bfloat16).astype(jnp.float32)
    axis = compact.ndim - 1
    return (high + roll(middle, 32, axis) + roll(low, 64, axis)).astype(jnp.bfloat16)


def spread(compact, width, cells):
    return jnp.dot(
        packed(compact, cells), spread_matrix(cells, width), preferred_element_type=jnp.float32
    )


def face_start_kernel(src, coef, inv, s_out, i_out, *messages):
    odd, side = index("gx") % 2, index("gz")
    rows_x, depth, width = src.shape
    cells = width // E
    c = jnp.swapaxes(1.0 / (6.0 + coef[...]), 1, 2)
    inv[...] = jnp.concatenate(
        [c, jnp.zeros((rows_x, depth, LANES - cells), jnp.float32)], axis=2
    )
    planes = []
    for d in range(3):
        s = jnp.where(side == 0, src[:, d, :], src[:, depth - 1 - d, :])
        i = jnp.where(side == 0, inv[:, d, :], inv[:, depth - 1 - d, :])
        planes.append([s, i])
    spreads = spread(jnp.concatenate([i for _, i in planes], axis=0), width, cells)
    for d in range(3):
        planes[d][1] = spreads[d * rows_x : (d + 1) * rows_x]
        s_out[d], i_out[d] = planes[d]
    for number, message in enumerate(messages):
        for d in range(2):
            for k in range(2):
                v = planes[d][k]
                row = 4 * k + 2 * d
                message[row : row + 2, :] = choose(odd, v[:2], v[rows_x - 2 :], number)


def edge_pair(s, i):
    lane = lane_ids(s[:, :LANES])
    low = jnp.where(lane < 2 * E, s[:, :LANES], roll(i[:, :LANES], 64, 1))
    high = jnp.where(lane < 2 * E, roll(s[:, -LANES:], 64, 1), i[:, -LANES:])
    return low, high


def face_side_kernel(nx, s_in, i_in, *refs):
    odd_x, odd_y = index("gx") % 2, index("gy") % 2
    got, messages = [r[...] for r in refs[:nx]], refs[nx:]
    rows_x = s_in.shape[1]
    below, above = from_low(odd_x, got), from_high(odd_x, got)
    pick = lax.broadcasted_iota(jnp.int32, below.shape, 0)
    s = jnp.where(pick == 0, roll(below, -1, 0), roll(above, 1, 0))
    i = jnp.where(pick == 0, roll(below, -5, 0), roll(above, -3, 0))
    s, i = (jnp.where(pick < 2, v, 0.0) for v in (s, i))
    parts = [edge_pair(s_in[0], i_in[0]), edge_pair(s_in[1], i_in[1]), edge_pair(s, i)]
    for number, message in enumerate(messages):
        row = 0
        for low, high in parts:
            message[row : row + low.shape[0], :] = choose(odd_y, low, high, number)
            row += low.shape[0]


def face_sweep_kernel(nx, ny, s_in, i_in, *refs):
    odd_x, odd_y = index("gx") % 2, index("gy") % 2
    got_x = [r[...] for r in refs[:nx]]
    got_y = [r[...] for r in refs[nx : nx + ny]]
    out, ext_s, ext_i = refs[nx + ny :]
    _, rows_x, width = s_in.shape
    below, above = from_low(odd_x, got_x), from_high(odd_x, got_x)
    left, right = from_low(odd_y, got_y), from_high(odd_y, got_y)
    lane = lane_ids(left)
    pad_s = jnp.where(lane < 2 * E, right, roll(left, 64, 1))
    pad_i = jnp.where(lane < 2 * E, roll(right, 64, 1), left)
    ext_s[...] = jnp.zeros(ext_s.shape, jnp.float32)
    ext_i[...] = jnp.zeros(ext_i.shape, jnp.float32)
    first, last = ROWS, ROWS + rows_x
    for ext, own, pad, k in ((ext_s, s_in, pad_s, 0), (ext_i, i_in, pad_i, 1)):
        for d in range(2):
            row = 4 * k + 2 * d
            ext[d, first:last, :width] = own[d]
            ext[d, first - 2 : first, :width] = below[row : row + 2]
            ext[d, last : last + 2, :width] = above[row : row + 2]
            ext[d, first:last, width:] = pad[d * rows_x : (d + 1) * rows_x]
        ext[0, first - 1 : first, width:] = pad[2 * rows_x : 2 * rows_x + 1]
        ext[0, last : last + 1, width:] = pad[2 * rows_x + 1 : 2 * rows_x + 2]

    def around(u):
        return roll(u, 1, 0) + roll(u, -1, 0) + roll(u, E, 1) + roll(u, -E, 1)

    s0, s1, i0, i1 = ext_s[0], ext_s[1], ext_i[0], ext_i[1]
    u0, u1 = s0 * i0, s1 * i1
    deep = s_in[2] * i_in[2]
    v0 = (s0 + (around(u0) + u1)) * i0
    own = (around(u1) + u0)[first:last, :width]
    v1 = (s_in[1] + (own + deep)) * i_in[1]
    face = (s_in[0] + (around(v0)[first:last, :width] + v1)) * i_in[0]
    pieces = []
    for cell in range(width // E):
        start = cell * E // LANES * LANES
        pieces.append(roll(face[:, start : start + LANES], -(cell * E - start), 1))
    stacked = jnp.concatenate(pieces, axis=0)
    out[...] = stacked.T[:E].astype(jnp.bfloat16)


def order_kernel(place, near_col, far_col, order, spot):
    rows_x, _, cells_y = place.shape
    at = place[...].reshape(rows_x, cells_y) if rows_x == 1 else place[:, 0, :]
    trace = lax.broadcasted_iota(jnp.int32, (rows_x, order.shape[1]), 1)
    for y in range(cells_y):
        hit = at[:, y : y + 1] == trace
        order[y * rows_x : (y + 1) * rows_x, :] = jnp.where(hit, 1.0, 0.0).astype(jnp.bfloat16)
    at_x, at_z = index("gx"), index("gz")
    size_x = lax.axis_size("gx")
    for k in range(spot.shape[0]):
        block = near_col[0] if k == 0 else far_col[k - 1]
        apart = (block // 2) ^ at_x
        where = ((block % 2) ^ at_z) * size_x
        for n, step in enumerate(doubling(size_x)):
            where = where + jnp.where(apart & step > 0, 1 << n, 0)
        spot[k] = where


def trace_kernel(*refs):
    order, out = refs[-2:]
    if len(refs) == 3:
        face = refs[0][...]
    else:
        own, other = refs[0][...], refs[1][...]
        first = index("gy") == 0
        face = jnp.concatenate(
            [jnp.where(first, own, other), jnp.where(first, other, own)], axis=1
        )
    out[0] = jnp.dot(face, order[...], preferred_element_type=jnp.float32).astype(jnp.bfloat16)


def join_kernel(one, two, out):
    count = one.shape[0]
    out[:count] = one[...]
    out[count:] = two[...]


ACROSS = (((1,), (1,)), ((), ()))


def operator_kernel(halves, wanted, here, there, near, far_v, far_u, order, *outs):
    count = wanted.shape[0] - 1
    rank = far_v.shape[0] // count
    across = functools.partial(
        lax.dot_general, dimension_numbers=ACROSS, preferred_element_type=jnp.float32
    )
    size = here.shape[0]

    def traces(k):
        at = wanted[k] % size
        return jnp.where(wanted[k] < size, here[at], there[at])

    rows = across(traces(0), near[...])
    far = jnp.concatenate([traces(1 + k) for k in range(count)], axis=0)
    products = across(far, far_v[...])
    group = lax.broadcasted_iota(jnp.int32, (E, count * rank), 1) // rank
    weights = jnp.zeros((E, count * rank), jnp.float32)
    for k in range(count):
        weights = jnp.where(group == k, products[k * E : (k + 1) * E], weights)
    rows = rows + jnp.dot(
        weights.astype(jnp.bfloat16), far_u[...], preferred_element_type=jnp.float32
    )
    high = rows.astype(jnp.bfloat16)
    rest = rows - high.astype(jnp.float32)
    middle = rest.astype(jnp.bfloat16)
    low = (rest - middle.astype(jnp.float32)).astype(jnp.bfloat16)
    placed = across(jnp.concatenate([high, middle, low], axis=0), order[...])
    placed = placed[:E] + (placed[E : 2 * E] + placed[2 * E :])
    if halves:
        half = placed.shape[1] // 2
        first = index("gy") == 0
        outs[0][...] = jnp.where(first, placed[:, :half], placed[:, half:])
        outs[1][...] = jnp.where(first, placed[:, half:], placed[:, :half])
    else:
        outs[0][...] = placed


def finish_kernel(count, *refs):
    parts = refs[:count]
    inv, slab, _, flux_out, out, sem = refs[count:]
    side = index("gz")
    rows_x, _, width = slab.shape
    total = parts[0][...]
    if count == 2:
        total = total + parts[1][...]
    wide = jnp.concatenate([total, jnp.zeros((LANES - E, total.shape[1]), jnp.float32)], axis=0).T
    columns = []
    for start in range(0, width // E, LANES // E):
        column = wide[start * rows_x : (start + 1) * rows_x]
        for k in range(1, LANES // E):
            column = column + roll(wide[(start + k) * rows_x : (start + k + 1) * rows_x], k * E, 1)
        columns.append(column)
    flux = jnp.concatenate(columns, axis=1)
    added = (flux * inv[0])[:, None, :]
    row = lax.broadcasted_iota(jnp.int32, slab.shape, 1)
    slab[...] = slab[...] + jnp.where(row == side * (ROWS - 1), added, 0.0)
    top = pl.multiple_of(side * (out.shape[1] - ROWS), ROWS)
    copy = pltpu.make_async_copy(slab, out.at[:, pl.ds(top, ROWS), :], sem)
    copy.start()
    flux_out[...] = flux[:, None, :]
    copy.wait()


def side_edge_kernel(source, inv, *messages):
    odd = index("gy") % 2
    cells = source.shape[2] // E
    c = inv[...]
    first, last = source[:, :, :LANES], source[:, :, source.shape[2] - LANES :]
    lane = lane_ids(c)
    width = HALO * E
    low = jnp.where(lane < width, first, roll(c, width, 2))
    high = jnp.where(lane < width, roll(last, width, 2), roll(c, width - (cells - HALO), 2))
    for number, message in enumerate(messages):
        message[...] = choose(odd, low, high, number)


def widen(cells, ring, s, c, left, right):
    lane = lane_ids(right)
    width = HALO * E
    axis = right.ndim - 1
    zero = jnp.zeros_like(right)
    after = jnp.where(lane < width, right, zero)
    before = jnp.where(lane >= LANES - width, roll(left, LANES - width, axis), zero)
    pads = [after + before] if ring - cells == LANES // E else [after, before]
    own = jnp.where(lane < cells, c, zero)
    c_after = jnp.where((lane >= cells) & (lane < cells + HALO), roll(right, cells - width, axis), zero)
    c_before = jnp.where(
        (lane >= ring - HALO) & (lane < ring), roll(left, ring - HALO - width, axis), zero
    )
    return [s, *pads], own + c_after + c_before


def row_edge_kernel(cells, ring, ny, source, inv, *refs):
    odd_x, odd_y = index("gx") % 2, index("gy") % 2
    got_y, messages = refs[:ny], refs[ny:]
    rows_x = source.shape[0]
    for k in range(HALO):
        sides = []
        for row in (k, rows_x - HALO + k):
            got = [r[row] for r in got_y]
            parts, compact = widen(
                cells, ring, source[row], inv[row], from_low(odd_y, got), from_high(odd_y, got)
            )
            sides.append(jnp.concatenate([*parts, compact], axis=1))
        for number, message in enumerate(messages):
            message[k] = choose(odd_x, sides[0], sides[1], number)


def depth_edge_kernel(cells, ring, ny, nx, source, inv, *refs):
    odd_x, odd_y, side = index("gx") % 2, index("gy") % 2, index("gz")
    got_y, got_x, out = refs[:ny], refs[ny : ny + nx], refs[-1]
    rows_x, depth, _ = source.shape
    inner = lambda r: jnp.where(side == 0, r[:, depth - ROWS :, :], r[:, :ROWS, :])
    got = [inner(r) for r in got_y]
    parts, compact = widen(
        cells, ring, inner(source), inner(inv), from_low(odd_y, got), from_high(odd_y, got)
    )
    out[HALO : HALO + rows_x] = jnp.concatenate([*parts, compact], axis=2)
    got = [inner(r) for r in got_x]
    out[:HALO] = from_low(odd_x, got)
    out[HALO + rows_x :] = from_high(odd_x, got)


def assemble_kernel(cells, ring, ny, nx, source, inv, *refs):
    odd_x, odd_y, side = index("gx") % 2, index("gy") % 2, index("gz")
    got_y, got_x, got_z = refs[:ny], refs[ny : ny + nx], refs[ny + nx]
    ext_s, ext_i, one, compacts, matrix = refs[ny + nx + 1 :]
    rows_x, depth, width = source.shape
    wide = ring * E
    all_x, all_z = ext_s.shape[:2]
    matrix[...] = spread_matrix(ring, wide)
    row = lax.broadcasted_iota(jnp.int32, (ROWS, LANES), 0)
    start = side * (ROWS - HALO)
    near = (row >= start) & (row < start + HALO)

    def place(x, parts, compact):
        zone = got_z[x]
        lanes = jnp.where(near, zone[:, wide:], 0.0)
        compacts[pl.ds(pl.multiple_of(x * all_z, ROWS), depth), :] = compact
        compacts[pl.ds(pl.multiple_of(x * all_z + depth, ROWS), ROWS), :] = lanes
        at = 0
        for part in parts:
            ext_s[x, :depth, at : at + part.shape[1]] = part
            at += part.shape[1]
        ext_s[x, depth:, :] = zone[:, :wide]

    def own(x, _):
        got = [r[x] for r in got_y]
        parts, compact = widen(
            cells, ring, source[x], inv[x], from_low(odd_y, got), from_high(odd_y, got)
        )
        place(x + HALO, parts, compact)
        return 0

    lax.fori_loop(0, rows_x, own, 0)
    for k in range(HALO):
        got = [r[k] for r in got_x]
        below, above = from_low(odd_x, got), from_high(odd_x, got)
        place(k, [below[:, :wide]], below[:, wide:])
        place(rows_x + HALO + k, [above[:, :wide]], above[:, wide:])
    group = 2

    def expand(n, _):
        rows = group * all_z
        some = packed(compacts[pl.ds(pl.multiple_of(n * rows, ROWS), rows), :], ring)
        inverse = jnp.dot(some, matrix[...], preferred_element_type=jnp.float32)
        for k in range(group):
            x = n * group + k
            value = inverse[k * all_z : (k + 1) * all_z]
            ext_i[x] = value
            one[x] = ext_s[x] * value
        return 0

    lax.fori_loop(0, all_x // group, expand, 0)


def swept(ext_s, ext_i, old, x):
    u = old[x]
    beside = old[x - 1] + old[x + 1]
    beside = beside + (roll(u, 1, 0) + roll(u, -1, 0)) + (roll(u, E, 1) + roll(u, -E, 1))
    return (ext_s[x] + beside) * ext_i[x]


def sweep_kernel(margin, ext_s, ext_i, old, new):
    def step(x, _):
        new[x] = swept(ext_s, ext_i, old, x)
        return 0

    lax.fori_loop(margin, old.shape[0] - margin, step, 0)


def last_sweep_kernel(ext_s, ext_i, old, out, slab):
    side = index("gz")
    rows_x, depth, width = out.shape

    def step(x, _):
        new = swept(ext_s, ext_i, old, x + HALO)[:depth, :width]
        out[x] = new
        slab[x] = jnp.where(side == 0, new[:ROWS], new[depth - ROWS :])
        return 0

    lax.fori_loop(0, rows_x, step, 0)


def body(source, coef, face_trace, near_col, far_col, near_tile, far_u, far_v):
    rows_x, depth, width = source.shape
    cells = coef.shape[2]
    groups = lax.axis_size("gy")
    size_x = lax.axis_size("gx")
    tile = near_tile.shape[3]
    count = far_u.shape[3]
    rank = far_u.shape[4]
    nx, ny = message_count("gx"), message_count("gy")
    bf16 = jnp.bfloat16
    both = [(0, 1), (1, 0)]
    source = held(source)
    coef = held(coef.transpose(0, 2, 1))

    planes = vector((3, rows_x, width))
    inv, s_face, i_face, *out_x = call(
        face_start_kernel, (source, coef),
        [vector((rows_x, depth, LANES)), planes, planes] + [vector((ROWS, width))] * nx,
    )
    got_x = swap(out_x, "gx")
    out_y = call(
        functools.partial(face_side_kernel, nx), (s_face, i_face, *got_x),
        [vector((2 * rows_x + ROWS, LANES))] * ny, work=200,
    )
    got_y = swap(out_y, "gy")
    ext = pltpu.VMEM((2, rows_x + 2 * ROWS, width + LANES), jnp.float32)
    part = rows_x * cells
    (face,) = call(
        functools.partial(face_sweep_kernel, nx, ny), (s_face, i_face, *got_x, *got_y),
        [(vector if groups == 2 else plain)((E, part), bf16)], scratch=(ext, ext), work=500,
    )

    order, spot = call(
        order_kernel, (face_trace, near_col.reshape(1), far_col.reshape(count)),
        [vector((tile, tile), bf16), pltpu.SMEM((count + 1,), jnp.int32)],
        in_specs=[VECTOR, SCALAR, SCALAR], out_specs=[VECTOR, SCALAR],
    )
    if groups == 2:
        faces = (face, held(lax.ppermute(face, "gy", both)))
    else:
        faces = (held(lax.all_gather(face, "gy", axis=1, tiled=True)),)
    (traces,) = call(trace_kernel, (*faces, order), [vector((1, E, tile), bf16)])
    for step in doubling(size_x):
        other = held(lax.ppermute(traces, "gx", [(i, i ^ step) for i in range(size_x)]))
        both_shape = (2 * traces.shape[0], E, tile)
        (traces,) = call(join_kernel, (traces, other), [vector(both_shape, bf16)], work=300)
    other = held(lax.ppermute(traces, "gz", both))

    halves = groups == 2
    rows = call(
        functools.partial(operator_kernel, halves),
        (spot, traces, other, held(near_tile.reshape(tile, tile)), held(far_v.reshape(count * rank, tile)),
         held(far_u.reshape(count * rank, tile)), order),
        [vector((E, part))] * 2 if halves else [plain((E, tile))],
        in_specs=[SCALAR] + [VECTOR] * 6, work=3000,
    )
    if halves:
        rows = (rows[0], held(lax.ppermute(rows[1], "gy", both)))
    else:
        rows = (held(lax.psum_scatter(rows[0], "gy", scatter_dimension=1, tiled=True)),)

    pad = LANES if groups == 2 else 2 * LANES
    ring = (width + pad) // E
    wide = width + pad
    out_y = call(side_edge_kernel, (source, inv), [vector((rows_x, depth, LANES))] * ny, work=500)
    vol_y = swap(out_y, "gy")
    out_x = call(
        functools.partial(row_edge_kernel, cells, ring, ny), (source, inv, *vol_y),
        [vector((HALO, depth, wide + LANES))] * nx, work=500,
    )
    vol_x = swap(out_x, "gx")
    all_x = rows_x + 2 * HALO
    (out_z,) = call(
        functools.partial(depth_edge_kernel, cells, ring, ny, nx), (source, inv, *vol_y, *vol_x),
        [vector((all_x, ROWS, wide + LANES))], work=500,
    )
    vol_z = held(lax.ppermute(out_z, "gz", both))
    all_z = depth + ROWS
    ext = vector((all_x, all_z, wide))
    ext_s, ext_i, one = call(
        functools.partial(assemble_kernel, cells, ring, ny, nx),
        (source, inv, *vol_y, *vol_x, vol_z), [ext, ext, ext], work=2000,
        scratch=(vector((all_x * all_z, LANES)), vector((LANES, wide), bf16)),
    )
    (two,) = call(functools.partial(sweep_kernel, 1), (ext_s, ext_i, one), [ext], work=2000)
    (three,) = call(functools.partial(sweep_kernel, 2), (ext_s, ext_i, two), [ext], work=2000)
    field, slab = call(
        last_sweep_kernel, (ext_s, ext_i, three),
        [plain(source.shape), vector((rows_x, ROWS, width))], work=3000,
    )

    flux, result = call(
        functools.partial(finish_kernel, len(rows)), (*rows, i_face, slab, field),
        [plain((rows_x, 1, width)), plain(source.shape)],
        in_specs=[VECTOR] * (len(rows) + 2) + [PLACED], out_specs=[VECTOR, PLACED],
        scratch=(pltpu.SemaphoreType.DMA,), input_output_aliases={len(rows) + 2: 1},
    )
    return (result, flux)


def solution(mesh):
    return jax.shard_map(
        body,
        mesh=mesh,
        in_specs=(
            P("gx", "gz", "gy"),
            P("gx", "gz", "gy"),
            P("gx", "gz", None),
            P("gx", "gz", "gy"),
            P("gx", "gz", "gy", None),
            P("gx", "gz", "gy", None, None),
            P("gx", "gz", "gy", None, None, None),
            P("gx", "gz", "gy", None, None, None),
        ),
        out_specs=(P("gx", "gz", "gy"), P("gx", "gz", "gy")),
        check_vma=False,
    )
```

```python
import functools
import math

import jax
import jax.numpy as jnp
from jax import lax
from jax.experimental import pallas as pl
from jax.experimental.pallas import tpu as pltpu
from jax.sharding import PartitionSpec as P

E = 32
LANES = 128
ROWS = 8
HALO = 3


def roll(value, shift, axis):
    return pltpu.roll(value, shift % value.shape[axis], axis)


def lane_ids(value):
    return lax.broadcasted_iota(jnp.int32, value.shape, value.ndim - 1)


def held(value):
    return pltpu.with_memory_space_constraint(value, pltpu.VMEM)


def kept(value):
    return pltpu.with_memory_space_constraint(value, pltpu.HBM)


VECTOR = pl.BlockSpec(memory_space=pltpu.VMEM)
SCALAR = pl.BlockSpec(memory_space=pltpu.SMEM)
PLACED = pl.BlockSpec(memory_space=pl.ANY)
MAIN = pl.BlockSpec(memory_space=pltpu.HBM)


def vector(shape, dtype=jnp.float32):
    return pltpu.VMEM(shape, dtype)


def plain(shape, dtype=jnp.float32):
    return jax.ShapeDtypeStruct(shape, dtype)


def size_of(a):
    return math.prod(a.shape) * jnp.dtype(a.dtype).itemsize


def call(kernel, operands, out_shape, in_specs=None, out_specs=None, scratch=(), room=8, work=1000, after=(), **kw):
    given, tokens = len(operands), len(after)

    def body(*refs):
        kernel(*refs[:given], *refs[given + tokens :])

    return pl.pallas_call(
        body,
        out_shape=out_shape,
        in_specs=(in_specs or [VECTOR] * given) + [PLACED] * tokens,
        out_specs=out_specs or [VECTOR] * len(out_shape),
        scratch_shapes=list(scratch),
        compiler_params=pltpu.CompilerParams(vmem_limit_bytes=room * 1024 * 1024),
        cost_estimate=pl.CostEstimate(flops=0, bytes_accessed=work * 3000, transcendentals=0),
        **kw,
    )(*operands, *after)


def index(axis):
    return lax.axis_index(axis).astype(jnp.int32)


def pairs(count):
    first = [(i, i ^ 1) for i in range(count)]
    second = [(i, i + 1) for i in range(1, count - 1, 2)]
    return first, second + [(b, a) for a, b in second]


def swap(messages, axis):
    count = lax.axis_size(axis)
    return [held(lax.ppermute(m, axis, p)) for m, p in zip(messages, pairs(count))]


def doubling(count):
    steps = []
    while count > 1:
        count //= 2
        steps.append(count)
    return steps


def message_count(axis):
    return 1 if lax.axis_size(axis) == 2 else 2


def choose(odd, low, high, number):
    return jnp.where(odd == number, high, low)


def from_low(odd, received):
    other = received[1] if len(received) == 2 else jnp.zeros_like(received[0])
    return jnp.where(odd == 1, received[0], other)


def from_high(odd, received):
    other = received[1] if len(received) == 2 else jnp.zeros_like(received[0])
    return jnp.where(odd == 1, other, received[0])


def spread_matrix(cells, width):
    k = lax.broadcasted_iota(jnp.int32, (LANES, width), 0)
    cell = lax.broadcasted_iota(jnp.int32, (LANES, width), 1) // E
    part = k // 32
    hit = (k - part * 32 == cell) & (part < 3) & (cell < cells)
    return jnp.where(hit, 1.0, 0.0).astype(jnp.bfloat16)


def packed(compact, cells):
    compact = jnp.where(lane_ids(compact) < cells, compact, 0.0)
    high = compact.astype(jnp.bfloat16).astype(jnp.float32)
    rest = compact - high
    middle = rest.astype(jnp.bfloat16).astype(jnp.float32)
    low = (rest - middle).astype(jnp.bfloat16).astype(jnp.float32)
    axis = compact.ndim - 1
    return (high + roll(middle, 32, axis) + roll(low, 64, axis)).astype(jnp.bfloat16)


def spread(compact, width, cells):
    return jnp.dot(
        packed(compact, cells), spread_matrix(cells, width), preferred_element_type=jnp.float32
    )


def face_start_kernel(nx, source, coef, inv, s_out, i_out, *refs):
    messages, (src, coefs, sems) = refs[:nx], refs[nx:]
    odd, side = index("gx") % 2, index("gz")
    rows_x, depth, width = source.shape
    cells = width // E
    top = pl.multiple_of(side * (depth - ROWS), ROWS)
    copies = [
        pltpu.make_async_copy(coef, coefs, sems.at[0]),
        pltpu.make_async_copy(source.at[:, pl.ds(top, ROWS), :], src, sems.at[1]),
    ]
    for copy in copies:
        copy.start()
    copies[0].wait()
    c = jnp.swapaxes(1.0 / (6.0 + coefs[...]), 1, 2)
    inv[...] = jnp.concatenate(
        [c, jnp.zeros((rows_x, depth, LANES - cells), jnp.float32)], axis=2
    )
    copies[1].wait()
    planes = []
    for d in range(3):
        s = jnp.where(side == 0, src[:, d, :], src[:, ROWS - 1 - d, :])
        i = jnp.where(side == 0, inv[:, d, :], inv[:, depth - 1 - d, :])
        planes.append([s, i])
    spreads = spread(jnp.concatenate([i for _, i in planes], axis=0), width, cells)
    for d in range(3):
        planes[d][1] = spreads[d * rows_x : (d + 1) * rows_x]
        s_out[d], i_out[d] = planes[d]
    for number, message in enumerate(messages):
        for d in range(2):
            for k in range(2):
                v = planes[d][k]
                row = 4 * k + 2 * d
                message[row : row + 2, :] = choose(odd, v[:2], v[rows_x - 2 :], number)


def edge_pair(s, i):
    lane = lane_ids(s[:, :LANES])
    low = jnp.where(lane < 2 * E, s[:, :LANES], roll(i[:, :LANES], 64, 1))
    high = jnp.where(lane < 2 * E, roll(s[:, -LANES:], 64, 1), i[:, -LANES:])
    return low, high


def face_side_kernel(nx, s_in, i_in, *refs):
    odd_x, odd_y = index("gx") % 2, index("gy") % 2
    got, messages = [r[...] for r in refs[:nx]], refs[nx:]
    rows_x = s_in.shape[1]
    below, above = from_low(odd_x, got), from_high(odd_x, got)
    pick = lax.broadcasted_iota(jnp.int32, below.shape, 0)
    s = jnp.where(pick == 0, roll(below, -1, 0), roll(above, 1, 0))
    i = jnp.where(pick == 0, roll(below, -5, 0), roll(above, -3, 0))
    s, i = (jnp.where(pick < 2, v, 0.0) for v in (s, i))
    parts = [edge_pair(s_in[0], i_in[0]), edge_pair(s_in[1], i_in[1]), edge_pair(s, i)]
    for number, message in enumerate(messages):
        row = 0
        for low, high in parts:
            message[row : row + low.shape[0], :] = choose(odd_y, low, high, number)
            row += low.shape[0]


def face_sweep_kernel(nx, ny, s_in, i_in, *refs):
    odd_x, odd_y = index("gx") % 2, index("gy") % 2
    got_x = [r[...] for r in refs[:nx]]
    got_y = [r[...] for r in refs[nx : nx + ny]]
    out, ext_s, ext_i = refs[nx + ny :]
    _, rows_x, width = s_in.shape
    below, above = from_low(odd_x, got_x), from_high(odd_x, got_x)
    left, right = from_low(odd_y, got_y), from_high(odd_y, got_y)
    lane = lane_ids(left)
    pad_s = jnp.where(lane < 2 * E, right, roll(left, 64, 1))
    pad_i = jnp.where(lane < 2 * E, roll(right, 64, 1), left)
    ext_s[...] = jnp.zeros(ext_s.shape, jnp.float32)
    ext_i[...] = jnp.zeros(ext_i.shape, jnp.float32)
    first, last = ROWS, ROWS + rows_x
    for ext, own, pad, k in ((ext_s, s_in, pad_s, 0), (ext_i, i_in, pad_i, 1)):
        for d in range(2):
            row = 4 * k + 2 * d
            ext[d, first:last, :width] = own[d]
            ext[d, first - 2 : first, :width] = below[row : row + 2]
            ext[d, last : last + 2, :width] = above[row : row + 2]
            ext[d, first:last, width:] = pad[d * rows_x : (d + 1) * rows_x]
        ext[0, first - 1 : first, width:] = pad[2 * rows_x : 2 * rows_x + 1]
        ext[0, last : last + 1, width:] = pad[2 * rows_x + 1 : 2 * rows_x + 2]

    def around(u):
        return roll(u, 1, 0) + roll(u, -1, 0) + roll(u, E, 1) + roll(u, -E, 1)

    s0, s1, i0, i1 = ext_s[0], ext_s[1], ext_i[0], ext_i[1]
    u0, u1 = s0 * i0, s1 * i1
    deep = s_in[2] * i_in[2]
    v0 = (s0 + (around(u0) + u1)) * i0
    own = (around(u1) + u0)[first:last, :width]
    v1 = (s_in[1] + (own + deep)) * i_in[1]
    face = (s_in[0] + (around(v0)[first:last, :width] + v1)) * i_in[0]
    pieces = []
    for cell in range(width // E):
        start = cell * E // LANES * LANES
        pieces.append(roll(face[:, start : start + LANES], -(cell * E - start), 1))
    stacked = jnp.concatenate(pieces, axis=0)
    out[...] = stacked.T[:E].astype(jnp.bfloat16)


def order_kernel(place, near_col, far_col, order, spot):
    rows_x, _, cells_y = place.shape
    at = place[...].reshape(rows_x, cells_y) if rows_x == 1 else place[:, 0, :]
    trace = lax.broadcasted_iota(jnp.int32, (rows_x, order.shape[1]), 1)
    for y in range(cells_y):
        hit = at[:, y : y + 1] == trace
        order[y * rows_x : (y + 1) * rows_x, :] = jnp.where(hit, 1.0, 0.0).astype(jnp.bfloat16)
    at_x, at_z = index("gx"), index("gz")
    size_x = lax.axis_size("gx")
    for k in range(spot.shape[0]):
        block = near_col[0] if k == 0 else far_col[k - 1]
        apart = (block // 2) ^ at_x
        where = ((block % 2) ^ at_z) * size_x
        for n, step in enumerate(doubling(size_x)):
            where = where + jnp.where(apart & step > 0, 1 << n, 0)
        spot[k] = where


def trace_kernel(*refs):
    order, out = refs[-2:]
    if len(refs) == 3:
        face = refs[0][...]
    else:
        own, other = refs[0][...], refs[1][...]
        first = index("gy") == 0
        face = jnp.concatenate(
            [jnp.where(first, own, other), jnp.where(first, other, own)], axis=1
        )
    out[0] = jnp.dot(face, order[...], preferred_element_type=jnp.float32).astype(jnp.bfloat16)


def join_kernel(one, two, out):
    count = one.shape[0]
    out[:count] = one[...]
    out[count:] = two[...]


ACROSS = (((1,), (1,)), ((), ()))


def operator_kernel(halves, wanted, here, there, near, far_v, far_u, order, *outs):
    count = wanted.shape[0] - 1
    rank = far_v.shape[0] // count
    across = functools.partial(
        lax.dot_general, dimension_numbers=ACROSS, preferred_element_type=jnp.float32
    )
    size = here.shape[0]

    def traces(k):
        at = wanted[k] % size
        return jnp.where(wanted[k] < size, here[at], there[at])

    rows = across(traces(0), near[...])
    far = jnp.concatenate([traces(1 + k) for k in range(count)], axis=0)
    products = across(far, far_v[...])
    group = lax.broadcasted_iota(jnp.int32, (E, count * rank), 1) // rank
    weights = jnp.zeros((E, count * rank), jnp.float32)
    for k in range(count):
        weights = jnp.where(group == k, products[k * E : (k + 1) * E], weights)
    rows = rows + jnp.dot(
        weights.astype(jnp.bfloat16), far_u[...], preferred_element_type=jnp.float32
    )
    high = rows.astype(jnp.bfloat16)
    rest = rows - high.astype(jnp.float32)
    middle = rest.astype(jnp.bfloat16)
    low = (rest - middle.astype(jnp.float32)).astype(jnp.bfloat16)
    placed = across(jnp.concatenate([high, middle, low], axis=0), order[...])
    placed = placed[:E] + (placed[E : 2 * E] + placed[2 * E :])
    if halves:
        half = placed.shape[1] // 2
        first = index("gy") == 0
        outs[0][...] = jnp.where(first, placed[:, :half], placed[:, half:])
        outs[1][...] = jnp.where(first, placed[:, half:], placed[:, :half])
    else:
        outs[0][...] = placed


def finish_kernel(count, *refs):
    parts = refs[:count]
    inv, slab, _, flux_out, out, held_flux, sems = refs[count:]
    side = index("gz")
    rows_x, _, width = slab.shape
    total = parts[0][...]
    if count == 2:
        total = total + parts[1][...]
    wide = jnp.concatenate([total, jnp.zeros((LANES - E, total.shape[1]), jnp.float32)], axis=0).T
    columns = []
    for start in range(0, width // E, LANES // E):
        column = wide[start * rows_x : (start + 1) * rows_x]
        for k in range(1, LANES // E):
            column = column + roll(wide[(start + k) * rows_x : (start + k + 1) * rows_x], k * E, 1)
        columns.append(column)
    flux = jnp.concatenate(columns, axis=1)
    held_flux[...] = flux[:, None, :]
    out_copy = pltpu.make_async_copy(held_flux, flux_out, sems.at[0])
    out_copy.start()
    added = (flux * inv[0])[:, None, :]
    row = lax.broadcasted_iota(jnp.int32, slab.shape, 1)
    slab[...] = slab[...] + jnp.where(row == side * (ROWS - 1), added, 0.0)
    top = pl.multiple_of(side * (out.shape[1] - ROWS), ROWS)
    copy = pltpu.make_async_copy(slab, out.at[:, pl.ds(top, ROWS), :], sems.at[1])
    copy.start()
    out_copy.wait()
    copy.wait()


def side_edge_kernel(source, inv, *messages):
    odd = index("gy") % 2
    cells = source.shape[2] // E
    c = inv[...]
    first, last = source[:, :, :LANES], source[:, :, source.shape[2] - LANES :]
    lane = lane_ids(c)
    width = HALO * E
    low = jnp.where(lane < width, first, roll(c, width, 2))
    high = jnp.where(lane < width, roll(last, width, 2), roll(c, width - (cells - HALO), 2))
    for number, message in enumerate(messages):
        message[...] = choose(odd, low, high, number)


def widen(cells, ring, s, c, left, right):
    lane = lane_ids(right)
    width = HALO * E
    axis = right.ndim - 1
    zero = jnp.zeros_like(right)
    after = jnp.where(lane < width, right, zero)
    before = jnp.where(lane >= LANES - width, roll(left, LANES - width, axis), zero)
    pads = [after + before] if ring - cells == LANES // E else [after, before]
    own = jnp.where(lane < cells, c, zero)
    c_after = jnp.where((lane >= cells) & (lane < cells + HALO), roll(right, cells - width, axis), zero)
    c_before = jnp.where(
        (lane >= ring - HALO) & (lane < ring), roll(left, ring - HALO - width, axis), zero
    )
    return [s, *pads], own + c_after + c_before


def row_edge_kernel(cells, ring, ny, source, inv, *refs):
    odd_x, odd_y = index("gx") % 2, index("gy") % 2
    got_y, messages = refs[:ny], refs[ny:]
    rows_x = source.shape[0]
    for k in range(HALO):
        sides = []
        for row in (k, rows_x - HALO + k):
            got = [r[row] for r in got_y]
            parts, compact = widen(
                cells, ring, source[row], inv[row], from_low(odd_y, got), from_high(odd_y, got)
            )
            sides.append(jnp.concatenate([*parts, compact], axis=1))
        for number, message in enumerate(messages):
            message[k] = choose(odd_x, sides[0], sides[1], number)


def depth_edge_kernel(cells, ring, ny, nx, source, inv, *refs):
    odd_x, odd_y, side = index("gx") % 2, index("gy") % 2, index("gz")
    got_y, got_x, out = refs[:ny], refs[ny : ny + nx], refs[-1]
    rows_x, depth, _ = source.shape
    inner = lambda r: jnp.where(side == 0, r[:, depth - ROWS :, :], r[:, :ROWS, :])
    got = [inner(r) for r in got_y]
    parts, compact = widen(
        cells, ring, inner(source), inner(inv), from_low(odd_y, got), from_high(odd_y, got)
    )
    out[HALO : HALO + rows_x] = jnp.concatenate([*parts, compact], axis=2)
    got = [inner(r) for r in got_x]
    out[:HALO] = from_low(odd_x, got)
    out[HALO + rows_x :] = from_high(odd_x, got)


def assemble_kernel(cells, ring, ny, nx, source, inv, *refs):
    odd_x, odd_y, side = index("gx") % 2, index("gy") % 2, index("gz")
    got_y, got_x, got_z = refs[:ny], refs[ny : ny + nx], refs[ny + nx]
    ext_s, ext_i, one, compacts, matrix = refs[ny + nx + 1 :]
    rows_x, depth, width = source.shape
    wide = ring * E
    all_z = depth + ROWS
    total = ext_s.shape[0]
    matrix[...] = spread_matrix(ring, wide)
    row = lax.broadcasted_iota(jnp.int32, (ROWS, LANES), 0)
    start = side * (ROWS - HALO)
    near = (row >= start) & (row < start + HALO)

    def place(x, parts, compact):
        zone = got_z[x]
        lanes = jnp.where(near, zone[:, wide:], 0.0)
        first = pl.ds(pl.multiple_of(x * all_z, ROWS), depth)
        rest = pl.ds(pl.multiple_of(x * all_z + depth, ROWS), ROWS)
        compacts[first, :] = compact
        compacts[rest, :] = lanes
        at = 0
        for part in parts:
            ext_s[first, at : at + part.shape[1]] = part
            at += part.shape[1]
        ext_s[rest, :] = zone[:, :wide]

    def own(x, _):
        got = [r[x] for r in got_y]
        parts, compact = widen(
            cells, ring, source[x], inv[x], from_low(odd_y, got), from_high(odd_y, got)
        )
        place(x + HALO, parts, compact)
        return 0

    lax.fori_loop(0, rows_x, own, 0, unroll=2)
    for k in range(HALO):
        got = [r[k] for r in got_x]
        below, above = from_low(odd_x, got), from_high(odd_x, got)
        place(k, [below[:, :wide]], below[:, wide:])
        place(rows_x + HALO + k, [above[:, :wide]], above[:, wide:])
    chunk = max(n for n in range(2 * ROWS, 321, 2 * ROWS) if total % n == 0)

    def expand(n, _):
        rows = pl.ds(pl.multiple_of(n * chunk, 2 * ROWS), chunk)
        some = packed(compacts[rows, :], ring)
        inverse = jnp.dot(some, matrix[...], preferred_element_type=jnp.float32)
        ext_i[rows, :] = inverse
        one[rows, :] = ext_s[rows, :] * inverse
        return 0

    lax.fori_loop(0, total // chunk, expand, 0)


def swept(ext_s, ext_i, old, x, all_z, depth, width, store):
    at = lambda x, rows: pl.ds(pl.multiple_of(x * all_z, ROWS), rows)
    tiles = old.shape[1] // LANES
    lane = lax.broadcasted_iota(jnp.int32, (all_z, LANES), 1)
    known = {}

    def tile(j):
        j %= tiles
        if j not in known:
            u = old[at(x, all_z), j * LANES : (j + 1) * LANES]
            known[j] = (u, roll(u, E, 1), roll(u, -E, 1))
        return known[j]

    for j in range(width // LANES):
        columns = slice(j * LANES, (j + 1) * LANES)
        here = tile(j)
        beside = old[at(x - 1, depth), columns] + old[at(x + 1, depth), columns]
        up = roll(here[0], 1, 0) + roll(here[0], -1, 0)
        side = jnp.where(lane < E, tile(j - 1)[1], here[1])
        side = side + jnp.where(lane >= LANES - E, tile(j + 1)[2], here[2])
        beside = beside + (up + side)[:depth]
        new = (ext_s[at(x, depth), columns] + beside) * ext_i[at(x, depth), columns]
        store(columns, new)


def sweep_kernel(margin, all_z, ext_s, ext_i, old, new):
    def step(x, _):
        def store(columns, value):
            new[pl.ds(pl.multiple_of(x * all_z, ROWS), all_z), columns] = value

        swept(ext_s, ext_i, old, x, all_z, all_z, old.shape[1], store)
        return 0

    lax.fori_loop(margin, old.shape[0] // all_z - margin, step, 0)


def last_sweep_kernel(ext_s, ext_i, old, out, slab, done, sems):
    side = index("gz")
    rows_x, depth, width = out.shape
    all_z = depth + ROWS

    def step(x, _):
        def store(columns, value):
            done[x, :, columns] = value
            slab[x, :, columns] = jnp.where(side == 0, value[:ROWS], value[depth - ROWS :])

        swept(ext_s, ext_i, old, x + HALO, all_z, depth, width, store)
        return 0

    pieces = sems.shape[0]
    size = rows_x // pieces
    copies = []
    for n in range(pieces):
        lax.fori_loop(n * size, (n + 1) * size, step, 0)
        rows = slice(n * size, (n + 1) * size)
        copies.append(pltpu.make_async_copy(done.at[rows], out.at[rows], sems.at[n]))
        copies[-1].start()
    for copy in copies:
        copy.wait()


def body(source, coef, face_trace, near_col, far_col, near_tile, far_u, far_v):
    rows_x, depth, width = source.shape
    cells = coef.shape[2]
    groups = lax.axis_size("gy")
    size_x = lax.axis_size("gx")
    tile = near_tile.shape[3]
    count = far_u.shape[3]
    rank = far_u.shape[4]
    nx, ny = message_count("gx"), message_count("gy")
    bf16 = jnp.bfloat16
    both = [(0, 1), (1, 0)]
    pad = LANES if groups == 2 else 2 * LANES
    ring = (width + pad) // E
    wide = width + pad
    all_x, all_z = rows_x + 2 * HALO, depth + ROWS
    part = rows_x * cells
    halves = groups == 2
    coef = coef.transpose(0, 2, 1)
    held_source = held(source)

    planes = vector((3, rows_x, width))
    inv, s_face, i_face, *face_x = call(
        functools.partial(face_start_kernel, nx), (kept(source), kept(coef)),
        [vector((rows_x, depth, LANES)), planes, planes] + [vector((ROWS, width))] * nx,
        in_specs=[MAIN, MAIN],
        scratch=(vector((rows_x, ROWS, width)), vector(coef.shape), pltpu.SemaphoreType.DMA((2,))),
    )
    got_x = swap(face_x, "gx")
    vol_y = call(
        side_edge_kernel, (held_source, inv), [vector((rows_x, depth, LANES))] * ny, work=500,
        after=face_x,
    )
    got_vol_y = swap(vol_y, "gy")
    face_y = call(
        functools.partial(face_side_kernel, nx), (s_face, i_face, *got_x),
        [vector((2 * rows_x + ROWS, LANES))] * ny, work=200, after=vol_y,
    )
    got_y = swap(face_y, "gy")
    ext = pltpu.VMEM((2, rows_x + 2 * ROWS, width + LANES), jnp.float32)
    (face,) = call(
        functools.partial(face_sweep_kernel, nx, ny), (s_face, i_face, *got_x, *got_y),
        [(vector if halves else plain)((E, part), bf16)], scratch=(ext, ext), work=500,
    )
    if halves:
        faces = (face, held(lax.ppermute(face, "gy", both)))
    else:
        faces = (held(lax.all_gather(face, "gy", axis=1, tiled=True)),)

    vol_x = call(
        functools.partial(row_edge_kernel, cells, ring, ny), (held_source, inv, *got_vol_y),
        [vector((HALO, depth, wide + LANES))] * nx, work=500, after=(face,),
    )
    got_vol_x = swap(vol_x, "gx")
    order, spot = call(
        order_kernel, (face_trace, near_col.reshape(1), far_col.reshape(count)),
        [vector((tile, tile), bf16), pltpu.SMEM((count + 1,), jnp.int32)],
        in_specs=[VECTOR, SCALAR, SCALAR], out_specs=[VECTOR, SCALAR], after=vol_x,
    )

    (traces,) = call(trace_kernel, (*faces, order), [vector((1, E, tile), bf16)])
    stages = []
    for step in doubling(size_x):
        other = held(lax.ppermute(traces, "gx", [(i, i ^ step) for i in range(size_x)]))
        twice = (2 * traces.shape[0], E, tile)
        (traces,) = call(join_kernel, (traces, other), [vector(twice, bf16)], work=300)
        stages.append(traces)
    other = held(lax.ppermute(traces, "gz", both))
    (vol_z,) = call(
        functools.partial(depth_edge_kernel, cells, ring, ny, nx),
        (held_source, inv, *got_vol_y, *got_vol_x),
        [vector((all_x, ROWS, wide + LANES))], work=500, after=(stages[-3],),
    )
    got_vol_z = held(lax.ppermute(vol_z, "gz", both))
    ext = vector((all_x * all_z, wide))
    ext_s, ext_i, one = call(
        functools.partial(assemble_kernel, cells, ring, ny, nx),
        (held_source, inv, *got_vol_y, *got_vol_x, got_vol_z), [ext, ext, ext], work=2000,
        scratch=(vector((all_x * all_z, LANES)), vector((LANES, wide), bf16)),
        after=(stages[-2],),
    )
    (two,) = call(functools.partial(sweep_kernel, 1, all_z), (ext_s, ext_i, one), [ext], work=2000)
    (three,) = call(functools.partial(sweep_kernel, 2, all_z), (ext_s, ext_i, two), [ext], work=2000)

    rows = call(
        functools.partial(operator_kernel, halves),
        (spot, traces, other, held(near_tile.reshape(tile, tile)),
         held(far_v.reshape(count * rank, tile)), held(far_u.reshape(count * rank, tile)), order),
        [vector((E, part))] * 2 if halves else [plain((E, tile))],
        in_specs=[SCALAR] + [VECTOR] * 6, work=3000, after=(three,),
    )
    if halves:
        sums = (rows[0], held(lax.ppermute(rows[1], "gy", both)))
    else:
        sums = (held(lax.psum_scatter(rows[0], "gy", scatter_dimension=1, tiled=True)),)
    pieces = 4
    field, slab = call(
        last_sweep_kernel, (ext_s, ext_i, three),
        [plain(source.shape), vector((rows_x, ROWS, width))], work=2000,
        out_specs=[MAIN, VECTOR], after=rows,
        scratch=(vector(source.shape), pltpu.SemaphoreType.DMA((pieces,))),
    )

    flux, result = call(
        functools.partial(finish_kernel, len(sums)), (*sums, i_face, slab, field),
        [plain((rows_x, 1, width)), plain(source.shape)],
        in_specs=[VECTOR] * (len(sums) + 2) + [MAIN], out_specs=[MAIN, MAIN],
        scratch=(vector((rows_x, 1, width)), pltpu.SemaphoreType.DMA((2,))),
        input_output_aliases={len(sums) + 2: 1},
    )
    return (result, flux)


def solution(mesh):
    return jax.shard_map(
        body,
        mesh=mesh,
        in_specs=(
            P("gx", "gz", "gy"),
            P("gx", "gz", "gy"),
            P("gx", "gz", None),
            P("gx", "gz", "gy"),
            P("gx", "gz", "gy", None),
            P("gx", "gz", "gy", None, None),
            P("gx", "gz", "gy", None, None, None),
            P("gx", "gz", "gy", None, None, None),
        ),
        out_specs=(P("gx", "gz", "gy"), P("gx", "gz", "gy")),
        check_vma=False,
    )
```

```python
import functools
import math

import jax
import jax.numpy as jnp
from jax import lax
from jax.experimental import pallas as pl
from jax.experimental.pallas import tpu as pltpu
from jax.sharding import PartitionSpec as P

E = 32
LANES = 128
ROWS = 8
HALO = 3


def roll(value, shift, axis):
    return pltpu.roll(value, shift % value.shape[axis], axis)


def lane_ids(value):
    return lax.broadcasted_iota(jnp.int32, value.shape, value.ndim - 1)


def held(value):
    return pltpu.with_memory_space_constraint(value, pltpu.VMEM)


def kept(value):
    return pltpu.with_memory_space_constraint(value, pltpu.HBM)


VECTOR = pl.BlockSpec(memory_space=pltpu.VMEM)
SCALAR = pl.BlockSpec(memory_space=pltpu.SMEM)
PLACED = pl.BlockSpec(memory_space=pl.ANY)
MAIN = pl.BlockSpec(memory_space=pltpu.HBM)


def vector(shape, dtype=jnp.float32):
    return pltpu.VMEM(shape, dtype)


def plain(shape, dtype=jnp.float32):
    return jax.ShapeDtypeStruct(shape, dtype)


def size_of(a):
    return math.prod(a.shape) * jnp.dtype(a.dtype).itemsize


def call(kernel, operands, out_shape, in_specs=None, out_specs=None, scratch=(), room=8, work=1000, after=(), **kw):
    given, tokens = len(operands), len(after)

    def body(*refs):
        kernel(*refs[:given], *refs[given + tokens :])

    return pl.pallas_call(
        body,
        out_shape=out_shape,
        in_specs=(in_specs or [VECTOR] * given) + [PLACED] * tokens,
        out_specs=out_specs or [VECTOR] * len(out_shape),
        scratch_shapes=list(scratch),
        compiler_params=pltpu.CompilerParams(vmem_limit_bytes=room * 1024 * 1024),
        cost_estimate=pl.CostEstimate(flops=0, bytes_accessed=work * 3000, transcendentals=0),
        **kw,
    )(*operands, *after)


def index(axis):
    return lax.axis_index(axis).astype(jnp.int32)


def pairs(count):
    first = [(i, i ^ 1) for i in range(count)]
    second = [(i, i + 1) for i in range(1, count - 1, 2)]
    return first, second + [(b, a) for a, b in second]


def swap(messages, axis):
    count = lax.axis_size(axis)
    return [held(lax.ppermute(m, axis, p)) for m, p in zip(messages, pairs(count))]


def doubling(count):
    steps = []
    while count > 1:
        count //= 2
        steps.append(count)
    return steps


def message_count(axis):
    return 1 if lax.axis_size(axis) == 2 else 2


def choose(odd, low, high, number):
    return jnp.where(odd == number, high, low)


def from_low(odd, received):
    other = received[1] if len(received) == 2 else jnp.zeros_like(received[0])
    return jnp.where(odd == 1, received[0], other)


def from_high(odd, received):
    other = received[1] if len(received) == 2 else jnp.zeros_like(received[0])
    return jnp.where(odd == 1, other, received[0])


def spread_matrix(cells, width):
    k = lax.broadcasted_iota(jnp.int32, (LANES, width), 0)
    cell = lax.broadcasted_iota(jnp.int32, (LANES, width), 1) // E
    part = k // 32
    hit = (k - part * 32 == cell) & (part < 3) & (cell < cells)
    return jnp.where(hit, 1.0, 0.0).astype(jnp.bfloat16)


def packed(compact, cells):
    compact = jnp.where(lane_ids(compact) < cells, compact, 0.0)
    high = compact.astype(jnp.bfloat16).astype(jnp.float32)
    rest = compact - high
    middle = rest.astype(jnp.bfloat16).astype(jnp.float32)
    low = (rest - middle).astype(jnp.bfloat16).astype(jnp.float32)
    axis = compact.ndim - 1
    return (high + roll(middle, 32, axis) + roll(low, 64, axis)).astype(jnp.bfloat16)


def spread(compact, width, cells):
    return jnp.dot(
        packed(compact, cells), spread_matrix(cells, width), preferred_element_type=jnp.float32
    )


def face_start_kernel(nx, source, coef, inv, s_out, i_out, *refs):
    messages, (src, coefs, sems) = refs[:nx], refs[nx:]
    odd, side = index("gx") % 2, index("gz")
    rows_x, depth, width = source.shape
    cells = width // E
    top = pl.multiple_of(side * (depth - ROWS), ROWS)
    copies = [
        pltpu.make_async_copy(coef, coefs, sems.at[0]),
        pltpu.make_async_copy(source.at[:, pl.ds(top, ROWS), :], src, sems.at[1]),
    ]
    for copy in copies:
        copy.start()
    copies[0].wait()
    c = jnp.swapaxes(1.0 / (6.0 + coefs[...]), 1, 2)
    inv[...] = jnp.concatenate(
        [c, jnp.zeros((rows_x, depth, LANES - cells), jnp.float32)], axis=2
    )
    copies[1].wait()
    planes = []
    for d in range(3):
        s = jnp.where(side == 0, src[:, d, :], src[:, ROWS - 1 - d, :])
        i = jnp.where(side == 0, inv[:, d, :], inv[:, depth - 1 - d, :])
        planes.append([s, i])
    spreads = spread(jnp.concatenate([i for _, i in planes], axis=0), width, cells)
    for d in range(3):
        planes[d][1] = spreads[d * rows_x : (d + 1) * rows_x]
        s_out[d], i_out[d] = planes[d]
    for number, message in enumerate(messages):
        for d in range(2):
            for k in range(2):
                v = planes[d][k]
                row = 4 * k + 2 * d
                message[row : row + 2, :] = choose(odd, v[:2], v[rows_x - 2 :], number)


def edge_pair(s, i):
    lane = lane_ids(s[:, :LANES])
    low = jnp.where(lane < 2 * E, s[:, :LANES], roll(i[:, :LANES], 64, 1))
    high = jnp.where(lane < 2 * E, roll(s[:, -LANES:], 64, 1), i[:, -LANES:])
    return low, high


def face_side_kernel(nx, s_in, i_in, *refs):
    odd_x, odd_y = index("gx") % 2, index("gy") % 2
    got, messages = [r[...] for r in refs[:nx]], refs[nx:]
    rows_x = s_in.shape[1]
    below, above = from_low(odd_x, got), from_high(odd_x, got)
    pick = lax.broadcasted_iota(jnp.int32, below.shape, 0)
    s = jnp.where(pick == 0, roll(below, -1, 0), roll(above, 1, 0))
    i = jnp.where(pick == 0, roll(below, -5, 0), roll(above, -3, 0))
    s, i = (jnp.where(pick < 2, v, 0.0) for v in (s, i))
    parts = [edge_pair(s_in[0], i_in[0]), edge_pair(s_in[1], i_in[1]), edge_pair(s, i)]
    for number, message in enumerate(messages):
        row = 0
        for low, high in parts:
            message[row : row + low.shape[0], :] = choose(odd_y, low, high, number)
            row += low.shape[0]


def face_sweep_kernel(nx, ny, s_in, i_in, *refs):
    odd_x, odd_y = index("gx") % 2, index("gy") % 2
    got_x = [r[...] for r in refs[:nx]]
    got_y = [r[...] for r in refs[nx : nx + ny]]
    out, ext_s, ext_i = refs[nx + ny :]
    _, rows_x, width = s_in.shape
    below, above = from_low(odd_x, got_x), from_high(odd_x, got_x)
    left, right = from_low(odd_y, got_y), from_high(odd_y, got_y)
    lane = lane_ids(left)
    pad_s = jnp.where(lane < 2 * E, right, roll(left, 64, 1))
    pad_i = jnp.where(lane < 2 * E, roll(right, 64, 1), left)
    ext_s[...] = jnp.zeros(ext_s.shape, jnp.float32)
    ext_i[...] = jnp.zeros(ext_i.shape, jnp.float32)
    first, last = ROWS, ROWS + rows_x
    for ext, own, pad, k in ((ext_s, s_in, pad_s, 0), (ext_i, i_in, pad_i, 1)):
        for d in range(2):
            row = 4 * k + 2 * d
            ext[d, first:last, :width] = own[d]
            ext[d, first - 2 : first, :width] = below[row : row + 2]
            ext[d, last : last + 2, :width] = above[row : row + 2]
            ext[d, first:last, width:] = pad[d * rows_x : (d + 1) * rows_x]
        ext[0, first - 1 : first, width:] = pad[2 * rows_x : 2 * rows_x + 1]
        ext[0, last : last + 1, width:] = pad[2 * rows_x + 1 : 2 * rows_x + 2]

    def around(u):
        return roll(u, 1, 0) + roll(u, -1, 0) + roll(u, E, 1) + roll(u, -E, 1)

    s0, s1, i0, i1 = ext_s[0], ext_s[1], ext_i[0], ext_i[1]
    u0, u1 = s0 * i0, s1 * i1
    deep = s_in[2] * i_in[2]
    v0 = (s0 + (around(u0) + u1)) * i0
    own = (around(u1) + u0)[first:last, :width]
    v1 = (s_in[1] + (own + deep)) * i_in[1]
    face = (s_in[0] + (around(v0)[first:last, :width] + v1)) * i_in[0]
    pieces = []
    for cell in range(width // E):
        start = cell * E // LANES * LANES
        pieces.append(roll(face[:, start : start + LANES], -(cell * E - start), 1))
    stacked = jnp.concatenate(pieces, axis=0)
    out[...] = stacked.T[:E].astype(jnp.bfloat16)


def order_kernel(place, near_col, far_col, order, spot):
    rows_x, _, cells_y = place.shape
    at = place[...].reshape(rows_x, cells_y) if rows_x == 1 else place[:, 0, :]
    trace = lax.broadcasted_iota(jnp.int32, (rows_x, order.shape[1]), 1)
    for y in range(cells_y):
        hit = at[:, y : y + 1] == trace
        order[y * rows_x : (y + 1) * rows_x, :] = jnp.where(hit, 1.0, 0.0).astype(jnp.bfloat16)
    at_x, at_z = index("gx"), index("gz")
    size_x = lax.axis_size("gx")
    for k in range(spot.shape[0]):
        block = near_col[0] if k == 0 else far_col[k - 1]
        apart = (block // 2) ^ at_x
        where = ((block % 2) ^ at_z) * size_x
        for n, step in enumerate(doubling(size_x)):
            where = where + jnp.where(apart & step > 0, 1 << n, 0)
        spot[k] = where


def trace_kernel(*refs):
    order, out = refs[-2:]
    if len(refs) == 3:
        face = refs[0][...]
    else:
        own, other = refs[0][...], refs[1][...]
        first = index("gy") == 0
        face = jnp.concatenate(
            [jnp.where(first, own, other), jnp.where(first, other, own)], axis=1
        )
    out[0] = jnp.dot(face, order[...], preferred_element_type=jnp.float32).astype(jnp.bfloat16)


def join_kernel(one, two, out):
    count = one.shape[0]
    out[:count] = one[...]
    out[count:] = two[...]


ACROSS = (((1,), (1,)), ((), ()))


def operator_kernel(halves, wanted, here, there, near, far_v, far_u, order, *outs):
    count = wanted.shape[0] - 1
    rank = far_v.shape[0] // count
    across = functools.partial(
        lax.dot_general, dimension_numbers=ACROSS, preferred_element_type=jnp.float32
    )
    size = here.shape[0]

    def traces(k):
        at = wanted[k] % size
        return jnp.where(wanted[k] < size, here[at], there[at])

    rows = across(traces(0), near[...])
    far = jnp.concatenate([traces(1 + k) for k in range(count)], axis=0)
    products = across(far, far_v[...])
    group = lax.broadcasted_iota(jnp.int32, (E, count * rank), 1) // rank
    weights = jnp.zeros((E, count * rank), jnp.float32)
    for k in range(count):
        weights = jnp.where(group == k, products[k * E : (k + 1) * E], weights)
    rows = rows + jnp.dot(
        weights.astype(jnp.bfloat16), far_u[...], preferred_element_type=jnp.float32
    )
    high = rows.astype(jnp.bfloat16)
    rest = rows - high.astype(jnp.float32)
    middle = rest.astype(jnp.bfloat16)
    low = (rest - middle.astype(jnp.float32)).astype(jnp.bfloat16)
    placed = across(jnp.concatenate([high, middle, low], axis=0), order[...])
    placed = placed[:E] + (placed[E : 2 * E] + placed[2 * E :])
    if halves:
        half = placed.shape[1] // 2
        first = index("gy") == 0
        outs[0][...] = jnp.where(first, placed[:, :half], placed[:, half:])
        outs[1][...] = jnp.where(first, placed[:, half:], placed[:, :half])
    else:
        outs[0][...] = placed


def finish_kernel(count, *refs):
    parts = refs[:count]
    inv, slab, _, flux_out, out, held_flux, sems = refs[count:]
    side = index("gz")
    rows_x, _, width = slab.shape
    total = parts[0][...]
    if count == 2:
        total = total + parts[1][...]
    wide = jnp.concatenate([total, jnp.zeros((LANES - E, total.shape[1]), jnp.float32)], axis=0).T
    columns = []
    for start in range(0, width // E, LANES // E):
        column = wide[start * rows_x : (start + 1) * rows_x]
        for k in range(1, LANES // E):
            column = column + roll(wide[(start + k) * rows_x : (start + k + 1) * rows_x], k * E, 1)
        columns.append(column)
    flux = jnp.concatenate(columns, axis=1)
    held_flux[...] = flux[:, None, :]
    out_copy = pltpu.make_async_copy(held_flux, flux_out, sems.at[0])
    out_copy.start()
    added = (flux * inv[0])[:, None, :]
    row = lax.broadcasted_iota(jnp.int32, slab.shape, 1)
    slab[...] = slab[...] + jnp.where(row == side * (ROWS - 1), added, 0.0)
    top = pl.multiple_of(side * (out.shape[1] - ROWS), ROWS)
    copy = pltpu.make_async_copy(slab, out.at[:, pl.ds(top, ROWS), :], sems.at[1])
    copy.start()
    out_copy.wait()
    copy.wait()


def row_edge_kernel(source, inv, *messages):
    odd = index("gx") % 2
    rows_x, _, width = source.shape
    for number, message in enumerate(messages):
        for k in range(HALO):
            last = rows_x - HALO + k
            message[k, :, :width] = choose(odd, source[k], source[last], number)
            message[k, :, width:] = choose(odd, inv[k], inv[last], number)


def side_edge_kernel(nx, source, inv, *refs):
    odd_x, odd_y = index("gx") % 2, index("gy") % 2
    got_x, messages = [r[...] for r in refs[:nx]], refs[nx:]
    rows_x, _, width = source.shape
    cells = width // E
    halo = HALO * E

    def put(rows, first, last, c):
        lane = lane_ids(c)
        low = jnp.where(lane < halo, first, roll(c, halo, 2))
        high = jnp.where(lane < halo, roll(last, halo, 2), roll(c, halo - (cells - HALO), 2))
        for number, message in enumerate(messages):
            message[rows] = choose(odd_y, low, high, number)

    put(slice(HALO, HALO + rows_x), source[:, :, :LANES], source[:, :, width - LANES :], inv[...])
    for rows, edge in (
        (slice(0, HALO), from_low(odd_x, got_x)),
        (slice(HALO + rows_x, None), from_high(odd_x, got_x)),
    ):
        put(rows, edge[:, :, :LANES], edge[:, :, width - LANES : width], edge[:, :, width:])


def widen(cells, ring, s, c, left, right):
    lane = lane_ids(right)
    width = HALO * E
    axis = right.ndim - 1
    zero = jnp.zeros_like(right)
    after = jnp.where(lane < width, right, zero)
    before = jnp.where(lane >= LANES - width, roll(left, LANES - width, axis), zero)
    pads = [after + before] if ring - cells == LANES // E else [after, before]
    own = jnp.where(lane < cells, c, zero)
    c_after = jnp.where((lane >= cells) & (lane < cells + HALO), roll(right, cells - width, axis), zero)
    c_before = jnp.where(
        (lane >= ring - HALO) & (lane < ring), roll(left, ring - HALO - width, axis), zero
    )
    return [s, *pads], own + c_after + c_before


def depth_edge_kernel(cells, ring, nx, ny, source, inv, *refs):
    odd_x, odd_y, side = index("gx") % 2, index("gy") % 2, index("gz")
    got_x, got_y, out = refs[:nx], refs[nx : nx + ny], refs[-1]
    rows_x, depth, width = source.shape
    inner = lambda r: jnp.where(side == 0, r[:, depth - ROWS :, :], r[:, :ROWS, :])
    got = [inner(r) for r in got_y]
    left, right = from_low(odd_y, got), from_high(odd_y, got)
    edges = [inner(r) for r in got_x]
    below, above = from_low(odd_x, edges), from_high(odd_x, edges)
    for rows, s, c in (
        (slice(0, HALO), below[:, :, :width], below[:, :, width:]),
        (slice(HALO, HALO + rows_x), inner(source), inner(inv)),
        (slice(HALO + rows_x, rows_x + 2 * HALO), above[:, :, :width], above[:, :, width:]),
    ):
        parts, compact = widen(cells, ring, s, c, left[rows], right[rows])
        out[rows] = jnp.concatenate([*parts, compact], axis=2)


def assemble_kernel(cells, ring, nx, ny, source, inv, *refs):
    odd_x, odd_y, side = index("gx") % 2, index("gy") % 2, index("gz")
    got_x, got_y, got_z = refs[:nx], refs[nx : nx + ny], refs[nx + ny]
    ext_s, ext_i, one, compacts, matrix = refs[nx + ny + 1 :]
    rows_x, depth, width = source.shape
    wide = ring * E
    all_z = depth + ROWS
    total = ext_s.shape[0]
    matrix[...] = spread_matrix(ring, wide)
    row = lax.broadcasted_iota(jnp.int32, (ROWS, LANES), 0)
    start = side * (ROWS - HALO)
    near = (row >= start) & (row < start + HALO)

    def place(x, s, c):
        got = [r[x] for r in got_y]
        parts, compact = widen(cells, ring, s, c, from_low(odd_y, got), from_high(odd_y, got))
        zone = got_z[x]
        lanes = jnp.where(near, zone[:, wide:], 0.0)
        first = pl.ds(pl.multiple_of(x * all_z, ROWS), depth)
        rest = pl.ds(pl.multiple_of(x * all_z + depth, ROWS), ROWS)
        compacts[first, :] = compact
        compacts[rest, :] = lanes
        at = 0
        for part in parts:
            ext_s[first, at : at + part.shape[1]] = part
            at += part.shape[1]
        ext_s[rest, :] = zone[:, :wide]

    def own(x, _):
        place(x + HALO, source[x], inv[x])
        return 0

    repeat(0, rows_x, own, 4)
    for k in range(HALO):
        got = [r[k] for r in got_x]
        below, above = from_low(odd_x, got), from_high(odd_x, got)
        place(k, below[:, :width], below[:, width:])
        place(rows_x + HALO + k, above[:, :width], above[:, width:])
    chunk = max(n for n in range(2 * ROWS, 321, 2 * ROWS) if total % n == 0)

    def expand(n, _):
        rows = pl.ds(pl.multiple_of(n * chunk, 2 * ROWS), chunk)
        some = packed(compacts[rows, :], ring)
        inverse = jnp.dot(some, matrix[...], preferred_element_type=jnp.float32)
        ext_i[rows, :] = inverse
        one[rows, :] = ext_s[rows, :] * inverse
        return 0

    lax.fori_loop(0, total // chunk, expand, 0)


def repeat(first, last, step, most):
    count = last - first
    unroll = max(n for n in range(1, most + 1) if count % n == 0)
    lax.fori_loop(first, last, step, 0, unroll=unroll)


def swept(ext_s, ext_i, old, x, all_z, depth, width, store):
    at = lambda x, rows: pl.ds(pl.multiple_of(x * all_z, ROWS), rows)
    tiles = old.shape[1] // LANES
    lane = lax.broadcasted_iota(jnp.int32, (all_z, LANES), 1)
    known = {}

    def tile(j):
        j %= tiles
        if j not in known:
            u = old[at(x, all_z), j * LANES : (j + 1) * LANES]
            known[j] = (u, roll(u, E, 1), roll(u, -E, 1))
        return known[j]

    for j in range(width // LANES):
        columns = slice(j * LANES, (j + 1) * LANES)
        here = tile(j)
        beside = old[at(x - 1, depth), columns] + old[at(x + 1, depth), columns]
        up = roll(here[0], 1, 0) + roll(here[0], -1, 0)
        side = jnp.where(lane < E, tile(j - 1)[1], here[1])
        side = side + jnp.where(lane >= LANES - E, tile(j + 1)[2], here[2])
        beside = beside + (up + side)[:depth]
        new = (ext_s[at(x, depth), columns] + beside) * ext_i[at(x, depth), columns]
        store(columns, new)


def sweep_kernel(all_z, ext_s, ext_i, old, new):
    def step(x, _):
        def store(columns, value):
            new[pl.ds(pl.multiple_of(x * all_z, ROWS), all_z), columns] = value

        swept(ext_s, ext_i, old, x, all_z, all_z, old.shape[1], store)
        return 0

    repeat(1, old.shape[0] // all_z - 1, step, 6)


def last_sweep_kernel(ext_s, ext_i, old, out, slab, done, sems):
    side = index("gz")
    rows_x, depth, width = out.shape
    all_z = depth + ROWS

    def step(x, _):
        def store(columns, value):
            done[x, :, columns] = value
            slab[x, :, columns] = jnp.where(side == 0, value[:ROWS], value[depth - ROWS :])

        swept(ext_s, ext_i, old, x + HALO, all_z, depth, width, store)
        return 0

    pieces = sems.shape[0]
    size = rows_x // pieces
    copies = []
    for n in range(pieces):
        repeat(n * size, (n + 1) * size, step, 4)
        rows = slice(n * size, (n + 1) * size)
        copies.append(pltpu.make_async_copy(done.at[rows], out.at[rows], sems.at[n]))
        copies[-1].start()
    for copy in copies:
        copy.wait()


def body(source, coef, face_trace, near_col, far_col, near_tile, far_u, far_v):
    rows_x, depth, width = source.shape
    cells = coef.shape[2]
    groups = lax.axis_size("gy")
    size_x = lax.axis_size("gx")
    tile = near_tile.shape[3]
    count = far_u.shape[3]
    rank = far_u.shape[4]
    nx, ny = message_count("gx"), message_count("gy")
    bf16 = jnp.bfloat16
    both = [(0, 1), (1, 0)]
    pad = LANES if groups == 2 else 2 * LANES
    ring = (width + pad) // E
    wide = width + pad
    all_x, all_z = rows_x + 2 * HALO, depth + ROWS
    part = rows_x * cells
    halves = groups == 2
    coef = coef.transpose(0, 2, 1)
    held_source = held(source)

    planes = vector((3, rows_x, width))
    inv, s_face, i_face, *face_x = call(
        functools.partial(face_start_kernel, nx), (kept(source), kept(coef)),
        [vector((rows_x, depth, LANES)), planes, planes] + [vector((ROWS, width))] * nx,
        in_specs=[MAIN, MAIN],
        scratch=(vector((rows_x, ROWS, width)), vector(coef.shape), pltpu.SemaphoreType.DMA((2,))),
    )
    got_x = swap(face_x, "gx")
    face_y = call(
        functools.partial(face_side_kernel, nx), (s_face, i_face, *got_x),
        [vector((2 * rows_x + ROWS, LANES))] * ny, work=200,
    )
    vol_x = call(
        row_edge_kernel, (held_source, inv), [vector((HALO, depth, width + LANES))] * nx, work=200,
        after=(face_y[0],),
    )
    got_vol_x = swap(vol_x, "gx")
    got_y = swap(face_y, "gy")
    ext = pltpu.VMEM((2, rows_x + 2 * ROWS, width + LANES), jnp.float32)
    (face,) = call(
        functools.partial(face_sweep_kernel, nx, ny), (s_face, i_face, *got_x, *got_y),
        [(vector if halves else plain)((E, part), bf16)], scratch=(ext, ext), work=500,
    )
    if halves:
        faces = (face, held(lax.ppermute(face, "gy", both)))
    else:
        faces = (held(lax.all_gather(face, "gy", axis=1, tiled=True)),)

    order, spot = call(
        order_kernel, (face_trace, near_col.reshape(1), far_col.reshape(count)),
        [vector((tile, tile), bf16), pltpu.SMEM((count + 1,), jnp.int32)],
        in_specs=[VECTOR, SCALAR, SCALAR], out_specs=[VECTOR, SCALAR], work=2000, after=(face,),
    )
    (traces,) = call(trace_kernel, (*faces, order), [vector((1, E, tile), bf16)])
    vol_y = call(
        functools.partial(side_edge_kernel, nx), (held_source, inv, *got_vol_x),
        [vector((all_x, depth, LANES))] * ny, work=300, after=(traces,),
    )
    got_vol_y = swap(vol_y, "gy")
    steps = doubling(size_x)
    for step in steps:
        other = held(lax.ppermute(traces, "gx", [(i, i ^ step) for i in range(size_x)]))
        twice = (2 * traces.shape[0], E, tile)
        before = ()
        if step == 1:
            (vol_z,) = call(
                functools.partial(depth_edge_kernel, cells, ring, nx, ny),
                (held_source, inv, *got_vol_x, *got_vol_y),
                [vector((all_x, ROWS, wide + LANES))], work=500, after=(traces,),
            )
            got_vol_z = held(lax.ppermute(vol_z, "gz", both))
            ext = vector((all_x * all_z, wide))
            ext_s, ext_i, one = call(
                functools.partial(assemble_kernel, cells, ring, nx, ny),
                (held_source, inv, *got_vol_x, *got_vol_y, got_vol_z), [ext, ext, ext], work=3000,
                scratch=(vector((all_x * all_z, LANES)), vector((LANES, wide), bf16)),
            )
            before = (one,)
        (traces,) = call(
            join_kernel, (traces, other), [vector(twice, bf16)], work=300, after=before
        )
    other = held(lax.ppermute(traces, "gz", both))
    (two,) = call(
        functools.partial(sweep_kernel, all_z), (ext_s, ext_i, one), [ext], work=2500,
        after=(traces,),
    )

    rows = call(
        functools.partial(operator_kernel, halves),
        (spot, traces, other, held(near_tile.reshape(tile, tile)),
         held(far_v.reshape(count * rank, tile)), held(far_u.reshape(count * rank, tile)), order),
        [vector((E, part))] * 2 if halves else [plain((E, tile))],
        in_specs=[SCALAR] + [VECTOR] * 6, work=2500, after=(two,),
    )
    if halves:
        sums = (rows[0], held(lax.ppermute(rows[1], "gy", both)))
    else:
        sums = (held(lax.psum_scatter(rows[0], "gy", scatter_dimension=1, tiled=True)),)
    (three,) = call(
        functools.partial(sweep_kernel, all_z), (ext_s, ext_i, two), [ext], work=2500, after=rows,
    )
    pieces = 4
    field, slab = call(
        last_sweep_kernel, (ext_s, ext_i, three),
        [plain(source.shape), vector((rows_x, ROWS, width))], work=2000,
        out_specs=[MAIN, VECTOR],
        scratch=(vector(source.shape), pltpu.SemaphoreType.DMA((pieces,))),
    )

    flux, result = call(
        functools.partial(finish_kernel, len(sums)), (*sums, i_face, slab, field),
        [plain((rows_x, 1, width)), plain(source.shape)],
        in_specs=[VECTOR] * (len(sums) + 2) + [MAIN], out_specs=[MAIN, MAIN],
        scratch=(vector((rows_x, 1, width)), pltpu.SemaphoreType.DMA((2,))),
        input_output_aliases={len(sums) + 2: 1},
    )
    return (result, flux)


def solution(mesh):
    return jax.shard_map(
        body,
        mesh=mesh,
        in_specs=(
            P("gx", "gz", "gy"),
            P("gx", "gz", "gy"),
            P("gx", "gz", None),
            P("gx", "gz", "gy"),
            P("gx", "gz", "gy", None),
            P("gx", "gz", "gy", None, None),
            P("gx", "gz", "gy", None, None, None),
            P("gx", "gz", "gy", None, None, None),
        ),
        out_specs=(P("gx", "gz", "gy"), P("gx", "gz", "gy")),
        check_vma=False,
    )
```

```python
import functools
import math

import jax
import jax.numpy as jnp
from jax import lax
from jax.experimental import pallas as pl
from jax.experimental.pallas import tpu as pltpu
from jax.sharding import PartitionSpec as P

E = 32
LANES = 128
ROWS = 8
HALO = 3
NEAR = 3


def roll(value, shift, axis):
    return pltpu.roll(value, shift % value.shape[axis], axis)


def lane_ids(value):
    return lax.broadcasted_iota(jnp.int32, value.shape, value.ndim - 1)


def held(value):
    return pltpu.with_memory_space_constraint(value, pltpu.VMEM)


def kept(value):
    return pltpu.with_memory_space_constraint(value, pltpu.HBM)


VECTOR = pl.BlockSpec(memory_space=pltpu.VMEM)
SCALAR = pl.BlockSpec(memory_space=pltpu.SMEM)
PLACED = pl.BlockSpec(memory_space=pl.ANY)
MAIN = pl.BlockSpec(memory_space=pltpu.HBM)


def vector(shape, dtype=jnp.float32):
    return pltpu.VMEM(shape, dtype)


def plain(shape, dtype=jnp.float32):
    return jax.ShapeDtypeStruct(shape, dtype)


def size_of(a):
    return math.prod(a.shape) * jnp.dtype(a.dtype).itemsize


def call(kernel, operands, out_shape, in_specs=None, out_specs=None, scratch=(), room=8, work=1000, after=(), **kw):
    given, tokens = len(operands), len(after)

    def body(*refs):
        kernel(*refs[:given], *refs[given + tokens :])

    return pl.pallas_call(
        body,
        out_shape=out_shape,
        in_specs=(in_specs or [VECTOR] * given) + [PLACED] * tokens,
        out_specs=out_specs or [VECTOR] * len(out_shape),
        scratch_shapes=list(scratch),
        compiler_params=pltpu.CompilerParams(vmem_limit_bytes=room * 1024 * 1024),
        cost_estimate=pl.CostEstimate(flops=0, bytes_accessed=work * 3000, transcendentals=0),
        **kw,
    )(*operands, *after)


def index(axis):
    return lax.axis_index(axis).astype(jnp.int32)


def pairs(count):
    first = [(i, i ^ 1) for i in range(count)]
    second = [(i, i + 1) for i in range(1, count - 1, 2)]
    return first, second + [(b, a) for a, b in second]


def swap(messages, axis):
    count = lax.axis_size(axis)
    return [held(lax.ppermute(m, axis, p)) for m, p in zip(messages, pairs(count))]


def doubling(count):
    steps = []
    while count > 1:
        count //= 2
        steps.append(count)
    return steps


def message_count(axis):
    return 1 if lax.axis_size(axis) == 2 else 2


def choose(odd, low, high, number):
    return jnp.where(odd == number, high, low)


def from_low(odd, received):
    other = received[1] if len(received) == 2 else jnp.zeros_like(received[0])
    return jnp.where(odd == 1, received[0], other)


def from_high(odd, received):
    other = received[1] if len(received) == 2 else jnp.zeros_like(received[0])
    return jnp.where(odd == 1, other, received[0])


def spread_matrix(cells, width):
    k = lax.broadcasted_iota(jnp.int32, (LANES, width), 0)
    cell = lax.broadcasted_iota(jnp.int32, (LANES, width), 1) // E
    part = k // 32
    hit = (k - part * 32 == cell) & (part < 3) & (cell < cells)
    return jnp.where(hit, 1.0, 0.0).astype(jnp.bfloat16)


def packed(compact, cells):
    compact = jnp.where(lane_ids(compact) < cells, compact, 0.0)
    high = compact.astype(jnp.bfloat16).astype(jnp.float32)
    rest = compact - high
    middle = rest.astype(jnp.bfloat16).astype(jnp.float32)
    low = (rest - middle).astype(jnp.bfloat16).astype(jnp.float32)
    axis = compact.ndim - 1
    return (high + roll(middle, 32, axis) + roll(low, 64, axis)).astype(jnp.bfloat16)


def spread(compact, width, cells):
    return jnp.dot(
        packed(compact, cells), spread_matrix(cells, width), preferred_element_type=jnp.float32
    )


def face_start_kernel(source, coef, held_source, inv, message, *refs):
    edges, (coefs, sems) = refs[:-2], refs[-2:]
    odd, side = index("gx") % 2, index("gz")
    rows_x, depth, width = source.shape
    cells = width // E
    copies = [
        pltpu.make_async_copy(coef, coefs, sems.at[0]),
        pltpu.make_async_copy(source, held_source, sems.at[1]),
    ]
    for copy in copies:
        copy.start()
    copies[0].wait()
    c = jnp.swapaxes(1.0 / (6.0 + coefs[...]), 1, 2)
    inv[...] = jnp.concatenate(
        [c, jnp.zeros((rows_x, depth, LANES - cells), jnp.float32)], axis=2
    )
    compact = jnp.zeros((rows_x, LANES), jnp.float32)
    for d in range(NEAR):
        plane = jnp.where(side == 0, inv[:, d, :], inv[:, depth - 1 - d, :])
        compact = compact + roll(plane, 32 * d, 1)
    for n in range(rows_x // ROWS):
        message[NEAR * rows_x :, n * LANES : (n + 1) * LANES] = compact[n * ROWS : (n + 1) * ROWS]
    copies[1].wait()
    for d in range(NEAR):
        plane = jnp.where(side == 0, held_source[:, d, :], held_source[:, depth - 1 - d, :])
        message[d * rows_x : (d + 1) * rows_x, :] = plane
    row_edges(odd, held_source, inv, edges)


def row_edges(odd, source, inv, messages):
    rows_x, _, width = source.shape
    for number, message in enumerate(messages):
        for k in range(HALO):
            last = rows_x - HALO + k
            message[k, :, :width] = choose(odd, source[k], source[last], number)
            message[k, :, width:] = choose(odd, inv[k], inv[last], number)


def face_side_kernel(groups, own, other, s_out, i_out, i_own, *messages):
    odd = index("gx") % 2
    if groups == 2:
        first = index("gy") == 0
        parts = [jnp.where(first, own[...], other[...]), jnp.where(first, other[...], own[...])]
    else:
        parts = [other[n] for n in range(groups)]
    width = own.shape[1]
    cells = width // E
    rows_x = i_own.shape[0]

    def inverse(part):
        pieces = [
            part[NEAR * rows_x :, n * LANES : (n + 1) * LANES] for n in range(rows_x // ROWS)
        ]
        compact = jnp.concatenate(pieces, axis=0)
        planes = jnp.concatenate([roll(compact, -32 * d, 1) for d in range(NEAR)], axis=0)
        return spread(planes, width, cells)

    i_own[...] = inverse(own[...])[:rows_x]
    s_all = jnp.concatenate([part[: NEAR * rows_x] for part in parts], axis=1)
    i_all = jnp.concatenate([inverse(part) for part in parts], axis=1)
    for all_planes, out in ((s_all, s_out), (i_all, i_out)):
        for d in range(NEAR):
            out[d] = all_planes[d * rows_x : (d + 1) * rows_x]
    for number, message in enumerate(messages):
        for k, all_planes in enumerate((s_all, i_all)):
            for d in range(2):
                row = 4 * k + 2 * d
                top = d * rows_x
                message[row : row + 2, :] = choose(
                    odd, all_planes[top : top + 2], all_planes[top + rows_x - 2 : top + rows_x], number
                )


def face_trace_kernel(nx, s_in, i_in, order, *refs):
    odd = index("gx") % 2
    got = [r[...] for r in refs[:nx]]
    out, ext_s, ext_i = refs[nx:]
    _, rows_x, width = s_in.shape
    below, above = from_low(odd, got), from_high(odd, got)
    ext_s[...] = jnp.zeros(ext_s.shape, jnp.float32)
    ext_i[...] = jnp.zeros(ext_i.shape, jnp.float32)
    first, last = ROWS, ROWS + rows_x
    for ext, own, k in ((ext_s, s_in, 0), (ext_i, i_in, 1)):
        for d in range(2):
            row = 4 * k + 2 * d
            ext[d, first:last, :width] = own[d]
            ext[d, first - 2 : first, :width] = below[row : row + 2]
            ext[d, last : last + 2, :width] = above[row : row + 2]

    def around(u):
        return roll(u, 1, 0) + roll(u, -1, 0) + roll(u, E, 1) + roll(u, -E, 1)

    s0, i0, i1 = ext_s[0], ext_i[0], ext_i[1]
    u0, u1 = s0 * i0, ext_s[1] * i1
    deep = s_in[2] * i_in[2]
    v0 = (s0 + (around(u0) + u1)) * i0
    own = (around(u1) + u0)[first:last, :width]
    v1 = (s_in[1] + (own + deep)) * i_in[1]
    face = (s_in[0] + (around(v0)[first:last, :width] + v1)) * i_in[0]
    pieces = []
    for cell in range(width // E):
        start = cell * E // LANES * LANES
        pieces.append(roll(face[:, start : start + LANES], -(cell * E - start), 1))
    stacked = jnp.concatenate(pieces, axis=0)
    values = stacked.T[:E].astype(jnp.bfloat16)
    out[0] = jnp.dot(values, order[...], preferred_element_type=jnp.float32).astype(jnp.bfloat16)


def order_kernel(place, near_col, far_col, order, spot):
    rows_x, _, cells_y = place.shape
    at = place[...].reshape(rows_x, cells_y) if rows_x == 1 else place[:, 0, :]
    trace = lax.broadcasted_iota(jnp.int32, (rows_x, order.shape[1]), 1)
    for y in range(cells_y):
        hit = at[:, y : y + 1] == trace
        order[y * rows_x : (y + 1) * rows_x, :] = jnp.where(hit, 1.0, 0.0).astype(jnp.bfloat16)
    at_x, at_z = index("gx"), index("gz")
    size_x = lax.axis_size("gx")
    for k in range(spot.shape[0]):
        block = near_col[0] if k == 0 else far_col[k - 1]
        apart = (block // 2) ^ at_x
        where = ((block % 2) ^ at_z) * size_x
        for n, step in enumerate(doubling(size_x)):
            where = where + jnp.where(apart & step > 0, 1 << n, 0)
        spot[k] = where


def join_kernel(one, two, out):
    count = one.shape[0]
    out[:count] = one[...]
    out[count:] = two[...]


ACROSS = (((1,), (1,)), ((), ()))


def operator_kernel(halves, wanted, here, there, near, far_v, far_u, order, *outs):
    count = wanted.shape[0] - 1
    rank = far_v.shape[0] // count
    across = functools.partial(
        lax.dot_general, dimension_numbers=ACROSS, preferred_element_type=jnp.float32
    )
    size = here.shape[0]

    def traces(k):
        at = wanted[k] % size
        return jnp.where(wanted[k] < size, here[at], there[at])

    rows = across(traces(0), near[...])
    far = jnp.concatenate([traces(1 + k) for k in range(count)], axis=0)
    products = across(far, far_v[...])
    group = lax.broadcasted_iota(jnp.int32, (E, count * rank), 1) // rank
    weights = jnp.zeros((E, count * rank), jnp.float32)
    for k in range(count):
        weights = jnp.where(group == k, products[k * E : (k + 1) * E], weights)
    rows = rows + jnp.dot(
        weights.astype(jnp.bfloat16), far_u[...], preferred_element_type=jnp.float32
    )
    high = rows.astype(jnp.bfloat16)
    rest = rows - high.astype(jnp.float32)
    middle = rest.astype(jnp.bfloat16)
    low = (rest - middle.astype(jnp.float32)).astype(jnp.bfloat16)
    placed = across(jnp.concatenate([high, middle, low], axis=0), order[...])
    placed = placed[:E] + (placed[E : 2 * E] + placed[2 * E :])
    if halves:
        half = placed.shape[1] // 2
        first = index("gy") == 0
        outs[0][...] = jnp.where(first, placed[:, :half], placed[:, half:])
        outs[1][...] = jnp.where(first, placed[:, half:], placed[:, :half])
    else:
        outs[0][...] = placed


def finish_kernel(count, *refs):
    parts = refs[:count]
    inv, slab, _, flux_out, out, held_flux, sems = refs[count:]
    side = index("gz")
    rows_x, _, width = slab.shape
    total = parts[0][...]
    if count == 2:
        total = total + parts[1][...]
    wide = jnp.concatenate([total, jnp.zeros((LANES - E, total.shape[1]), jnp.float32)], axis=0).T
    columns = []
    for start in range(0, width // E, LANES // E):
        column = wide[start * rows_x : (start + 1) * rows_x]
        for k in range(1, LANES // E):
            column = column + roll(wide[(start + k) * rows_x : (start + k + 1) * rows_x], k * E, 1)
        columns.append(column)
    flux = jnp.concatenate(columns, axis=1)
    held_flux[...] = flux[:, None, :]
    out_copy = pltpu.make_async_copy(held_flux, flux_out, sems.at[0])
    out_copy.start()
    added = (flux * inv[...])[:, None, :]
    row = lax.broadcasted_iota(jnp.int32, slab.shape, 1)
    slab[...] = slab[...] + jnp.where(row == side * (ROWS - 1), added, 0.0)
    top = pl.multiple_of(side * (out.shape[1] - ROWS), ROWS)
    copy = pltpu.make_async_copy(slab, out.at[:, pl.ds(top, ROWS), :], sems.at[1])
    copy.start()
    out_copy.wait()
    copy.wait()


def side_edge_kernel(nx, source, inv, *refs):
    odd_x, odd_y = index("gx") % 2, index("gy") % 2
    got_x, messages = [r[...] for r in refs[:nx]], refs[nx:]
    rows_x, _, width = source.shape
    cells = width // E
    halo = HALO * E

    def put(rows, first, last, c):
        lane = lane_ids(c)
        low = jnp.where(lane < halo, first, roll(c, halo, 2))
        high = jnp.where(lane < halo, roll(last, halo, 2), roll(c, halo - (cells - HALO), 2))
        for number, message in enumerate(messages):
            message[rows] = choose(odd_y, low, high, number)

    put(slice(HALO, HALO + rows_x), source[:, :, :LANES], source[:, :, width - LANES :], inv[...])
    for rows, edge in (
        (slice(0, HALO), from_low(odd_x, got_x)),
        (slice(HALO + rows_x, None), from_high(odd_x, got_x)),
    ):
        put(rows, edge[:, :, :LANES], edge[:, :, width - LANES : width], edge[:, :, width:])


def widen(cells, ring, s, c, left, right):
    lane = lane_ids(right)
    width = HALO * E
    axis = right.ndim - 1
    zero = jnp.zeros_like(right)
    after = jnp.where(lane < width, right, zero)
    before = jnp.where(lane >= LANES - width, roll(left, LANES - width, axis), zero)
    pads = [after + before] if ring - cells == LANES // E else [after, before]
    own = jnp.where(lane < cells, c, zero)
    c_after = jnp.where((lane >= cells) & (lane < cells + HALO), roll(right, cells - width, axis), zero)
    c_before = jnp.where(
        (lane >= ring - HALO) & (lane < ring), roll(left, ring - HALO - width, axis), zero
    )
    return [s, *pads], own + c_after + c_before


def depth_edge_kernel(cells, ring, nx, ny, source, inv, *refs):
    odd_x, odd_y, side = index("gx") % 2, index("gy") % 2, index("gz")
    got_x, got_y, (two_out, one_out) = refs[:nx], refs[nx : nx + ny], refs[nx + ny :]
    rows_x, depth, width = source.shape
    wide = ring * E
    rows = two_out.shape[1]
    packs = jnp.zeros((rows, LANES), jnp.float32)
    for k in range(HALO):
        inner = lambda r: jnp.where(side == 0, r[:, depth - HALO + k, :], r[:, k, :])
        edges = [inner(r) for r in got_x]
        below, above = from_low(odd_x, edges), from_high(odd_x, edges)
        empty = jnp.zeros((rows - rows_x - 2 * HALO, LANES), jnp.float32)
        beside = [jnp.concatenate([inner(r), empty], axis=0) for r in got_y]
        own = jnp.concatenate([inner(source), inner(inv)], axis=1)
        blank = jnp.zeros((empty.shape[0], width + LANES), jnp.float32)
        all_rows = jnp.concatenate([below, own, above, blank], axis=0)
        parts, compact = widen(
            cells, ring, all_rows[:, :width], all_rows[:, width:],
            from_low(odd_y, beside), from_high(odd_y, beside),
        )
        compact = jnp.where(lane_ids(compact) < ring, compact, 0.0)
        packs = packs + roll(compact, 32 * k, 1)
        out = jnp.concatenate(parts, axis=1)
        if k < 2:
            two_out[k] = out
        else:
            one_out[:, :wide] = out
    one_out[:, wide:] = packs


def assemble_kernel(cells, ring, nx, ny, source, inv, *refs):
    odd_x, odd_y, side = index("gx") % 2, index("gy") % 2, index("gz")
    got_x, got_y = refs[:nx], refs[nx : nx + ny]
    z_two, z_one, ext_s, ext_i, one, compacts, matrix = refs[nx + ny :]
    rows_x, depth, width = source.shape
    wide = ring * E
    all_z = depth + ROWS
    total = ext_s.shape[0]
    matrix[...] = spread_matrix(ring, wide)
    start = side * (ROWS - HALO)

    def spaced(rows):
        at = lax.broadcasted_iota(jnp.int32, (ROWS, rows[0].shape[1]), 0) - start
        tile = jnp.zeros(at.shape, jnp.float32)
        for k, value in enumerate(rows):
            tile = jnp.where(at == k, value, tile)
        return tile

    def place(x, s, c):
        got = [r[x] for r in got_y]
        parts, compact = widen(cells, ring, s, c, from_low(odd_y, got), from_high(odd_y, got))
        last = z_one[pl.ds(x, 1), :]
        zone = spaced([z_two[0, pl.ds(x, 1), :], z_two[1, pl.ds(x, 1), :], last[:, :wide]])
        packs = jnp.broadcast_to(last[:, wide:], (ROWS, LANES))
        lanes = spaced([roll(packs, -32 * k, 1) for k in range(HALO)])
        first = pl.ds(pl.multiple_of(x * all_z, ROWS), depth)
        rest = pl.ds(pl.multiple_of(x * all_z + depth, ROWS), ROWS)
        compacts[first, :] = compact
        compacts[rest, :] = lanes
        at = 0
        for part in parts:
            ext_s[first, at : at + part.shape[1]] = part
            at += part.shape[1]
        ext_s[rest, :] = zone

    def own(x, _):
        place(x + HALO, source[x], inv[x])
        return 0

    repeat(0, rows_x, own, 4)
    for k in range(HALO):
        got = [r[k] for r in got_x]
        below, above = from_low(odd_x, got), from_high(odd_x, got)
        place(k, below[:, :width], below[:, width:])
        place(rows_x + HALO + k, above[:, :width], above[:, width:])
    chunk = max(n for n in range(2 * ROWS, 321, 2 * ROWS) if total % n == 0)

    def expand(n, _):
        rows = pl.ds(pl.multiple_of(n * chunk, 2 * ROWS), chunk)
        some = packed(compacts[rows, :], ring)
        inverse = jnp.dot(some, matrix[...], preferred_element_type=jnp.float32)
        ext_i[rows, :] = inverse
        one[rows, :] = ext_s[rows, :] * inverse
        return 0

    lax.fori_loop(0, total // chunk, expand, 0)


def repeat(first, last, step, most):
    count = last - first
    unroll = max(n for n in range(1, most + 1) if count % n == 0)
    lax.fori_loop(first, last, step, 0, unroll=unroll)


def swept(ext_s, ext_i, old, x, all_z, depth, width, store):
    at = lambda x, rows: pl.ds(pl.multiple_of(x * all_z, ROWS), rows)
    tiles = old.shape[1] // LANES
    lane = lax.broadcasted_iota(jnp.int32, (depth, LANES), 1)
    known = {}

    def tile(j):
        j %= tiles
        if j not in known:
            u = old[at(x, all_z), j * LANES : (j + 1) * LANES]
            known[j] = (u, roll(u[:depth], E, 1), roll(u[:depth], -E, 1))
        return known[j]

    for j in range(width // LANES):
        columns = slice(j * LANES, (j + 1) * LANES)
        here = tile(j)
        beside = old[at(x - 1, depth), columns] + old[at(x + 1, depth), columns]
        up = roll(here[0], 1, 0) + roll(here[0], -1, 0)
        side = jnp.where(lane < E, tile(j - 1)[1], here[1])
        side = side + jnp.where(lane >= LANES - E, tile(j + 1)[2], here[2])
        beside = beside + (up[:depth] + side)
        new = (ext_s[at(x, depth), columns] + beside) * ext_i[at(x, depth), columns]
        store(columns, new)


def sweep_kernel(all_z, ext_s, ext_i, old, new):
    def step(x, _):
        def store(columns, value):
            new[pl.ds(pl.multiple_of(x * all_z, ROWS), all_z), columns] = value

        swept(ext_s, ext_i, old, x, all_z, all_z, old.shape[1], store)
        return 0

    repeat(1, old.shape[0] // all_z - 1, step, 12)


def last_sweep_kernel(ext_s, ext_i, old, out, slab, done, sems):
    side = index("gz")
    rows_x, depth, width = out.shape
    all_z = depth + ROWS

    def step(x, _):
        def store(columns, value):
            done[x, :, columns] = value
            slab[x, :, columns] = jnp.where(side == 0, value[:ROWS], value[depth - ROWS :])

        swept(ext_s, ext_i, old, x + HALO, all_z, depth, width, store)
        return 0

    pieces = sems.shape[0]
    size = rows_x // pieces
    copies = []
    for n in range(pieces):
        repeat(n * size, (n + 1) * size, step, 8)
        rows = slice(n * size, (n + 1) * size)
        copies.append(pltpu.make_async_copy(done.at[rows], out.at[rows], sems.at[n]))
        copies[-1].start()
    for copy in copies:
        copy.wait()


def body(source, coef, face_trace, near_col, far_col, near_tile, far_u, far_v):
    rows_x, depth, width = source.shape
    cells = coef.shape[2]
    groups = lax.axis_size("gy")
    size_x = lax.axis_size("gx")
    tile = near_tile.shape[3]
    count = far_u.shape[3]
    rank = far_u.shape[4]
    nx, ny = message_count("gx"), message_count("gy")
    bf16 = jnp.bfloat16
    both = [(0, 1), (1, 0)]
    pad = LANES if groups == 2 else 2 * LANES
    ring = (width + pad) // E
    wide = width + pad
    all_x, all_z = rows_x + 2 * HALO, depth + ROWS
    part = rows_x * cells
    halves = groups == 2
    coef = coef.transpose(0, 2, 1)

    held_source, inv, near, *vol_x = call(
        face_start_kernel, (kept(source), kept(coef)),
        [vector(source.shape), vector((rows_x, depth, LANES)), vector((NEAR * rows_x + ROWS, width))]
        + [vector((HALO, depth, width + LANES))] * nx,
        in_specs=[MAIN, MAIN],
        scratch=(vector(coef.shape), pltpu.SemaphoreType.DMA((2,))),
    )
    if halves:
        other = held(lax.ppermute(near, "gy", both))
    else:
        other = held(lax.all_gather(near, "gy", axis=0, tiled=False))
    got_vol_x = swap(vol_x, "gx")
    full = vector((NEAR, rows_x, width * groups))
    s_face, i_face, i_own, *face_x = call(
        functools.partial(face_side_kernel, groups), (near, other),
        [full, full, vector((rows_x, width))] + [vector((ROWS, width * groups))] * nx, work=500,
    )
    got_x = swap(face_x, "gx")
    order, spot = call(
        order_kernel, (face_trace, near_col.reshape(1), far_col.reshape(count)),
        [vector((tile, tile), bf16), pltpu.SMEM((count + 1,), jnp.int32)],
        in_specs=[VECTOR, SCALAR, SCALAR], out_specs=[VECTOR, SCALAR], work=2000, after=(near,),
    )
    vol_y = call(
        functools.partial(side_edge_kernel, nx), (held_source, inv, *got_vol_x),
        [vector((all_x, depth, LANES))] * ny, work=300, after=(order, *got_x),
    )
    got_vol_y = swap(vol_y, "gy")

    ext = pltpu.VMEM((2, rows_x + 2 * ROWS, width * groups + LANES), jnp.float32)
    (traces,) = call(
        functools.partial(face_trace_kernel, nx), (s_face, i_face, order, *got_x),
        [vector((1, E, tile), bf16)], scratch=(ext, ext),
    )
    steps = doubling(size_x)
    for step in steps:
        other = held(lax.ppermute(traces, "gx", [(i, i ^ step) for i in range(size_x)]))
        twice = (2 * traces.shape[0], E, tile)
        before = ()
        if step == 1:
            rounded = -(-all_x // ROWS) * ROWS
            vol_z = call(
                functools.partial(depth_edge_kernel, cells, ring, nx, ny),
                (held_source, inv, *got_vol_x, *got_vol_y),
                [vector((2, rounded, wide)), vector((rounded, wide + LANES))], work=500,
                after=(traces,),
            )
            got_vol_z = [held(lax.ppermute(v, "gz", both)) for v in vol_z]
            ext = vector((all_x * all_z, wide))
            ext_s, ext_i, one = call(
                functools.partial(assemble_kernel, cells, ring, nx, ny),
                (held_source, inv, *got_vol_x, *got_vol_y, *got_vol_z), [ext, ext, ext], work=3000,
                scratch=(vector((all_x * all_z, LANES)), vector((LANES, wide), bf16)),
            )
            (two,) = call(
                functools.partial(sweep_kernel, all_z), (ext_s, ext_i, one), [ext], work=2500
            )
            before = (two,)
        (traces,) = call(
            join_kernel, (traces, other), [vector(twice, bf16)], work=300, after=before
        )
    other = held(lax.ppermute(traces, "gz", both))
    (three,) = call(
        functools.partial(sweep_kernel, all_z), (ext_s, ext_i, two), [ext], work=2500,
        after=(traces,),
    )

    rows = call(
        functools.partial(operator_kernel, halves),
        (spot, traces, other, held(near_tile.reshape(tile, tile)),
         held(far_v.reshape(count * rank, tile)), held(far_u.reshape(count * rank, tile)), order),
        [vector((E, part))] * 2 if halves else [plain((E, tile))],
        in_specs=[SCALAR] + [VECTOR] * 6, work=2500, after=(three,),
    )
    if halves:
        sums = (rows[0], held(lax.ppermute(rows[1], "gy", both)))
    else:
        sums = (held(lax.psum_scatter(rows[0], "gy", scatter_dimension=1, tiled=True)),)
    pieces = 4
    field, slab = call(
        last_sweep_kernel, (ext_s, ext_i, three),
        [plain(source.shape), vector((rows_x, ROWS, width))], work=2000,
        out_specs=[MAIN, VECTOR], after=rows,
        scratch=(vector(source.shape), pltpu.SemaphoreType.DMA((pieces,))),
    )

    flux, result = call(
        functools.partial(finish_kernel, len(sums)), (*sums, i_own, slab, field),
        [plain((rows_x, 1, width)), plain(source.shape)],
        in_specs=[VECTOR] * (len(sums) + 2) + [MAIN], out_specs=[MAIN, MAIN],
        scratch=(vector((rows_x, 1, width)), pltpu.SemaphoreType.DMA((2,))),
        input_output_aliases={len(sums) + 2: 1},
    )
    return (result, flux)


def solution(mesh):
    return jax.shard_map(
        body,
        mesh=mesh,
        in_specs=(
            P("gx", "gz", "gy"),
            P("gx", "gz", "gy"),
            P("gx", "gz", None),
            P("gx", "gz", "gy"),
            P("gx", "gz", "gy", None),
            P("gx", "gz", "gy", None, None),
            P("gx", "gz", "gy", None, None, None),
            P("gx", "gz", "gy", None, None, None),
        ),
        out_specs=(P("gx", "gz", "gy"), P("gx", "gz", "gy")),
        check_vma=False,
    )
```

```python
import functools
import math

import jax
import jax.numpy as jnp
from jax import lax
from jax.experimental import pallas as pl
from jax.experimental.pallas import tpu as pltpu
from jax.sharding import PartitionSpec as P

E = 32
LANES = 128
ROWS = 8
HALO = 3
NEAR = 3


def roll(value, shift, axis):
    return pltpu.roll(value, shift % value.shape[axis], axis)


def lane_ids(value):
    return lax.broadcasted_iota(jnp.int32, value.shape, value.ndim - 1)


def held(value):
    return pltpu.with_memory_space_constraint(value, pltpu.VMEM)


def kept(value):
    return pltpu.with_memory_space_constraint(value, pltpu.HBM)


VECTOR = pl.BlockSpec(memory_space=pltpu.VMEM)
SCALAR = pl.BlockSpec(memory_space=pltpu.SMEM)
PLACED = pl.BlockSpec(memory_space=pl.ANY)
MAIN = pl.BlockSpec(memory_space=pltpu.HBM)


def vector(shape, dtype=jnp.float32):
    return pltpu.VMEM(shape, dtype)


def plain(shape, dtype=jnp.float32):
    return jax.ShapeDtypeStruct(shape, dtype)


def size_of(a):
    return math.prod(a.shape) * jnp.dtype(a.dtype).itemsize


def call(kernel, operands, out_shape, in_specs=None, out_specs=None, scratch=(), room=8, work=1000, after=(), **kw):
    given, tokens = len(operands), len(after)

    def body(*refs):
        kernel(*refs[:given], *refs[given + tokens :])

    return pl.pallas_call(
        body,
        out_shape=out_shape,
        in_specs=(in_specs or [VECTOR] * given) + [PLACED] * tokens,
        out_specs=out_specs or [VECTOR] * len(out_shape),
        scratch_shapes=list(scratch),
        compiler_params=pltpu.CompilerParams(vmem_limit_bytes=room * 1024 * 1024),
        cost_estimate=pl.CostEstimate(flops=0, bytes_accessed=work * 3000, transcendentals=0),
        **kw,
    )(*operands, *after)


def index(axis):
    return lax.axis_index(axis).astype(jnp.int32)


def pairs(count):
    first = [(i, i ^ 1) for i in range(count)]
    second = [(i, i + 1) for i in range(1, count - 1, 2)]
    return first, second + [(b, a) for a, b in second]


def swap(messages, axis):
    count = lax.axis_size(axis)
    return [held(lax.ppermute(m, axis, p)) for m, p in zip(messages, pairs(count))]


def doubling(count):
    steps = []
    while count > 1:
        count //= 2
        steps.append(count)
    return steps


def message_count(axis):
    return 1 if lax.axis_size(axis) == 2 else 2


def choose(odd, low, high, number):
    return jnp.where(odd == number, high, low)


def from_low(odd, received):
    other = received[1] if len(received) == 2 else jnp.zeros_like(received[0])
    return jnp.where(odd == 1, received[0], other)


def from_high(odd, received):
    other = received[1] if len(received) == 2 else jnp.zeros_like(received[0])
    return jnp.where(odd == 1, other, received[0])


def spread_matrix(cells, width):
    k = lax.broadcasted_iota(jnp.int32, (LANES, width), 0)
    cell = lax.broadcasted_iota(jnp.int32, (LANES, width), 1) // E
    part = k // 32
    hit = (k - part * 32 == cell) & (part < 3) & (cell < cells)
    return jnp.where(hit, 1.0, 0.0).astype(jnp.bfloat16)


def packed(compact, cells):
    compact = jnp.where(lane_ids(compact) < cells, compact, 0.0)
    high = compact.astype(jnp.bfloat16).astype(jnp.float32)
    rest = compact - high
    middle = rest.astype(jnp.bfloat16).astype(jnp.float32)
    low = (rest - middle).astype(jnp.bfloat16).astype(jnp.float32)
    axis = compact.ndim - 1
    return (high + roll(middle, 32, axis) + roll(low, 64, axis)).astype(jnp.bfloat16)


def spread(compact, width, cells):
    return jnp.dot(
        packed(compact, cells), spread_matrix(cells, width), preferred_element_type=jnp.float32
    )


def face_start_kernel(source, coef, held_source, inv, message, *refs):
    edges, (coefs, sems) = refs[:-2], refs[-2:]
    odd, side = index("gx") % 2, index("gz")
    rows_x, depth, width = source.shape
    cells = width // E
    copies = [
        pltpu.make_async_copy(coef, coefs, sems.at[0]),
        pltpu.make_async_copy(source, held_source, sems.at[1]),
    ]
    for copy in copies:
        copy.start()
    copies[0].wait()
    c = jnp.swapaxes(1.0 / (6.0 + coefs[...]), 1, 2)
    inv[...] = jnp.concatenate(
        [c, jnp.zeros((rows_x, depth, LANES - cells), jnp.float32)], axis=2
    )
    compact = jnp.zeros((rows_x, LANES), jnp.float32)
    for d in range(NEAR):
        plane = jnp.where(side == 0, inv[:, d, :], inv[:, depth - 1 - d, :])
        compact = compact + roll(plane, 32 * d, 1)
    for n in range(rows_x // ROWS):
        message[NEAR * rows_x :, n * LANES : (n + 1) * LANES] = compact[n * ROWS : (n + 1) * ROWS]
    copies[1].wait()
    for d in range(NEAR):
        plane = jnp.where(side == 0, held_source[:, d, :], held_source[:, depth - 1 - d, :])
        message[d * rows_x : (d + 1) * rows_x, :] = plane
    row_edges(odd, held_source, inv, edges)


def row_edges(odd, source, inv, messages):
    rows_x, depth, width = source.shape
    for number, message in enumerate(messages):
        packs = jnp.zeros((depth, LANES), jnp.float32)
        for k in range(HALO):
            last = rows_x - HALO + k
            message[k * depth : (k + 1) * depth, :] = choose(odd, source[k], source[last], number)
            packs = packs + roll(choose(odd, inv[k], inv[last], number), 32 * k, 1)
        for n in range(depth // ROWS):
            message[HALO * depth :, n * LANES : (n + 1) * LANES] = packs[n * ROWS : (n + 1) * ROWS]


def row_layers(message, depth):
    packs = jnp.concatenate(
        [message[HALO * depth :, n * LANES : (n + 1) * LANES] for n in range(depth // ROWS)], axis=0
    )
    planes = [message[k * depth : (k + 1) * depth] for k in range(HALO)]
    return planes, [jnp.where(lane_ids(packs) < 32, roll(packs, -32 * k, 1), 0.0) for k in range(HALO)]


def face_side_kernel(groups, own, other, s_out, i_out, i_own, *messages):
    odd = index("gx") % 2
    if groups == 2:
        first = index("gy") == 0
        parts = [jnp.where(first, own[...], other[...]), jnp.where(first, other[...], own[...])]
    else:
        parts = [other[n] for n in range(groups)]
    width = own.shape[1]
    cells = width // E
    rows_x = i_own.shape[0]

    def inverse(part):
        pieces = [
            part[NEAR * rows_x :, n * LANES : (n + 1) * LANES] for n in range(rows_x // ROWS)
        ]
        compact = jnp.concatenate(pieces, axis=0)
        planes = jnp.concatenate([roll(compact, -32 * d, 1) for d in range(NEAR)], axis=0)
        return spread(planes, width, cells)

    i_own[...] = inverse(own[...])[:rows_x]
    s_all = jnp.concatenate([part[: NEAR * rows_x] for part in parts], axis=1)
    i_all = jnp.concatenate([inverse(part) for part in parts], axis=1)
    for all_planes, out in ((s_all, s_out), (i_all, i_out)):
        for d in range(NEAR):
            out[d] = all_planes[d * rows_x : (d + 1) * rows_x]
    for number, message in enumerate(messages):
        for k, all_planes in enumerate((s_all, i_all)):
            for d in range(2):
                row = 4 * k + 2 * d
                top = d * rows_x
                message[row : row + 2, :] = choose(
                    odd, all_planes[top : top + 2], all_planes[top + rows_x - 2 : top + rows_x], number
                )


def face_trace_kernel(nx, s_in, i_in, order, *refs):
    odd = index("gx") % 2
    got = [r[...] for r in refs[:nx]]
    out, ext_s, ext_i = refs[nx:]
    _, rows_x, width = s_in.shape
    below, above = from_low(odd, got), from_high(odd, got)
    ext_s[...] = jnp.zeros(ext_s.shape, jnp.float32)
    ext_i[...] = jnp.zeros(ext_i.shape, jnp.float32)
    first, last = ROWS, ROWS + rows_x
    for ext, own, k in ((ext_s, s_in, 0), (ext_i, i_in, 1)):
        for d in range(2):
            row = 4 * k + 2 * d
            ext[d, first:last, :width] = own[d]
            ext[d, first - 2 : first, :width] = below[row : row + 2]
            ext[d, last : last + 2, :width] = above[row : row + 2]

    def around(u):
        return roll(u, 1, 0) + roll(u, -1, 0) + roll(u, E, 1) + roll(u, -E, 1)

    s0, i0, i1 = ext_s[0], ext_i[0], ext_i[1]
    u0, u1 = s0 * i0, ext_s[1] * i1
    deep = s_in[2] * i_in[2]
    v0 = (s0 + (around(u0) + u1)) * i0
    own = (around(u1) + u0)[first:last, :width]
    v1 = (s_in[1] + (own + deep)) * i_in[1]
    face = (s_in[0] + (around(v0)[first:last, :width] + v1)) * i_in[0]
    pieces = []
    for cell in range(width // E):
        start = cell * E // LANES * LANES
        pieces.append(roll(face[:, start : start + LANES], -(cell * E - start), 1))
    stacked = jnp.concatenate(pieces, axis=0)
    values = stacked.T[:E].astype(jnp.bfloat16)
    out[0] = jnp.dot(values, order[...], preferred_element_type=jnp.float32).astype(jnp.bfloat16)


def order_kernel(place, near_col, far_col, order, spot):
    rows_x, _, cells_y = place.shape
    at = place[...].reshape(rows_x, cells_y) if rows_x == 1 else place[:, 0, :]
    trace = lax.broadcasted_iota(jnp.int32, (rows_x, order.shape[1]), 1)
    for y in range(cells_y):
        hit = at[:, y : y + 1] == trace
        order[y * rows_x : (y + 1) * rows_x, :] = jnp.where(hit, 1.0, 0.0).astype(jnp.bfloat16)
    at_x, at_z = index("gx"), index("gz")
    size_x = lax.axis_size("gx")
    for k in range(spot.shape[0]):
        block = near_col[0] if k == 0 else far_col[k - 1]
        apart = (block // 2) ^ at_x
        where = ((block % 2) ^ at_z) * size_x
        for n, step in enumerate(doubling(size_x)):
            where = where + jnp.where(apart & step > 0, 1 << n, 0)
        spot[k] = where


def join_kernel(one, two, out):
    count = one.shape[0]
    out[:count] = one[...]
    out[count:] = two[...]


ACROSS = (((1,), (1,)), ((), ()))


def row_order_kernel(order, near, far_u, near_out, far_out):
    size = 2 * LANES

    def step(n, _):
        columns = pl.ds(pl.multiple_of(n * size, size), size)
        rows = jnp.dot(order[...], near[:, columns], preferred_element_type=jnp.float32)
        near_out[:, columns] = rows.astype(jnp.bfloat16)
        return 0

    lax.fori_loop(0, near.shape[1] // size, step, 0)
    rows = lax.dot_general(far_u[...], order[...], ACROSS, preferred_element_type=jnp.float32)
    far_out[...] = rows.astype(jnp.bfloat16)


def operator_kernel(halves, wanted, here, there, near, far_v, far_u, *outs):
    count = wanted.shape[0] - 1
    rank = far_v.shape[0] // count
    across = functools.partial(
        lax.dot_general, dimension_numbers=ACROSS, preferred_element_type=jnp.float32
    )
    size = here.shape[0]

    def traces(k):
        at = wanted[k] % size
        return jnp.where(wanted[k] < size, here[at], there[at])

    rows = across(traces(0), near[...])
    far = jnp.concatenate([traces(1 + k) for k in range(count)], axis=0)
    products = across(far, far_v[...])
    group = lax.broadcasted_iota(jnp.int32, (E, count * rank), 1) // rank
    weights = jnp.zeros((E, count * rank), jnp.float32)
    for k in range(count):
        weights = jnp.where(group == k, products[k * E : (k + 1) * E], weights)
    rows = rows + jnp.dot(
        weights.astype(jnp.bfloat16), far_u[...], preferred_element_type=jnp.float32
    )
    if halves:
        half = rows.shape[1] // 2
        first = index("gy") == 0
        outs[0][...] = jnp.where(first, rows[:, :half], rows[:, half:])
        outs[1][...] = jnp.where(first, rows[:, half:], rows[:, :half])
    else:
        outs[0][...] = rows


def finish_kernel(count, *refs):
    parts = refs[:count]
    inv, slab, _, flux_out, out, held_flux, sems = refs[count:]
    side = index("gz")
    rows_x, _, width = slab.shape
    total = parts[0][...]
    if count == 2:
        total = total + parts[1][...]
    wide = jnp.concatenate([total, jnp.zeros((LANES - E, total.shape[1]), jnp.float32)], axis=0).T
    columns = []
    for start in range(0, width // E, LANES // E):
        column = wide[start * rows_x : (start + 1) * rows_x]
        for k in range(1, LANES // E):
            column = column + roll(wide[(start + k) * rows_x : (start + k + 1) * rows_x], k * E, 1)
        columns.append(column)
    flux = jnp.concatenate(columns, axis=1)
    held_flux[...] = flux[:, None, :]
    out_copy = pltpu.make_async_copy(held_flux, flux_out, sems.at[0])
    out_copy.start()
    added = (flux * inv[...])[:, None, :]
    row = lax.broadcasted_iota(jnp.int32, slab.shape, 1)
    slab[...] = slab[...] + jnp.where(row == side * (ROWS - 1), added, 0.0)
    top = pl.multiple_of(side * (out.shape[1] - ROWS), ROWS)
    copy = pltpu.make_async_copy(slab, out.at[:, pl.ds(top, ROWS), :], sems.at[1])
    copy.start()
    out_copy.wait()
    copy.wait()


def side_edge_kernel(nx, source, inv, *refs):
    odd_x, odd_y = index("gx") % 2, index("gy") % 2
    got_x, messages = [r[...] for r in refs[:nx]], refs[nx:]
    rows_x, depth, width = source.shape
    cells = width // E
    halo = HALO * E

    def put(rows, first, last, c):
        lane = lane_ids(c)
        axis = c.ndim - 1
        low = jnp.where(lane < halo, first, roll(c, halo, axis))
        high = jnp.where(lane < halo, roll(last, halo, axis), roll(c, halo - (cells - HALO), axis))
        for number, message in enumerate(messages):
            message[rows] = choose(odd_y, low, high, number)

    own = slice(HALO - 1, HALO - 1 + rows_x)
    put(own, source[:, :, :LANES], source[:, :, width - LANES :], inv[...])
    for start, skip, edge in (
        (0, 1, from_low(odd_x, got_x)),
        (HALO - 1 + rows_x, 0, from_high(odd_x, got_x)),
    ):
        planes, compacts = row_layers(edge, depth)
        for k in range(HALO - 1):
            s, c = planes[k + skip], compacts[k + skip]
            put(start + k, s[:, :LANES], s[:, width - LANES :], c)


def widen(cells, ring, s, c, left, right):
    lane = lane_ids(right)
    width = HALO * E
    axis = right.ndim - 1
    zero = jnp.zeros_like(right)
    after = jnp.where(lane < width, right, zero)
    before = jnp.where(lane >= LANES - width, roll(left, LANES - width, axis), zero)
    pads = [after + before] if ring - cells == LANES // E else [after, before]
    own = jnp.where(lane < cells, c, zero)
    c_after = jnp.where((lane >= cells) & (lane < cells + HALO), roll(right, cells - width, axis), zero)
    c_before = jnp.where(
        (lane >= ring - HALO) & (lane < ring), roll(left, ring - HALO - width, axis), zero
    )
    return [s, *pads], own + c_after + c_before


def depth_edge_kernel(cells, ring, nx, ny, source, inv, *refs):
    odd_x, odd_y, side = index("gx") % 2, index("gy") % 2, index("gz")
    got_x, got_y, (two_out, one_out) = refs[:nx], refs[nx : nx + ny], refs[nx + ny :]
    rows_x, depth, width = source.shape
    wide = ring * E
    rows = two_out.shape[1]
    packs = jnp.zeros((rows, LANES), jnp.float32)

    def layer(message, z):
        lanes = message[HALO * depth + z % ROWS : HALO * depth + z % ROWS + 1, z // ROWS * LANES :]
        lanes = lanes[:, :LANES]
        lines = []
        for n in range(HALO):
            line = message[n * depth + z : n * depth + z + 1, :]
            compact = jnp.where(lane_ids(lanes) < 32, roll(lanes, -32 * n, 1), 0.0)
            lines.append(jnp.concatenate([line, compact], axis=1))
        return jnp.concatenate(lines, axis=0)

    for k in range(HALO):
        inner = lambda r: jnp.where(side == 0, r[:, depth - HALO + k, :], r[:, k, :])
        edges = [jnp.where(side == 0, layer(r, depth - HALO + k), layer(r, k)) for r in got_x]
        below, above = from_low(odd_x, edges), from_high(odd_x, edges)
        empty = jnp.zeros((rows - rows_x - 2 * HALO + 1, LANES), jnp.float32)
        beside = [jnp.concatenate([empty[:1], inner(r), empty], axis=0) for r in got_y]
        own = jnp.concatenate([inner(source), inner(inv)], axis=1)
        blank = jnp.zeros((rows - rows_x - 2 * HALO, width + LANES), jnp.float32)
        all_rows = jnp.concatenate([below, own, above, blank], axis=0)
        parts, compact = widen(
            cells, ring, all_rows[:, :width], all_rows[:, width:],
            from_low(odd_y, beside), from_high(odd_y, beside),
        )
        compact = jnp.where(lane_ids(compact) < ring, compact, 0.0)
        packs = packs + roll(compact, 32 * k, 1)
        out = jnp.concatenate(parts, axis=1)
        if k < 2:
            two_out[k] = out
        else:
            one_out[:, :wide] = out
    one_out[:, wide:] = packs


def assemble_kernel(cells, ring, nx, ny, source, inv, *refs):
    odd_x, odd_y, side = index("gx") % 2, index("gy") % 2, index("gz")
    got_x, got_y = refs[:nx], refs[nx : nx + ny]
    z_two, z_one, ext_s, ext_i, one, compacts, matrix = refs[nx + ny :]
    rows_x, depth, width = source.shape
    wide = ring * E
    all_z = depth + ROWS
    total = ext_s.shape[0]
    matrix[...] = spread_matrix(ring, wide)
    start = side * (ROWS - HALO)

    def spaced(rows):
        at = lax.broadcasted_iota(jnp.int32, (ROWS, rows[0].shape[1]), 0) - start
        tile = jnp.zeros(at.shape, jnp.float32)
        for k, value in enumerate(rows):
            tile = jnp.where(at == k, value, tile)
        return tile

    def place(x, s, c, got):
        parts, compact = widen(cells, ring, s, c, from_low(odd_y, got), from_high(odd_y, got))
        last = z_one[pl.ds(x, 1), :]
        zone = spaced([z_two[0, pl.ds(x, 1), :], z_two[1, pl.ds(x, 1), :], last[:, :wide]])
        packs = jnp.broadcast_to(last[:, wide:], (ROWS, LANES))
        lanes = spaced([roll(packs, -32 * k, 1) for k in range(HALO)])
        first = pl.ds(pl.multiple_of(x * all_z, ROWS), depth)
        rest = pl.ds(pl.multiple_of(x * all_z + depth, ROWS), ROWS)
        compacts[first, :] = compact
        compacts[rest, :] = lanes
        at = 0
        for part in parts:
            ext_s[first, at : at + part.shape[1]] = part
            at += part.shape[1]
        ext_s[rest, :] = zone

    def own(x, _):
        place(x + HALO, source[x], inv[x], [r[x + HALO - 1] for r in got_y])
        return 0

    repeat(0, rows_x, own, 4)
    got = [r[...] for r in got_x]
    for base, skip, edge in ((0, 0, from_low(odd_x, got)), (rows_x + HALO, 2, from_high(odd_x, got))):
        planes, compact = row_layers(edge, depth)
        for k in range(HALO):
            if k == skip:
                beside = [jnp.zeros((depth, LANES), jnp.float32) for _ in got_y]
            else:
                beside = [r[base + k - 1] for r in got_y]
            place(base + k, planes[k], compact[k], beside)
    chunk = max(n for n in range(2 * ROWS, 321, 2 * ROWS) if total % n == 0)

    def expand(n, _):
        rows = pl.ds(pl.multiple_of(n * chunk, 2 * ROWS), chunk)
        some = packed(compacts[rows, :], ring)
        inverse = jnp.dot(some, matrix[...], preferred_element_type=jnp.float32)
        ext_i[rows, :] = inverse
        one[rows, :] = ext_s[rows, :] * inverse
        return 0

    lax.fori_loop(0, total // chunk, expand, 0)


def repeat(first, last, step, most):
    count = last - first
    unroll = max(n for n in range(1, most + 1) if count % n == 0)
    lax.fori_loop(first, last, step, 0, unroll=unroll)


def swept(ext_s, ext_i, old, x, all_z, depth, width, store):
    at = lambda x, rows: pl.ds(pl.multiple_of(x * all_z, ROWS), rows)
    tiles = old.shape[1] // LANES
    lane = lax.broadcasted_iota(jnp.int32, (depth, LANES), 1)
    known = {}

    def tile(j):
        j %= tiles
        if j not in known:
            u = old[at(x, all_z), j * LANES : (j + 1) * LANES]
            known[j] = (u, roll(u[:depth], E, 1), roll(u[:depth], -E, 1))
        return known[j]

    for j in range(width // LANES):
        columns = slice(j * LANES, (j + 1) * LANES)
        here = tile(j)
        beside = old[at(x - 1, depth), columns] + old[at(x + 1, depth), columns]
        up = roll(here[0], 1, 0) + roll(here[0], -1, 0)
        side = jnp.where(lane < E, tile(j - 1)[1], here[1])
        side = side + jnp.where(lane >= LANES - E, tile(j + 1)[2], here[2])
        beside = beside + (up[:depth] + side)
        new = (ext_s[at(x, depth), columns] + beside) * ext_i[at(x, depth), columns]
        store(columns, new)


def sweep_kernel(all_z, first, last, ext_s, ext_i, old, *refs):
    new = refs[-1]

    def step(x, _):
        def store(columns, value):
            new[pl.ds(pl.multiple_of(x * all_z, ROWS), all_z), columns] = value

        swept(ext_s, ext_i, old, x, all_z, all_z, old.shape[1], store)
        return 0

    repeat(first, last, step, 12)


def last_sweep_kernel(ext_s, ext_i, old, out, slab, done, sems):
    side = index("gz")
    rows_x, depth, width = out.shape
    all_z = depth + ROWS

    def step(x, _):
        def store(columns, value):
            done[x, :, columns] = value
            slab[x, :, columns] = jnp.where(side == 0, value[:ROWS], value[depth - ROWS :])

        swept(ext_s, ext_i, old, x + HALO, all_z, depth, width, store)
        return 0

    pieces = sems.shape[0]
    size = rows_x // pieces
    copies = []
    for n in range(pieces):
        repeat(n * size, (n + 1) * size, step, 8)
        rows = slice(n * size, (n + 1) * size)
        copies.append(pltpu.make_async_copy(done.at[rows], out.at[rows], sems.at[n]))
        copies[-1].start()
    for copy in copies:
        copy.wait()


def body(source, coef, face_trace, near_col, far_col, near_tile, far_u, far_v):
    rows_x, depth, width = source.shape
    cells = coef.shape[2]
    groups = lax.axis_size("gy")
    size_x = lax.axis_size("gx")
    tile = near_tile.shape[3]
    count = far_u.shape[3]
    rank = far_u.shape[4]
    nx, ny = message_count("gx"), message_count("gy")
    bf16 = jnp.bfloat16
    both = [(0, 1), (1, 0)]
    pad = LANES if groups == 2 else 2 * LANES
    ring = (width + pad) // E
    wide = width + pad
    all_x, all_z = rows_x + 2 * HALO, depth + ROWS
    part = rows_x * cells
    halves = groups == 2
    coef = coef.transpose(0, 2, 1)

    held_source, inv, near, *vol_x = call(
        face_start_kernel, (kept(source), kept(coef)),
        [vector(source.shape), vector((rows_x, depth, LANES)), vector((NEAR * rows_x + ROWS, width))]
        + [vector((HALO * depth + ROWS, width))] * nx,
        in_specs=[MAIN, MAIN],
        scratch=(vector(coef.shape), pltpu.SemaphoreType.DMA((2,))),
    )
    if halves:
        other = held(lax.ppermute(near, "gy", both))
    else:
        other = held(lax.all_gather(near, "gy", axis=0, tiled=False))
    got_vol_x = swap(vol_x, "gx")
    full = vector((NEAR, rows_x, width * groups))
    s_face, i_face, i_own, *face_x = call(
        functools.partial(face_side_kernel, groups), (near, other),
        [full, full, vector((rows_x, width))] + [vector((ROWS, width * groups))] * nx, work=500,
    )
    got_x = swap(face_x, "gx")
    order, spot = call(
        order_kernel, (face_trace, near_col.reshape(1), far_col.reshape(count)),
        [vector((tile, tile), bf16), pltpu.SMEM((count + 1,), jnp.int32)],
        in_specs=[VECTOR, SCALAR, SCALAR], out_specs=[VECTOR, SCALAR], work=2000, after=(near,),
    )
    vol_y = call(
        functools.partial(side_edge_kernel, nx), (held_source, inv, *got_vol_x),
        [vector((all_x - 2, depth, LANES))] * ny, work=300, after=(order, *got_x),
    )
    got_vol_y = swap(vol_y, "gy")

    ext = pltpu.VMEM((2, rows_x + 2 * ROWS, width * groups + LANES), jnp.float32)
    (traces,) = call(
        functools.partial(face_trace_kernel, nx), (s_face, i_face, order, *got_x),
        [vector((1, E, tile), bf16)], scratch=(ext, ext),
    )
    steps = doubling(size_x)
    for step in steps:
        other = held(lax.ppermute(traces, "gx", [(i, i ^ step) for i in range(size_x)]))
        twice = (2 * traces.shape[0], E, tile)
        before = ()
        if step == steps[-2]:
            near, far_rows = call(
                row_order_kernel,
                (order, held(near_tile.reshape(tile, tile)), held(far_u.reshape(count * rank, tile))),
                [vector((tile, tile), bf16), vector((count * rank, tile), bf16)], work=3000,
                after=(traces,),
            )
            before = (near,)
        if step == 1:
            rounded = -(-all_x // ROWS) * ROWS
            vol_z = call(
                functools.partial(depth_edge_kernel, cells, ring, nx, ny),
                (held_source, inv, *got_vol_x, *got_vol_y),
                [vector((2, rounded, wide)), vector((rounded, wide + LANES))], work=500,
                after=(traces,),
            )
            got_vol_z = [held(lax.ppermute(v, "gz", both)) for v in vol_z]
            ext = vector((all_x * all_z, wide))
            ext_s, ext_i, one = call(
                functools.partial(assemble_kernel, cells, ring, nx, ny),
                (held_source, inv, *got_vol_x, *got_vol_y, *got_vol_z), [ext, ext, ext], work=3000,
                scratch=(vector((all_x * all_z, LANES)), vector((LANES, wide), bf16)),
            )
            (two,) = call(
                functools.partial(sweep_kernel, all_z, 1, all_x - 1), (ext_s, ext_i, one), [ext],
                work=2500,
            )
            before = (two,)
        (traces,) = call(
            join_kernel, (traces, other), [vector(twice, bf16)], work=300, after=before
        )
    other = held(lax.ppermute(traces, "gz", both))
    count_x = (all_x - 4) // 2
    middle = 2 + count_x - count_x % 4
    (three,) = call(
        functools.partial(sweep_kernel, all_z, 2, middle), (ext_s, ext_i, two), [ext], work=1400,
        after=(traces,),
    )

    rows = call(
        functools.partial(operator_kernel, halves),
        (spot, traces, other, near, held(far_v.reshape(count * rank, tile)), far_rows),
        [vector((E, part))] * 2 if halves else [plain((E, tile))],
        in_specs=[SCALAR] + [VECTOR] * 5, work=2500, after=(three,),
    )
    if halves:
        sums = (rows[0], held(lax.ppermute(rows[1], "gy", both)))
    else:
        sums = (held(lax.psum_scatter(rows[0], "gy", scatter_dimension=1, tiled=True)),)
    (three,) = call(
        functools.partial(sweep_kernel, all_z, middle, all_x - 2), (ext_s, ext_i, two, three), [ext],
        work=1400, input_output_aliases={3: 0}, after=rows,
    )
    pieces = 4
    field, slab = call(
        last_sweep_kernel, (ext_s, ext_i, three),
        [plain(source.shape), vector((rows_x, ROWS, width))], work=2000,
        out_specs=[MAIN, VECTOR],
        scratch=(vector(source.shape), pltpu.SemaphoreType.DMA((pieces,))),
    )

    flux, result = call(
        functools.partial(finish_kernel, len(sums)), (*sums, i_own, slab, field),
        [plain((rows_x, 1, width)), plain(source.shape)],
        in_specs=[VECTOR] * (len(sums) + 2) + [MAIN], out_specs=[MAIN, MAIN],
        scratch=(vector((rows_x, 1, width)), pltpu.SemaphoreType.DMA((2,))),
        input_output_aliases={len(sums) + 2: 1},
    )
    return (result, flux)


def solution(mesh):
    return jax.shard_map(
        body,
        mesh=mesh,
        in_specs=(
            P("gx", "gz", "gy"),
            P("gx", "gz", "gy"),
            P("gx", "gz", None),
            P("gx", "gz", "gy"),
            P("gx", "gz", "gy", None),
            P("gx", "gz", "gy", None, None),
            P("gx", "gz", "gy", None, None, None),
            P("gx", "gz", "gy", None, None, None),
        ),
        out_specs=(P("gx", "gz", "gy"), P("gx", "gz", "gy")),
        check_vma=False,
    )
```

```python
import functools
import math

import jax
import jax.numpy as jnp
from jax import lax
from jax.experimental import pallas as pl
from jax.experimental.pallas import tpu as pltpu
from jax.sharding import PartitionSpec as P

E = 32
LANES = 128
ROWS = 8
HALO = 3
NEAR = 3


def roll(value, shift, axis):
    return pltpu.roll(value, shift % value.shape[axis], axis)


def lane_ids(value):
    return lax.broadcasted_iota(jnp.int32, value.shape, value.ndim - 1)


def held(value):
    return pltpu.with_memory_space_constraint(value, pltpu.VMEM)


def kept(value):
    return pltpu.with_memory_space_constraint(value, pltpu.HBM)


VECTOR = pl.BlockSpec(memory_space=pltpu.VMEM)
SCALAR = pl.BlockSpec(memory_space=pltpu.SMEM)
PLACED = pl.BlockSpec(memory_space=pl.ANY)
MAIN = pl.BlockSpec(memory_space=pltpu.HBM)


def vector(shape, dtype=jnp.float32):
    return pltpu.VMEM(shape, dtype)


def plain(shape, dtype=jnp.float32):
    return jax.ShapeDtypeStruct(shape, dtype)


def size_of(a):
    return math.prod(a.shape) * jnp.dtype(a.dtype).itemsize


def call(kernel, operands, out_shape, in_specs=None, out_specs=None, scratch=(), room=8, work=1000, after=(), **kw):
    given, tokens = len(operands), len(after)

    def body(*refs):
        kernel(*refs[:given], *refs[given + tokens :])

    return pl.pallas_call(
        body,
        out_shape=out_shape,
        in_specs=(in_specs or [VECTOR] * given) + [PLACED] * tokens,
        out_specs=out_specs or [VECTOR] * len(out_shape),
        scratch_shapes=list(scratch),
        compiler_params=pltpu.CompilerParams(vmem_limit_bytes=room * 1024 * 1024),
        cost_estimate=pl.CostEstimate(flops=0, bytes_accessed=work * 3000, transcendentals=0),
        **kw,
    )(*operands, *after)


def index(axis):
    return lax.axis_index(axis).astype(jnp.int32)


def pairs(count):
    first = [(i, i ^ 1) for i in range(count)]
    second = [(i, i + 1) for i in range(1, count - 1, 2)]
    return first, second + [(b, a) for a, b in second]


def swap(messages, axis):
    count = lax.axis_size(axis)
    return [held(lax.ppermute(m, axis, p)) for m, p in zip(messages, pairs(count))]


def doubling(count):
    steps = []
    while count > 1:
        count //= 2
        steps.append(count)
    return steps


def message_count(axis):
    return 1 if lax.axis_size(axis) == 2 else 2


def choose(odd, low, high, number):
    return jnp.where(odd == number, high, low)


def from_low(odd, received):
    other = received[1] if len(received) == 2 else jnp.zeros_like(received[0])
    return jnp.where(odd == 1, received[0], other)


def from_high(odd, received):
    other = received[1] if len(received) == 2 else jnp.zeros_like(received[0])
    return jnp.where(odd == 1, other, received[0])


def spread_matrix(cells, width):
    k = lax.broadcasted_iota(jnp.int32, (LANES, width), 0)
    cell = lax.broadcasted_iota(jnp.int32, (LANES, width), 1) // E
    part = k // 32
    hit = (k - part * 32 == cell) & (part < 3) & (cell < cells)
    return jnp.where(hit, 1.0, 0.0).astype(jnp.bfloat16)


def packed(compact, cells):
    compact = jnp.where(lane_ids(compact) < cells, compact, 0.0)
    high = compact.astype(jnp.bfloat16).astype(jnp.float32)
    rest = compact - high
    middle = rest.astype(jnp.bfloat16).astype(jnp.float32)
    low = (rest - middle).astype(jnp.bfloat16).astype(jnp.float32)
    axis = compact.ndim - 1
    return (high + roll(middle, 32, axis) + roll(low, 64, axis)).astype(jnp.bfloat16)


def spread(compact, width, cells):
    return jnp.dot(
        packed(compact, cells), spread_matrix(cells, width), preferred_element_type=jnp.float32
    )


def face_start_kernel(source, coef, held_source, inv, message, *refs):
    edges, (coefs, sems) = refs[:-2], refs[-2:]
    odd, side = index("gx") % 2, index("gz")
    rows_x, depth, width = source.shape
    cells = width // E
    copies = [
        pltpu.make_async_copy(coef, coefs, sems.at[0]),
        pltpu.make_async_copy(source, held_source, sems.at[1]),
    ]
    for copy in copies:
        copy.start()
    copies[0].wait()
    c = jnp.swapaxes(1.0 / (6.0 + coefs[...]), 1, 2)
    inv[...] = jnp.concatenate(
        [c, jnp.zeros((rows_x, depth, LANES - cells), jnp.float32)], axis=2
    )
    compact = jnp.zeros((rows_x, LANES), jnp.float32)
    for d in range(NEAR):
        plane = jnp.where(side == 0, inv[:, d, :], inv[:, depth - 1 - d, :])
        compact = compact + roll(plane, 32 * d, 1)
    for n in range(rows_x // ROWS):
        message[NEAR * rows_x :, n * LANES : (n + 1) * LANES] = compact[n * ROWS : (n + 1) * ROWS]
    copies[1].wait()
    for d in range(NEAR):
        plane = jnp.where(side == 0, held_source[:, d, :], held_source[:, depth - 1 - d, :])
        message[d * rows_x : (d + 1) * rows_x, :] = plane
    row_edges(odd, held_source, inv, edges)


def row_edges(odd, source, inv, messages):
    rows_x, depth, width = source.shape
    for number, message in enumerate(messages):
        packs = jnp.zeros((depth, LANES), jnp.float32)
        for k in range(HALO):
            last = rows_x - HALO + k
            message[k * depth : (k + 1) * depth, :] = choose(odd, source[k], source[last], number)
            packs = packs + roll(choose(odd, inv[k], inv[last], number), 32 * k, 1)
        for n in range(depth // ROWS):
            message[HALO * depth :, n * LANES : (n + 1) * LANES] = packs[n * ROWS : (n + 1) * ROWS]


def row_layers(message, depth):
    packs = jnp.concatenate(
        [message[HALO * depth :, n * LANES : (n + 1) * LANES] for n in range(depth // ROWS)], axis=0
    )
    planes = [message[k * depth : (k + 1) * depth] for k in range(HALO)]
    return planes, [jnp.where(lane_ids(packs) < 32, roll(packs, -32 * k, 1), 0.0) for k in range(HALO)]


def face_side_kernel(groups, own, other, s_out, i_out, i_own, *messages):
    odd = index("gx") % 2
    if groups == 2:
        first = index("gy") == 0
        parts = [jnp.where(first, own[...], other[...]), jnp.where(first, other[...], own[...])]
    else:
        parts = [other[n] for n in range(groups)]
    width = own.shape[1]
    cells = width // E
    rows_x = i_own.shape[0]

    def inverse(part):
        pieces = [
            part[NEAR * rows_x :, n * LANES : (n + 1) * LANES] for n in range(rows_x // ROWS)
        ]
        compact = jnp.concatenate(pieces, axis=0)
        planes = jnp.concatenate([roll(compact, -32 * d, 1) for d in range(NEAR)], axis=0)
        return spread(planes, width, cells)

    i_own[...] = inverse(own[...])[:rows_x]
    s_all = jnp.concatenate([part[: NEAR * rows_x] for part in parts], axis=1)
    i_all = jnp.concatenate([inverse(part) for part in parts], axis=1)
    for all_planes, out in ((s_all, s_out), (i_all, i_out)):
        for d in range(NEAR):
            out[d] = all_planes[d * rows_x : (d + 1) * rows_x]
    for number, message in enumerate(messages):
        for k, all_planes in enumerate((s_all, i_all)):
            for d in range(2):
                row = 4 * k + 2 * d
                top = d * rows_x
                message[row : row + 2, :] = choose(
                    odd, all_planes[top : top + 2], all_planes[top + rows_x - 2 : top + rows_x], number
                )


def face_trace_kernel(nx, s_in, i_in, order, *refs):
    odd = index("gx") % 2
    got = [r[:ROWS] for r in refs[:nx]]
    out, ext_s, ext_i = refs[nx:]
    _, rows_x, width = s_in.shape
    below, above = from_low(odd, got), from_high(odd, got)
    ext_s[...] = jnp.zeros(ext_s.shape, jnp.float32)
    ext_i[...] = jnp.zeros(ext_i.shape, jnp.float32)
    first, last = ROWS, ROWS + rows_x
    for ext, own, k in ((ext_s, s_in, 0), (ext_i, i_in, 1)):
        for d in range(2):
            row = 4 * k + 2 * d
            ext[d, first:last, :width] = own[d]
            ext[d, first - 2 : first, :width] = below[row : row + 2]
            ext[d, last : last + 2, :width] = above[row : row + 2]

    def around(u):
        return roll(u, 1, 0) + roll(u, -1, 0) + roll(u, E, 1) + roll(u, -E, 1)

    s0, i0, i1 = ext_s[0], ext_i[0], ext_i[1]
    u0, u1 = s0 * i0, ext_s[1] * i1
    deep = s_in[2] * i_in[2]
    v0 = (s0 + (around(u0) + u1)) * i0
    own = (around(u1) + u0)[first:last, :width]
    v1 = (s_in[1] + (own + deep)) * i_in[1]
    face = (s_in[0] + (around(v0)[first:last, :width] + v1)) * i_in[0]
    pieces = []
    for cell in range(width // E):
        start = cell * E // LANES * LANES
        pieces.append(roll(face[:, start : start + LANES], -(cell * E - start), 1))
    stacked = jnp.concatenate(pieces, axis=0)
    values = stacked.T[:E].astype(jnp.bfloat16)
    out[0] = jnp.dot(values, order[...], preferred_element_type=jnp.float32).astype(jnp.bfloat16)


def order_kernel(place, order):
    rows_x, _, cells_y = place.shape
    at = place[:, 0, :]
    trace = lax.broadcasted_iota(jnp.int32, (rows_x, order.shape[1]), 1)
    for y in range(cells_y):
        hit = at[:, y : y + 1] == trace
        order[y * rows_x : (y + 1) * rows_x, :] = jnp.where(hit, 1.0, 0.0).astype(jnp.bfloat16)


def spot_kernel(near_col, far_col, spot):
    at_x, at_z = index("gx"), index("gz")
    size_x = lax.axis_size("gx")
    for k in range(spot.shape[0]):
        block = near_col[0, 0, 0] if k == 0 else far_col[0, 0, 0, k - 1]
        apart = (block // 2) ^ at_x
        where = ((block % 2) ^ at_z) * size_x
        for n, step in enumerate(doubling(size_x)):
            where = where + jnp.where(apart & step > 0, 1 << n, 0)
        spot[k] = where


def join_kernel(one, two, out):
    count = one.shape[0]
    out[:count] = one[...]
    out[count:] = two[...]


ACROSS = (((1,), (1,)), ((), ()))


def row_order_kernel(order, near, far_u, near_out, far_out):
    size = 2 * LANES

    def step(n, _):
        columns = pl.ds(pl.multiple_of(n * size, size), size)
        rows = jnp.dot(order[...], near[:, columns], preferred_element_type=jnp.float32)
        near_out[:, columns] = rows.astype(jnp.bfloat16)
        return 0

    repeat(0, near.shape[1] // size, step, 4)
    rows = lax.dot_general(far_u[...], order[...], ACROSS, preferred_element_type=jnp.float32)
    far_out[...] = rows.astype(jnp.bfloat16)


def operator_kernel(halves, wanted, here, there, near, far_v, far_u, *outs):
    count = wanted.shape[0] - 1
    rank = far_v.shape[0] // count
    across = functools.partial(
        lax.dot_general, dimension_numbers=ACROSS, preferred_element_type=jnp.float32
    )
    size = here.shape[0]

    def traces(k):
        at = wanted[k] % size
        return jnp.where(wanted[k] < size, here[at], there[at])

    rows = across(traces(0), near[...])
    far = jnp.concatenate([traces(1 + k) for k in range(count)], axis=0)
    products = across(far, far_v[...])
    group = lax.broadcasted_iota(jnp.int32, (E, count * rank), 1) // rank
    weights = jnp.zeros((E, count * rank), jnp.float32)
    for k in range(count):
        weights = jnp.where(group == k, products[k * E : (k + 1) * E], weights)
    rows = rows + jnp.dot(
        weights.astype(jnp.bfloat16), far_u[...], preferred_element_type=jnp.float32
    )
    if halves:
        half = rows.shape[1] // 2
        first = index("gy") == 0
        outs[0][...] = jnp.where(first, rows[:, :half], rows[:, half:])
        outs[1][...] = jnp.where(first, rows[:, half:], rows[:, :half])
    else:
        outs[0][...] = rows


def finish_kernel(count, *refs):
    parts = refs[:count]
    inv, slab, tail, _, flux_out, out, held_flux, sems = refs[count:]
    side = index("gz")
    rows_x, _, width = slab.shape
    size, depth, _ = tail.shape
    columns = off_face(side, depth)
    tail_copy = pltpu.make_async_copy(
        tail.at[:, columns, :], out.at[rows_x - size :, columns, :], sems.at[2]
    )
    tail_copy.start()
    total = parts[0][...]
    if count == 2:
        total = total + parts[1][...]
    wide = jnp.concatenate([total, jnp.zeros((LANES - E, total.shape[1]), jnp.float32)], axis=0).T
    columns = []
    for start in range(0, width // E, LANES // E):
        column = wide[start * rows_x : (start + 1) * rows_x]
        for k in range(1, LANES // E):
            column = column + roll(wide[(start + k) * rows_x : (start + k + 1) * rows_x], k * E, 1)
        columns.append(column)
    flux = jnp.concatenate(columns, axis=1)
    held_flux[...] = flux[:, None, :]
    out_copy = pltpu.make_async_copy(held_flux, flux_out, sems.at[0])
    out_copy.start()
    added = (flux * inv[...])[:, None, :]
    row = lax.broadcasted_iota(jnp.int32, slab.shape, 1)
    slab[...] = slab[...] + jnp.where(row == side * (ROWS - 1), added, 0.0)
    top = pl.multiple_of(side * (out.shape[1] - ROWS), ROWS)
    copy = pltpu.make_async_copy(slab, out.at[:, pl.ds(top, ROWS), :], sems.at[1])
    copy.start()
    tail_copy.wait()
    out_copy.wait()
    copy.wait()


def side_edge_kernel(nx, source, inv, *refs):
    odd_x, odd_y = index("gx") % 2, index("gy") % 2
    got_x, messages = [r[...] for r in refs[:nx]], refs[nx:]
    rows_x, depth, width = source.shape
    cells = width // E
    halo = HALO * E

    def put(rows, first, last, c):
        lane = lane_ids(c)
        axis = c.ndim - 1
        low = jnp.where(lane < halo, first, roll(c, halo, axis))
        high = jnp.where(lane < halo, roll(last, halo, axis), roll(c, halo - (cells - HALO), axis))
        for number, message in enumerate(messages):
            message[rows] = choose(odd_y, low, high, number)

    own = slice(HALO - 1, HALO - 1 + rows_x)
    put(own, source[:, :, :LANES], source[:, :, width - LANES :], inv[...])
    for start, skip, edge in (
        (0, 1, from_low(odd_x, got_x)),
        (HALO - 1 + rows_x, 0, from_high(odd_x, got_x)),
    ):
        planes, compacts = row_layers(edge, depth)
        for k in range(HALO - 1):
            s, c = planes[k + skip], compacts[k + skip]
            put(start + k, s[:, :LANES], s[:, width - LANES :], c)


def widen(cells, ring, s, c, left, right):
    lane = lane_ids(right)
    width = HALO * E
    axis = right.ndim - 1
    zero = jnp.zeros_like(right)
    after = jnp.where(lane < width, right, zero)
    before = jnp.where(lane >= LANES - width, roll(left, LANES - width, axis), zero)
    pads = [after + before] if ring - cells == LANES // E else [after, before]
    own = jnp.where(lane < cells, c, zero)
    c_after = jnp.where((lane >= cells) & (lane < cells + HALO), roll(right, cells - width, axis), zero)
    c_before = jnp.where(
        (lane >= ring - HALO) & (lane < ring), roll(left, ring - HALO - width, axis), zero
    )
    return [s, *pads], own + c_after + c_before


def depth_edge_kernel(cells, ring, nx, ny, source, inv, *refs):
    odd_x, odd_y, side = index("gx") % 2, index("gy") % 2, index("gz")
    got_x, got_y, (two_out, one_out) = refs[:nx], refs[nx : nx + ny], refs[nx + ny :]
    rows_x, depth, width = source.shape
    wide = ring * E
    rows = two_out.shape[1]
    packs = jnp.zeros((rows, LANES), jnp.float32)

    def layer(message, z):
        lanes = message[HALO * depth + z % ROWS : HALO * depth + z % ROWS + 1, z // ROWS * LANES :]
        lanes = lanes[:, :LANES]
        lines = []
        for n in range(HALO):
            line = message[n * depth + z : n * depth + z + 1, :]
            compact = jnp.where(lane_ids(lanes) < 32, roll(lanes, -32 * n, 1), 0.0)
            lines.append(jnp.concatenate([line, compact], axis=1))
        return jnp.concatenate(lines, axis=0)

    for k in range(HALO):
        inner = lambda r: jnp.where(side == 0, r[:, depth - HALO + k, :], r[:, k, :])
        edges = [jnp.where(side == 0, layer(r, depth - HALO + k), layer(r, k)) for r in got_x]
        below, above = from_low(odd_x, edges), from_high(odd_x, edges)
        empty = jnp.zeros((rows - rows_x - 2 * HALO + 1, LANES), jnp.float32)
        beside = [jnp.concatenate([empty[:1], inner(r), empty], axis=0) for r in got_y]
        own = jnp.concatenate([inner(source), inner(inv)], axis=1)
        blank = jnp.zeros((rows - rows_x - 2 * HALO, width + LANES), jnp.float32)
        all_rows = jnp.concatenate([below, own, above, blank], axis=0)
        parts, compact = widen(
            cells, ring, all_rows[:, :width], all_rows[:, width:],
            from_low(odd_y, beside), from_high(odd_y, beside),
        )
        compact = jnp.where(lane_ids(compact) < ring, compact, 0.0)
        packs = packs + roll(compact, 32 * k, 1)
        out = jnp.concatenate(parts, axis=1)
        if k < 2:
            two_out[k] = out
        else:
            one_out[:, :wide] = out
    one_out[:, wide:] = packs


def assemble_kernel(cells, ring, nx, ny, source, inv, *refs):
    odd_x, odd_y, side = index("gx") % 2, index("gy") % 2, index("gz")
    got_x, got_y = refs[:nx], refs[nx : nx + ny]
    z_two, z_one, ext_s, ext_i, one, compacts, matrix = refs[nx + ny :]
    rows_x, depth, width = source.shape
    wide = ring * E
    all_z = depth + ROWS
    total = ext_s.shape[0]
    matrix[...] = spread_matrix(ring, wide)
    start = side * (ROWS - HALO)

    def spaced(rows):
        at = lax.broadcasted_iota(jnp.int32, (ROWS, rows[0].shape[1]), 0) - start
        tile = jnp.zeros(at.shape, jnp.float32)
        for k, value in enumerate(rows):
            tile = jnp.where(at == k, value, tile)
        return tile

    def place(x, s, c, got):
        parts, compact = widen(cells, ring, s, c, from_low(odd_y, got), from_high(odd_y, got))
        last = z_one[pl.ds(x, 1), :]
        zone = spaced([z_two[0, pl.ds(x, 1), :], z_two[1, pl.ds(x, 1), :], last[:, :wide]])
        packs = jnp.broadcast_to(last[:, wide:], (ROWS, LANES))
        lanes = spaced([roll(packs, -32 * k, 1) for k in range(HALO)])
        first = pl.ds(pl.multiple_of(x * all_z, ROWS), depth)
        rest = pl.ds(pl.multiple_of(x * all_z + depth, ROWS), ROWS)
        compacts[first, :] = compact
        compacts[rest, :] = lanes
        at = 0
        for part in parts:
            ext_s[first, at : at + part.shape[1]] = part
            at += part.shape[1]
        ext_s[rest, :] = zone

    def own(x, _):
        place(x + HALO, source[x], inv[x], [r[x + HALO - 1] for r in got_y])
        return 0

    repeat(0, rows_x, own, 16)
    got = [r[...] for r in got_x]
    for base, skip, edge in ((0, 0, from_low(odd_x, got)), (rows_x + HALO, 2, from_high(odd_x, got))):
        planes, compact = row_layers(edge, depth)
        for k in range(HALO):
            if k == skip:
                beside = [jnp.zeros((depth, LANES), jnp.float32) for _ in got_y]
            else:
                beside = [r[base + k - 1] for r in got_y]
            place(base + k, planes[k], compact[k], beside)
    chunk = max(n for n in range(2 * ROWS, 321, 2 * ROWS) if total % n == 0)

    def expand(n, _):
        rows = pl.ds(pl.multiple_of(n * chunk, 2 * ROWS), chunk)
        some = packed(compacts[rows, :], ring)
        inverse = jnp.dot(some, matrix[...], preferred_element_type=jnp.float32)
        ext_i[rows, :] = inverse
        one[rows, :] = ext_s[rows, :] * inverse
        return 0

    repeat(0, total // chunk, expand, 5)


def repeat(first, last, step, most):
    count = last - first
    unroll = max(n for n in range(1, most + 1) if count % n == 0)
    lax.fori_loop(first, last, step, 0, unroll=unroll)


def swept(ext_s, ext_i, old, x, all_z, depth, width, store):
    at = lambda x, rows: pl.ds(pl.multiple_of(x * all_z, ROWS), rows)
    tiles = old.shape[1] // LANES
    lane = lax.broadcasted_iota(jnp.int32, (depth, LANES), 1)
    known = {}

    def tile(j):
        j %= tiles
        if j not in known:
            u = old[at(x, all_z), j * LANES : (j + 1) * LANES]
            known[j] = (u, roll(u[:depth], E, 1), roll(u[:depth], -E, 1))
        return known[j]

    for j in range(width // LANES):
        columns = slice(j * LANES, (j + 1) * LANES)
        here = tile(j)
        beside = old[at(x - 1, depth), columns] + old[at(x + 1, depth), columns]
        up = roll(here[0], 1, 0) + roll(here[0], -1, 0)
        side = jnp.where(lane < E, tile(j - 1)[1], here[1])
        side = side + jnp.where(lane >= LANES - E, tile(j + 1)[2], here[2])
        beside = beside + (up[:depth] + side)
        new = (ext_s[at(x, depth), columns] + beside) * ext_i[at(x, depth), columns]
        store(columns, new)


def sweep_kernel(all_z, first, last, ext_s, ext_i, old, *refs):
    new = refs[-1]

    def step(x, _):
        def store(columns, value):
            new[pl.ds(pl.multiple_of(x * all_z, ROWS), all_z), columns] = value

        swept(ext_s, ext_i, old, x, all_z, all_z, old.shape[1], store)
        return 0

    repeat(first, last, step, 12)


def off_face(side, depth):
    return pl.ds(pl.multiple_of((1 - side) * ROWS, ROWS), depth - ROWS)


def last_sweep_kernel(pieces, ext_s, ext_i, old, out, slab, tail, done, sems):
    side = index("gz")
    rows_x, depth, width = out.shape
    all_z = depth + ROWS
    size = rows_x // pieces
    copies = []
    for n in range(pieces):
        target, shift = (tail, n * size) if n == pieces - 1 else (done, 0)

        def step(x, _, target=target, shift=shift):
            def store(columns, value):
                target[x - shift, :, columns] = value
                slab[x, :, columns] = jnp.where(side == 0, value[:ROWS], value[depth - ROWS :])

            swept(ext_s, ext_i, old, x + HALO, all_z, depth, width, store)
            return 0

        repeat(n * size, (n + 1) * size, step, 8)
        if n < pieces - 1:
            rows, columns = slice(n * size, (n + 1) * size), off_face(side, depth)
            copies.append(
                pltpu.make_async_copy(done.at[rows, columns, :], out.at[rows, columns, :], sems.at[n])
            )
            copies[-1].start()
    for copy in copies:
        copy.wait()


def body(source, coef, face_trace, near_col, far_col, near_tile, far_u, far_v):
    rows_x, depth, width = source.shape
    cells = coef.shape[2]
    groups = lax.axis_size("gy")
    size_x = lax.axis_size("gx")
    tile = near_tile.shape[3]
    count = far_u.shape[3]
    rank = far_u.shape[4]
    nx, ny = message_count("gx"), message_count("gy")
    bf16 = jnp.bfloat16
    both = [(0, 1), (1, 0)]
    pad = LANES if groups == 2 else 2 * LANES
    ring = (width + pad) // E
    wide = width + pad
    all_x, all_z = rows_x + 2 * HALO, depth + ROWS
    part = rows_x * cells
    halves = groups == 2
    coef = coef.transpose(0, 2, 1)

    held_source, inv, near, *vol_x = call(
        face_start_kernel, (kept(source), kept(coef)),
        [vector(source.shape), vector((rows_x, depth, LANES)), vector((NEAR * rows_x + ROWS, width))]
        + [vector((HALO * depth + ROWS, width))] * nx,
        in_specs=[MAIN, MAIN],
        scratch=(vector(coef.shape), pltpu.SemaphoreType.DMA((2,))),
    )
    if halves:
        other = held(lax.ppermute(near, "gy", both))
    else:
        other = held(lax.all_gather(near, "gy", axis=0, tiled=False))
    got_vol_x = swap(vol_x, "gx")
    full = vector((NEAR, rows_x, width * groups))
    s_face, i_face, i_own, *face_x = call(
        functools.partial(face_side_kernel, groups), (near, other),
        [full, full, vector((rows_x, width))]
        + [vector(((1 + n) * ROWS, width * groups)) for n in range(nx)], work=500,
    )
    got_x = swap(face_x, "gx")
    (order,) = call(order_kernel, (face_trace,), [vector((tile, tile), bf16)], after=(near,))
    vol_y = call(
        functools.partial(side_edge_kernel, nx), (held_source, inv, *got_vol_x),
        [vector((all_x - 2, depth, LANES))] * ny, work=300, after=(order, *got_x),
    )
    got_vol_y = swap(vol_y, "gy")

    ext = pltpu.VMEM((2, rows_x + 2 * ROWS, width * groups + LANES), jnp.float32)
    (traces,) = call(
        functools.partial(face_trace_kernel, nx), (s_face, i_face, order, *got_x),
        [vector((1, E, tile), bf16)], scratch=(ext, ext),
    )
    steps = doubling(size_x)
    for step in steps:
        other = held(lax.ppermute(traces, "gx", [(i, i ^ step) for i in range(size_x)]))
        twice = (2 * traces.shape[0], E, tile)
        before = ()
        if step == steps[0]:
            (spot,) = call(
                spot_kernel, (near_col, far_col), [pltpu.SMEM((count + 1,), jnp.int32)],
                in_specs=[SCALAR, SCALAR], out_specs=[SCALAR], after=(traces,),
            )
            before = (spot,)
        if step == steps[-2]:
            near, far_rows = call(
                row_order_kernel,
                (order, held(near_tile.reshape(tile, tile)), held(far_u.reshape(count * rank, tile))),
                [vector((tile, tile), bf16), vector((count * rank, tile), bf16)], work=3000,
                after=(traces,),
            )
            before = (*before, near)
        if step == 1:
            rounded = -(-all_x // ROWS) * ROWS
            vol_z = call(
                functools.partial(depth_edge_kernel, cells, ring, nx, ny),
                (held_source, inv, *got_vol_x, *got_vol_y),
                [vector((2, rounded, wide)), vector((rounded, wide + LANES))], work=500,
                after=(traces,),
            )
            got_vol_z = [held(lax.ppermute(v, "gz", both)) for v in vol_z]
            ext = vector((all_x * all_z, wide))
            ext_s, ext_i, one = call(
                functools.partial(assemble_kernel, cells, ring, nx, ny),
                (held_source, inv, *got_vol_x, *got_vol_y, *got_vol_z), [ext, ext, ext], work=3000,
                scratch=(vector((all_x * all_z, LANES)), vector((LANES, wide), bf16)),
            )
            (two,) = call(
                functools.partial(sweep_kernel, all_z, 1, all_x - 1), (ext_s, ext_i, one), [ext],
                work=2500,
            )
            before = (two,)
        (traces,) = call(
            join_kernel, (traces, other), [vector(twice, bf16)], work=300, after=before
        )
    other = held(lax.ppermute(traces, "gz", both))
    count_x = (all_x - 4) // 2
    middle = 2 + count_x - count_x % 4
    (three,) = call(
        functools.partial(sweep_kernel, all_z, 2, middle), (ext_s, ext_i, two), [ext], work=1400,
        after=(traces,),
    )

    rows = call(
        functools.partial(operator_kernel, halves),
        (spot, traces, other, near, held(far_v.reshape(count * rank, tile)), far_rows),
        [vector((E, part))] * 2 if halves else [plain((E, tile))],
        in_specs=[SCALAR] + [VECTOR] * 5, work=2500, after=(three,),
    )
    if halves:
        sums = (rows[0], held(lax.ppermute(rows[1], "gy", both)))
    else:
        sums = (held(lax.psum_scatter(rows[0], "gy", scatter_dimension=1, tiled=True)),)
    (three,) = call(
        functools.partial(sweep_kernel, all_z, middle, all_x - 2), (ext_s, ext_i, two, three), [ext],
        work=1400, input_output_aliases={3: 0}, after=rows,
    )
    pieces = 4
    size = rows_x // pieces
    field, slab, tail = call(
        functools.partial(last_sweep_kernel, pieces), (ext_s, ext_i, three),
        [plain(source.shape), vector((rows_x, ROWS, width)), vector((size, depth, width))],
        out_specs=[MAIN, VECTOR, VECTOR], work=2000,
        scratch=(vector((rows_x - size, depth, width)), pltpu.SemaphoreType.DMA((pieces - 1,))),
    )

    flux, result = call(
        functools.partial(finish_kernel, len(sums)), (*sums, i_own, slab, tail, field),
        [plain((rows_x, 1, width)), plain(source.shape)],
        in_specs=[VECTOR] * (len(sums) + 3) + [MAIN], out_specs=[MAIN, MAIN],
        scratch=(vector((rows_x, 1, width)), pltpu.SemaphoreType.DMA((3,))),
        input_output_aliases={len(sums) + 3: 1},
    )
    return (result, flux)


def solution(mesh):
    return jax.shard_map(
        body,
        mesh=mesh,
        in_specs=(
            P("gx", "gz", "gy"),
            P("gx", "gz", "gy"),
            P("gx", "gz", None),
            P("gx", "gz", "gy"),
            P("gx", "gz", "gy", None),
            P("gx", "gz", "gy", None, None),
            P("gx", "gz", "gy", None, None, None),
            P("gx", "gz", "gy", None, None, None),
        ),
        out_specs=(P("gx", "gz", "gy"), P("gx", "gz", "gy")),
        check_vma=False,
    )
```

```python
import functools
import math

import jax
import jax.numpy as jnp
from jax import lax
from jax.experimental import pallas as pl
from jax.experimental.pallas import tpu as pltpu
from jax.sharding import PartitionSpec as P

E = 32
LANES = 128
ROWS = 8
HALO = 3
NEAR = 3


def roll(value, shift, axis):
    return pltpu.roll(value, shift % value.shape[axis], axis)


def lane_ids(value):
    return lax.broadcasted_iota(jnp.int32, value.shape, value.ndim - 1)


def held(value):
    return pltpu.with_memory_space_constraint(value, pltpu.VMEM)


def kept(value):
    return pltpu.with_memory_space_constraint(value, pltpu.HBM)


VECTOR = pl.BlockSpec(memory_space=pltpu.VMEM)
SCALAR = pl.BlockSpec(memory_space=pltpu.SMEM)
PLACED = pl.BlockSpec(memory_space=pl.ANY)
MAIN = pl.BlockSpec(memory_space=pltpu.HBM)


def vector(shape, dtype=jnp.float32):
    return pltpu.VMEM(shape, dtype)


def plain(shape, dtype=jnp.float32):
    return jax.ShapeDtypeStruct(shape, dtype)


def size_of(a):
    return math.prod(a.shape) * jnp.dtype(a.dtype).itemsize


def call(kernel, operands, out_shape, in_specs=None, out_specs=None, scratch=(), room=8, work=1000, after=(), **kw):
    given, tokens = len(operands), len(after)

    def body(*refs):
        kernel(*refs[:given], *refs[given + tokens :])

    return pl.pallas_call(
        body,
        out_shape=out_shape,
        in_specs=(in_specs or [VECTOR] * given) + [PLACED] * tokens,
        out_specs=out_specs or [VECTOR] * len(out_shape),
        scratch_shapes=list(scratch),
        compiler_params=pltpu.CompilerParams(vmem_limit_bytes=room * 1024 * 1024),
        cost_estimate=pl.CostEstimate(flops=0, bytes_accessed=work * 3000, transcendentals=0),
        **kw,
    )(*operands, *after)


def index(axis):
    return lax.axis_index(axis).astype(jnp.int32)


def pairs(count):
    first = [(i, i ^ 1) for i in range(count)]
    second = [(i, i + 1) for i in range(1, count - 1, 2)]
    return first, second + [(b, a) for a, b in second]


def swap(messages, axis):
    count = lax.axis_size(axis)
    return [held(lax.ppermute(m, axis, p)) for m, p in zip(messages, pairs(count))]


def doubling(count):
    steps = []
    while count > 1:
        count //= 2
        steps.append(count)
    return steps


def message_count(axis):
    return 1 if lax.axis_size(axis) == 2 else 2


def choose(odd, low, high, number):
    return jnp.where(odd == number, high, low)


def from_low(odd, received):
    other = received[1] if len(received) == 2 else jnp.zeros_like(received[0])
    return jnp.where(odd == 1, received[0], other)


def from_high(odd, received):
    other = received[1] if len(received) == 2 else jnp.zeros_like(received[0])
    return jnp.where(odd == 1, other, received[0])


def spread_matrix(cells, width):
    k = lax.broadcasted_iota(jnp.int32, (LANES, width), 0)
    cell = lax.broadcasted_iota(jnp.int32, (LANES, width), 1) // E
    part = k // 32
    hit = (k - part * 32 == cell) & (part < 3) & (cell < cells)
    return jnp.where(hit, 1.0, 0.0).astype(jnp.bfloat16)


def packed(compact, cells):
    compact = jnp.where(lane_ids(compact) < cells, compact, 0.0)
    high = compact.astype(jnp.bfloat16).astype(jnp.float32)
    rest = compact - high
    middle = rest.astype(jnp.bfloat16).astype(jnp.float32)
    low = (rest - middle).astype(jnp.bfloat16).astype(jnp.float32)
    axis = compact.ndim - 1
    return (high + roll(middle, 32, axis) + roll(low, 64, axis)).astype(jnp.bfloat16)


def spread(compact, width, cells):
    return jnp.dot(
        packed(compact, cells), spread_matrix(cells, width), preferred_element_type=jnp.float32
    )


def face_start_kernel(source, coef, held_source, inv, message, *refs):
    edges, (coefs, sems) = refs[:-2], refs[-2:]
    odd, side = index("gx") % 2, index("gz")
    rows_x, depth, width = source.shape
    cells = width // E
    copies = [
        pltpu.make_async_copy(coef, coefs, sems.at[0]),
        pltpu.make_async_copy(source, held_source, sems.at[1]),
    ]
    for copy in copies:
        copy.start()
    copies[0].wait()
    c = jnp.swapaxes(1.0 / (6.0 + coefs[...]), 1, 2)
    inv[...] = jnp.concatenate(
        [c, jnp.zeros((rows_x, depth, LANES - cells), jnp.float32)], axis=2
    )
    compact = jnp.zeros((rows_x, LANES), jnp.float32)
    for d in range(NEAR):
        plane = jnp.where(side == 0, inv[:, d, :], inv[:, depth - 1 - d, :])
        compact = compact + roll(plane, 32 * d, 1)
    for n in range(rows_x // ROWS):
        message[NEAR * rows_x :, n * LANES : (n + 1) * LANES] = compact[n * ROWS : (n + 1) * ROWS]
    copies[1].wait()
    for d in range(NEAR):
        plane = jnp.where(side == 0, held_source[:, d, :], held_source[:, depth - 1 - d, :])
        message[d * rows_x : (d + 1) * rows_x, :] = plane
    row_edges(odd, held_source, inv, edges)


def row_edges(odd, source, inv, messages):
    rows_x, depth, width = source.shape
    for number, message in enumerate(messages):
        packs = jnp.zeros((depth, LANES), jnp.float32)
        for k in range(HALO):
            last = rows_x - HALO + k
            message[k * depth : (k + 1) * depth, :] = choose(odd, source[k], source[last], number)
            packs = packs + roll(choose(odd, inv[k], inv[last], number), 32 * k, 1)
        for n in range(depth // ROWS):
            message[HALO * depth :, n * LANES : (n + 1) * LANES] = packs[n * ROWS : (n + 1) * ROWS]


def row_layers(message, depth):
    packs = jnp.concatenate(
        [message[HALO * depth :, n * LANES : (n + 1) * LANES] for n in range(depth // ROWS)], axis=0
    )
    planes = [message[k * depth : (k + 1) * depth] for k in range(HALO)]
    return planes, [jnp.where(lane_ids(packs) < 32, roll(packs, -32 * k, 1), 0.0) for k in range(HALO)]


def face_side_kernel(groups, own, other, s_out, i_out, i_own, *messages):
    odd = index("gx") % 2
    if groups == 2:
        first = index("gy") == 0
        parts = [jnp.where(first, own[...], other[...]), jnp.where(first, other[...], own[...])]
    else:
        parts = [other[n] for n in range(groups)]
    width = own.shape[1]
    cells = width // E
    rows_x = i_own.shape[0]

    def inverse(part):
        pieces = [
            part[NEAR * rows_x :, n * LANES : (n + 1) * LANES] for n in range(rows_x // ROWS)
        ]
        compact = jnp.concatenate(pieces, axis=0)
        planes = jnp.concatenate([roll(compact, -32 * d, 1) for d in range(NEAR)], axis=0)
        return spread(planes, width, cells)

    i_own[...] = inverse(own[...])[:rows_x]
    s_all = jnp.concatenate([part[: NEAR * rows_x] for part in parts], axis=1)
    i_all = jnp.concatenate([inverse(part) for part in parts], axis=1)
    for all_planes, out in ((s_all, s_out), (i_all, i_out)):
        for d in range(NEAR):
            out[d] = all_planes[d * rows_x : (d + 1) * rows_x]
    for number, message in enumerate(messages):
        for k, all_planes in enumerate((s_all, i_all)):
            for d in range(2):
                row = 4 * k + 2 * d
                top = d * rows_x
                message[row : row + 2, :] = choose(
                    odd, all_planes[top : top + 2], all_planes[top + rows_x - 2 : top + rows_x], number
                )


def face_trace_kernel(nx, s_in, i_in, order, *refs):
    odd = index("gx") % 2
    got = [r[:ROWS] for r in refs[:nx]]
    out, ext_s, ext_i = refs[nx:]
    _, rows_x, width = s_in.shape
    below, above = from_low(odd, got), from_high(odd, got)
    ext_s[...] = jnp.zeros(ext_s.shape, jnp.float32)
    ext_i[...] = jnp.zeros(ext_i.shape, jnp.float32)
    first, last = ROWS, ROWS + rows_x
    for ext, own, k in ((ext_s, s_in, 0), (ext_i, i_in, 1)):
        for d in range(2):
            row = 4 * k + 2 * d
            ext[d, first:last, :width] = own[d]
            ext[d, first - 2 : first, :width] = below[row : row + 2]
            ext[d, last : last + 2, :width] = above[row : row + 2]

    def around(u):
        return roll(u, 1, 0) + roll(u, -1, 0) + roll(u, E, 1) + roll(u, -E, 1)

    s0, i0, i1 = ext_s[0], ext_i[0], ext_i[1]
    u0, u1 = s0 * i0, ext_s[1] * i1
    deep = s_in[2] * i_in[2]
    v0 = (s0 + (around(u0) + u1)) * i0
    own = (around(u1) + u0)[first:last, :width]
    v1 = (s_in[1] + (own + deep)) * i_in[1]
    face = (s_in[0] + (around(v0)[first:last, :width] + v1)) * i_in[0]
    pieces = []
    for cell in range(width // E):
        start = cell * E // LANES * LANES
        pieces.append(roll(face[:, start : start + LANES], -(cell * E - start), 1))
    stacked = jnp.concatenate(pieces, axis=0)
    values = stacked.T[:E].astype(jnp.bfloat16)
    out[0] = jnp.dot(values, order[...], preferred_element_type=jnp.float32).astype(jnp.bfloat16)


def order_kernel(place, order):
    rows_x, _, cells_y = place.shape
    at = place[:, 0, :]
    trace = lax.broadcasted_iota(jnp.int32, (rows_x, order.shape[1]), 1)
    for y in range(cells_y):
        hit = at[:, y : y + 1] == trace
        order[y * rows_x : (y + 1) * rows_x, :] = jnp.where(hit, 1.0, 0.0).astype(jnp.bfloat16)


def spot_kernel(near_col, far_col, spot):
    at_x, at_z = index("gx"), index("gz")
    size_x = lax.axis_size("gx")
    for k in range(spot.shape[0]):
        block = near_col[0, 0, 0] if k == 0 else far_col[0, 0, 0, k - 1]
        apart = (block // 2) ^ at_x
        where = ((block % 2) ^ at_z) * size_x
        for n, step in enumerate(doubling(size_x)):
            where = where + jnp.where(apart & step > 0, 1 << n, 0)
        spot[k] = where


def join_kernel(one, two, out):
    count = one.shape[0]
    out[:count] = one[...]
    out[count:] = two[...]


ACROSS = (((1,), (1,)), ((), ()))


def row_order_kernel(order, near, far_u, near_out, far_out):
    size = 2 * LANES

    def step(n, _):
        columns = pl.ds(pl.multiple_of(n * size, size), size)
        rows = jnp.dot(order[...], near[:, columns], preferred_element_type=jnp.float32)
        near_out[:, columns] = rows.astype(jnp.bfloat16)
        return 0

    repeat(0, near.shape[1] // size, step, 4)
    rows = lax.dot_general(far_u[...], order[...], ACROSS, preferred_element_type=jnp.float32)
    far_out[...] = rows.astype(jnp.bfloat16)


def operator_kernel(halves, wanted, here, there, near, far_v, far_u, *outs):
    count = wanted.shape[0] - 1
    rank = far_v.shape[0] // count
    across = functools.partial(
        lax.dot_general, dimension_numbers=ACROSS, preferred_element_type=jnp.float32
    )
    size = here.shape[0]

    def traces(k):
        at = wanted[k] % size
        return jnp.where(wanted[k] < size, here[at], there[at])

    rows = across(traces(0), near[...])
    far = jnp.concatenate([traces(1 + k) for k in range(count)], axis=0)
    products = across(far, far_v[...])
    group = lax.broadcasted_iota(jnp.int32, (E, count * rank), 1) // rank
    weights = jnp.zeros((E, count * rank), jnp.float32)
    for k in range(count):
        weights = jnp.where(group == k, products[k * E : (k + 1) * E], weights)
    rows = rows + jnp.dot(
        weights.astype(jnp.bfloat16), far_u[...], preferred_element_type=jnp.float32
    )
    if halves:
        half = rows.shape[1] // 2
        first = index("gy") == 0
        outs[0][...] = jnp.where(first, rows[:, :half], rows[:, half:])
        outs[1][...] = jnp.where(first, rows[:, half:], rows[:, :half])
    else:
        outs[0][...] = rows


def finish_kernel(count, *refs):
    parts = refs[:count]
    inv, slab, tail, _, flux_out, out, held_flux, sems = refs[count:]
    side = index("gz")
    rows_x, _, width = slab.shape
    size, depth, _ = tail.shape
    columns = off_face(side, depth)
    tail_copy = pltpu.make_async_copy(
        tail.at[:, columns, :], out.at[rows_x - size :, columns, :], sems.at[2]
    )
    tail_copy.start()
    total = parts[0][...]
    if count == 2:
        total = total + parts[1][...]
    wide = jnp.concatenate([total, jnp.zeros((LANES - E, total.shape[1]), jnp.float32)], axis=0).T
    columns = []
    for start in range(0, width // E, LANES // E):
        column = wide[start * rows_x : (start + 1) * rows_x]
        for k in range(1, LANES // E):
            column = column + roll(wide[(start + k) * rows_x : (start + k + 1) * rows_x], k * E, 1)
        columns.append(column)
    flux = jnp.concatenate(columns, axis=1)
    held_flux[...] = flux[:, None, :]
    out_copy = pltpu.make_async_copy(held_flux, flux_out, sems.at[0])
    out_copy.start()
    added = (flux * inv[...])[:, None, :]
    row = lax.broadcasted_iota(jnp.int32, slab.shape, 1)
    slab[...] = slab[...] + jnp.where(row == side * (ROWS - 1), added, 0.0)
    top = pl.multiple_of(side * (out.shape[1] - ROWS), ROWS)
    copy = pltpu.make_async_copy(slab, out.at[:, pl.ds(top, ROWS), :], sems.at[1])
    copy.start()
    tail_copy.wait()
    out_copy.wait()
    copy.wait()


def put_side(cells, odd, messages, rows, first, last, c):
    halo = HALO * E
    lane = lane_ids(c)
    axis = c.ndim - 1
    low = jnp.where(lane < halo, first, roll(c, halo, axis))
    high = jnp.where(lane < halo, roll(last, halo, axis), roll(c, halo - (cells - HALO), axis))
    for number, message in enumerate(messages):
        message[rows] = choose(odd, low, high, number)


def side_edge_kernel(source, inv, *messages):
    rows_x, _, width = source.shape
    first, last = source[:, :, :LANES], source[:, :, width - LANES :]
    own = slice(HALO - 1, HALO - 1 + rows_x)
    put_side(width // E, index("gy") % 2, messages, own, first, last, inv[...])


def side_halo_kernel(nx, ny, depth, *refs):
    odd_x, odd_y = index("gx") % 2, index("gy") % 2
    got_x, messages = [r[...] for r in refs[:nx]], refs[nx + ny :]
    width = got_x[0].shape[1]
    rows_x = messages[0].shape[0] - 2 * (HALO - 1)
    for start, skip, edge in (
        (0, 1, from_low(odd_x, got_x)),
        (HALO - 1 + rows_x, 0, from_high(odd_x, got_x)),
    ):
        planes, compacts = row_layers(edge, depth)
        for k in range(HALO - 1):
            s, c = planes[k + skip], compacts[k + skip]
            first, last = s[:, :LANES], s[:, width - LANES :]
            put_side(width // E, odd_y, messages, start + k, first, last, c)


def widen(cells, ring, s, c, left, right):
    lane = lane_ids(right)
    width = HALO * E
    axis = right.ndim - 1
    zero = jnp.zeros_like(right)
    after = jnp.where(lane < width, right, zero)
    before = jnp.where(lane >= LANES - width, roll(left, LANES - width, axis), zero)
    pads = [after + before] if ring - cells == LANES // E else [after, before]
    own = jnp.where(lane < cells, c, zero)
    c_after = jnp.where((lane >= cells) & (lane < cells + HALO), roll(right, cells - width, axis), zero)
    c_before = jnp.where(
        (lane >= ring - HALO) & (lane < ring), roll(left, ring - HALO - width, axis), zero
    )
    return [s, *pads], own + c_after + c_before


def depth_edge_kernel(cells, ring, nx, ny, source, inv, *refs):
    odd_x, odd_y, side = index("gx") % 2, index("gy") % 2, index("gz")
    got_x, got_y, (two_out, one_out) = refs[:nx], refs[nx : nx + ny], refs[nx + ny :]
    rows_x, depth, width = source.shape
    wide = ring * E
    rows = two_out.shape[1]
    packs = jnp.zeros((rows, LANES), jnp.float32)

    def layer(message, z):
        lanes = message[HALO * depth + z % ROWS : HALO * depth + z % ROWS + 1, z // ROWS * LANES :]
        lanes = lanes[:, :LANES]
        lines = []
        for n in range(HALO):
            line = message[n * depth + z : n * depth + z + 1, :]
            compact = jnp.where(lane_ids(lanes) < 32, roll(lanes, -32 * n, 1), 0.0)
            lines.append(jnp.concatenate([line, compact], axis=1))
        return jnp.concatenate(lines, axis=0)

    for k in range(HALO):
        inner = lambda r: jnp.where(side == 0, r[:, depth - HALO + k, :], r[:, k, :])
        edges = [jnp.where(side == 0, layer(r, depth - HALO + k), layer(r, k)) for r in got_x]
        below, above = from_low(odd_x, edges), from_high(odd_x, edges)
        empty = jnp.zeros((rows - rows_x - 2 * HALO + 1, LANES), jnp.float32)
        beside = [jnp.concatenate([empty[:1], inner(r), empty], axis=0) for r in got_y]
        own = jnp.concatenate([inner(source), inner(inv)], axis=1)
        blank = jnp.zeros((rows - rows_x - 2 * HALO, width + LANES), jnp.float32)
        all_rows = jnp.concatenate([below, own, above, blank], axis=0)
        parts, compact = widen(
            cells, ring, all_rows[:, :width], all_rows[:, width:],
            from_low(odd_y, beside), from_high(odd_y, beside),
        )
        compact = jnp.where(lane_ids(compact) < ring, compact, 0.0)
        packs = packs + roll(compact, 32 * k, 1)
        out = jnp.concatenate(parts, axis=1)
        if k < 2:
            two_out[k] = out
        else:
            one_out[:, :wide] = out
    one_out[:, wide:] = packs


def assemble_kernel(cells, ring, nx, ny, source, inv, *refs):
    odd_x, odd_y = index("gx") % 2, index("gy") % 2
    got_x, got_y = refs[:nx], refs[nx : nx + ny]
    ext_s, ext_i, one, compacts, matrix = refs[nx + ny :]
    rows_x, depth, width = source.shape
    wide = ring * E
    all_z = depth + ROWS
    total = ext_s.shape[0]
    matrix[...] = spread_matrix(ring, wide)
    def place(x, s, c, got):
        parts, compact = widen(cells, ring, s, c, from_low(odd_y, got), from_high(odd_y, got))
        first = pl.ds(pl.multiple_of(x * all_z, ROWS), depth)
        compacts[first, :] = compact
        at = 0
        for part in parts:
            ext_s[first, at : at + part.shape[1]] = part
            at += part.shape[1]

    def own(x, _):
        place(x + HALO, source[x], inv[x], [r[x + HALO - 1] for r in got_y])
        return 0

    repeat(0, rows_x, own, 32)
    got = [r[...] for r in got_x]
    for base, skip, edge in ((0, 0, from_low(odd_x, got)), (rows_x + HALO, 2, from_high(odd_x, got))):
        planes, compact = row_layers(edge, depth)
        for k in range(HALO):
            if k == skip:
                beside = [jnp.zeros((depth, LANES), jnp.float32) for _ in got_y]
            else:
                beside = [r[base + k - 1] for r in got_y]
            place(base + k, planes[k], compact[k], beside)
    chunk = max(n for n in range(2 * ROWS, 321, 2 * ROWS) if total % n == 0)

    def expand(n, _):
        rows = pl.ds(pl.multiple_of(n * chunk, 2 * ROWS), chunk)
        some = packed(compacts[rows, :], ring)
        inverse = jnp.dot(some, matrix[...], preferred_element_type=jnp.float32)
        ext_i[rows, :] = inverse
        one[rows, :] = ext_s[rows, :] * inverse
        return 0

    repeat(0, total // chunk, expand, 5)


def depth_rows_kernel(ring, z_two, z_one, _s, _i, _o, ext_s, ext_i, one, compacts, inverses, matrix):
    all_x = compacts.shape[0] // ROWS
    all_z = ext_s.shape[0] // all_x
    depth, wide = all_z - ROWS, ring * E
    matrix[...] = spread_matrix(ring, wide)
    start = index("gz") * (ROWS - HALO)

    def rest(x):
        return pl.ds(pl.multiple_of(x * all_z + depth, ROWS), ROWS)

    def tile_of(x):
        return pl.ds(pl.multiple_of(x * ROWS, ROWS), ROWS)

    def spaced(rows):
        at = lax.broadcasted_iota(jnp.int32, (ROWS, rows[0].shape[1]), 0) - start
        tile = jnp.zeros(at.shape, jnp.float32)
        for k, value in enumerate(rows):
            tile = jnp.where(at == k, value, tile)
        return tile

    def zone(x, _):
        last = z_one[pl.ds(x, 1), :]
        ext_s[rest(x), :] = spaced(
            [z_two[0, pl.ds(x, 1), :], z_two[1, pl.ds(x, 1), :], last[:, :wide]]
        )
        packs = jnp.broadcast_to(last[:, wide:], (ROWS, LANES))
        compacts[tile_of(x), :] = spaced([roll(packs, -32 * k, 1) for k in range(HALO)])
        return 0

    def spread_out(x, _):
        i = inverses[tile_of(x), :]
        ext_i[rest(x), :] = i
        one[rest(x), :] = ext_s[rest(x), :] * i
        return 0

    repeat(0, all_x, zone, 38)
    some = packed(compacts[...], ring)
    inverses[...] = jnp.dot(some, matrix[...], preferred_element_type=jnp.float32)
    repeat(0, all_x, spread_out, 38)


def repeat(first, last, step, most):
    count = last - first
    unroll = max(n for n in range(1, most + 1) if count % n == 0)
    lax.fori_loop(first, last, step, 0, unroll=unroll)


def swept(ext_s, ext_i, old, x, all_z, depth, width, store):
    at = lambda x, rows: pl.ds(pl.multiple_of(x * all_z, ROWS), rows)
    tiles = old.shape[1] // LANES
    lane = lax.broadcasted_iota(jnp.int32, (depth, LANES), 1)
    known = {}

    def tile(j):
        j %= tiles
        if j not in known:
            u = old[at(x, all_z), j * LANES : (j + 1) * LANES]
            known[j] = (u, roll(u[:depth], E, 1), roll(u[:depth], -E, 1))
        return known[j]

    for j in range(width // LANES):
        columns = slice(j * LANES, (j + 1) * LANES)
        here = tile(j)
        beside = old[at(x - 1, depth), columns] + old[at(x + 1, depth), columns]
        up = roll(here[0], 1, 0) + roll(here[0], -1, 0)
        side = jnp.where(lane < E, tile(j - 1)[1], here[1])
        side = side + jnp.where(lane >= LANES - E, tile(j + 1)[2], here[2])
        beside = beside + (up[:depth] + side)
        new = (ext_s[at(x, depth), columns] + beside) * ext_i[at(x, depth), columns]
        store(columns, new)


def sweep_kernel(all_z, first, last, ext_s, ext_i, old, *refs):
    new = refs[-1]

    def step(x, _):
        def store(columns, value):
            new[pl.ds(pl.multiple_of(x * all_z, ROWS), all_z), columns] = value

        swept(ext_s, ext_i, old, x, all_z, all_z, old.shape[1], store)
        return 0

    repeat(first, last, step, 36)


def off_face(side, depth):
    return pl.ds(pl.multiple_of((1 - side) * ROWS, ROWS), depth - ROWS)


def last_sweep_kernel(pieces, ext_s, ext_i, old, out, slab, tail, done, sems):
    side = index("gz")
    rows_x, depth, width = out.shape
    all_z = depth + ROWS
    size = rows_x // pieces
    copies = []
    for n in range(pieces):
        target, shift = (tail, n * size) if n == pieces - 1 else (done, 0)

        def step(x, _, target=target, shift=shift):
            def store(columns, value):
                target[x - shift, :, columns] = value
                slab[x, :, columns] = jnp.where(side == 0, value[:ROWS], value[depth - ROWS :])

            swept(ext_s, ext_i, old, x + HALO, all_z, depth, width, store)
            return 0

        repeat(n * size, (n + 1) * size, step, 8)
        if n < pieces - 1:
            rows, columns = slice(n * size, (n + 1) * size), off_face(side, depth)
            copies.append(
                pltpu.make_async_copy(done.at[rows, columns, :], out.at[rows, columns, :], sems.at[n])
            )
            copies[-1].start()
    for copy in copies:
        copy.wait()


def body(source, coef, face_trace, near_col, far_col, near_tile, far_u, far_v):
    rows_x, depth, width = source.shape
    cells = coef.shape[2]
    groups = lax.axis_size("gy")
    size_x = lax.axis_size("gx")
    tile = near_tile.shape[3]
    count = far_u.shape[3]
    rank = far_u.shape[4]
    nx, ny = message_count("gx"), message_count("gy")
    bf16 = jnp.bfloat16
    both = [(0, 1), (1, 0)]
    pad = LANES if groups == 2 else 2 * LANES
    ring = (width + pad) // E
    wide = width + pad
    all_x, all_z = rows_x + 2 * HALO, depth + ROWS
    part = rows_x * cells
    halves = groups == 2
    coef = coef.transpose(0, 2, 1)

    held_source, inv, near, *vol_x = call(
        face_start_kernel, (kept(source), kept(coef)),
        [vector(source.shape), vector((rows_x, depth, LANES)), vector((NEAR * rows_x + ROWS, width))]
        + [vector((HALO * depth + ROWS, width))] * nx,
        in_specs=[MAIN, MAIN],
        scratch=(vector(coef.shape), pltpu.SemaphoreType.DMA((2,))),
    )
    if halves:
        other = held(lax.ppermute(near, "gy", both))
    else:
        other = held(lax.all_gather(near, "gy", axis=0, tiled=False))
    got_vol_x = swap(vol_x, "gx")
    full = vector((NEAR, rows_x, width * groups))
    s_face, i_face, i_own, *face_x = call(
        functools.partial(face_side_kernel, groups), (near, other),
        [full, full, vector((rows_x, width))]
        + [vector(((1 + n) * ROWS, width * groups)) for n in range(nx)], work=500,
    )
    got_x = swap(face_x, "gx")
    (order,) = call(order_kernel, (face_trace,), [vector((tile, tile), bf16)], after=(near,))
    sides = [vector((all_x - 2, depth, LANES))] * ny
    vol_y = call(side_edge_kernel, (held_source, inv), sides, after=(near,))
    vol_y = call(
        functools.partial(side_halo_kernel, nx, ny, depth), (*got_vol_x, *vol_y), sides,
        after=(order, *got_x), input_output_aliases={nx + n: n for n in range(ny)},
    )
    got_vol_y = swap(vol_y, "gy")

    ext = pltpu.VMEM((2, rows_x + 2 * ROWS, width * groups + LANES), jnp.float32)
    (traces,) = call(
        functools.partial(face_trace_kernel, nx), (s_face, i_face, order, *got_x),
        [vector((1, E, tile), bf16)], scratch=(ext, ext),
    )
    steps = doubling(size_x)
    for step in steps:
        other = held(lax.ppermute(traces, "gx", [(i, i ^ step) for i in range(size_x)]))
        twice = (2 * traces.shape[0], E, tile)
        before = ()
        if step == steps[0]:
            (spot,) = call(
                spot_kernel, (near_col, far_col), [pltpu.SMEM((count + 1,), jnp.int32)],
                in_specs=[SCALAR, SCALAR], out_specs=[SCALAR], after=(traces,),
            )
            before = (spot,)
        if step == steps[-2]:
            near, far_rows = call(
                row_order_kernel,
                (order, held(near_tile.reshape(tile, tile)), held(far_u.reshape(count * rank, tile))),
                [vector((tile, tile), bf16), vector((count * rank, tile), bf16)], work=3000,
                after=(traces,),
            )
            before = (*before, near)
        if step == 1:
            rounded = -(-all_x // ROWS) * ROWS
            vol_z = call(
                functools.partial(depth_edge_kernel, cells, ring, nx, ny),
                (held_source, inv, *got_vol_x, *got_vol_y),
                [vector((2, rounded, wide)), vector((rounded, wide + LANES))], work=500,
                after=(traces,),
            )
            got_vol_z = [held(lax.ppermute(v, "gz", both)) for v in vol_z]
            ext = vector((all_x * all_z, wide))
            most = call(
                functools.partial(assemble_kernel, cells, ring, nx, ny),
                (held_source, inv, *got_vol_x, *got_vol_y), [ext, ext, ext],
                scratch=(vector((all_x * all_z, LANES)), vector((LANES, wide), bf16)),
                after=vol_z,
            )
            ext_s, ext_i, one = call(
                functools.partial(depth_rows_kernel, ring), (*got_vol_z, *most), [ext, ext, ext],
                scratch=(
                    vector((all_x * ROWS, LANES)), vector((all_x * ROWS, wide)),
                    vector((LANES, wide), bf16),
                ),
                input_output_aliases={2: 0, 3: 1, 4: 2},
            )
            (two,) = call(
                functools.partial(sweep_kernel, all_z, 1, all_x - 1), (ext_s, ext_i, one), [ext],
                work=2500,
            )
            before = (two,)
        (traces,) = call(
            join_kernel, (traces, other), [vector(twice, bf16)], work=300, after=before
        )
    other = held(lax.ppermute(traces, "gz", both))
    middle = 2 + (all_x - 4) * 3 // 5
    (three,) = call(
        functools.partial(sweep_kernel, all_z, 2, middle), (ext_s, ext_i, two), [ext], work=1400,
        after=(traces,),
    )

    rows = call(
        functools.partial(operator_kernel, halves),
        (spot, traces, other, near, held(far_v.reshape(count * rank, tile)), far_rows),
        [vector((E, part))] * 2 if halves else [plain((E, tile))],
        in_specs=[SCALAR] + [VECTOR] * 5, work=2500, after=(three,),
    )
    if halves:
        sums = (rows[0], held(lax.ppermute(rows[1], "gy", both)))
    else:
        sums = (held(lax.psum_scatter(rows[0], "gy", scatter_dimension=1, tiled=True)),)
    (three,) = call(
        functools.partial(sweep_kernel, all_z, middle, all_x - 2), (ext_s, ext_i, two, three), [ext],
        work=1400, input_output_aliases={3: 0}, after=rows,
    )
    pieces = 4
    size = rows_x // pieces
    field, slab, tail = call(
        functools.partial(last_sweep_kernel, pieces), (ext_s, ext_i, three),
        [plain(source.shape), vector((rows_x, ROWS, width)), vector((size, depth, width))],
        out_specs=[MAIN, VECTOR, VECTOR], work=2000,
        scratch=(vector((rows_x - size, depth, width)), pltpu.SemaphoreType.DMA((pieces - 1,))),
    )

    flux, result = call(
        functools.partial(finish_kernel, len(sums)), (*sums, i_own, slab, tail, field),
        [plain((rows_x, 1, width)), plain(source.shape)],
        in_specs=[VECTOR] * (len(sums) + 3) + [MAIN], out_specs=[MAIN, MAIN],
        scratch=(vector((rows_x, 1, width)), pltpu.SemaphoreType.DMA((3,))),
        input_output_aliases={len(sums) + 3: 1},
    )
    return (result, flux)


def solution(mesh):
    return jax.shard_map(
        body,
        mesh=mesh,
        in_specs=(
            P("gx", "gz", "gy"),
            P("gx", "gz", "gy"),
            P("gx", "gz", None),
            P("gx", "gz", "gy"),
            P("gx", "gz", "gy", None),
            P("gx", "gz", "gy", None, None),
            P("gx", "gz", "gy", None, None, None),
            P("gx", "gz", "gy", None, None, None),
        ),
        out_specs=(P("gx", "gz", "gy"), P("gx", "gz", "gy")),
        check_vma=False,
    )
```

```python
import functools
import math

import jax
import jax.numpy as jnp
from jax import lax
from jax.experimental import pallas as pl
from jax.experimental.pallas import tpu as pltpu
from jax.sharding import PartitionSpec as P

E = 32
LANES = 128
ROWS = 8
HALO = 3
NEAR = 3


def roll(value, shift, axis):
    return pltpu.roll(value, shift % value.shape[axis], axis)


def lane_ids(value):
    return lax.broadcasted_iota(jnp.int32, value.shape, value.ndim - 1)


def held(value):
    return pltpu.with_memory_space_constraint(value, pltpu.VMEM)


def kept(value):
    return pltpu.with_memory_space_constraint(value, pltpu.HBM)


VECTOR = pl.BlockSpec(memory_space=pltpu.VMEM)
SCALAR = pl.BlockSpec(memory_space=pltpu.SMEM)
PLACED = pl.BlockSpec(memory_space=pl.ANY)
MAIN = pl.BlockSpec(memory_space=pltpu.HBM)


def vector(shape, dtype=jnp.float32):
    return pltpu.VMEM(shape, dtype)


def plain(shape, dtype=jnp.float32):
    return jax.ShapeDtypeStruct(shape, dtype)


def size_of(a):
    return math.prod(a.shape) * jnp.dtype(a.dtype).itemsize


def call(kernel, operands, out_shape, in_specs=None, out_specs=None, scratch=(), room=8, work=1000, after=(), **kw):
    given, tokens = len(operands), len(after)

    def body(*refs):
        kernel(*refs[:given], *refs[given + tokens :])

    return pl.pallas_call(
        body,
        out_shape=out_shape,
        in_specs=(in_specs or [VECTOR] * given) + [PLACED] * tokens,
        out_specs=out_specs or [VECTOR] * len(out_shape),
        scratch_shapes=list(scratch),
        compiler_params=pltpu.CompilerParams(vmem_limit_bytes=room * 1024 * 1024),
        cost_estimate=pl.CostEstimate(flops=0, bytes_accessed=work * 3000, transcendentals=0),
        **kw,
    )(*operands, *after)


def index(axis):
    return lax.axis_index(axis).astype(jnp.int32)


def pairs(count):
    first = [(i, i ^ 1) for i in range(count)]
    second = [(i, i + 1) for i in range(1, count - 1, 2)]
    return first, second + [(b, a) for a, b in second]


def swap(messages, axis):
    count = lax.axis_size(axis)
    return [held(lax.ppermute(m, axis, p)) for m, p in zip(messages, pairs(count))]


def doubling(count):
    steps = []
    while count > 1:
        count //= 2
        steps.append(count)
    return steps


def message_count(axis):
    return 1 if lax.axis_size(axis) == 2 else 2


def choose(odd, low, high, number):
    return jnp.where(odd == number, high, low)


def from_low(odd, received):
    other = received[1] if len(received) == 2 else jnp.zeros_like(received[0])
    return jnp.where(odd == 1, received[0], other)


def from_high(odd, received):
    other = received[1] if len(received) == 2 else jnp.zeros_like(received[0])
    return jnp.where(odd == 1, other, received[0])


def spread_matrix(cells, width):
    k = lax.broadcasted_iota(jnp.int32, (LANES, width), 0)
    cell = lax.broadcasted_iota(jnp.int32, (LANES, width), 1) // E
    part = k // 32
    hit = (k - part * 32 == cell) & (part < 3) & (cell < cells)
    return jnp.where(hit, 1.0, 0.0).astype(jnp.bfloat16)


def packed(compact, cells):
    compact = jnp.where(lane_ids(compact) < cells, compact, 0.0)
    high = compact.astype(jnp.bfloat16).astype(jnp.float32)
    rest = compact - high
    middle = rest.astype(jnp.bfloat16).astype(jnp.float32)
    low = (rest - middle).astype(jnp.bfloat16).astype(jnp.float32)
    axis = compact.ndim - 1
    return (high + roll(middle, 32, axis) + roll(low, 64, axis)).astype(jnp.bfloat16)


def spread(compact, width, cells):
    return jnp.dot(
        packed(compact, cells), spread_matrix(cells, width), preferred_element_type=jnp.float32
    )


def face_start_kernel(source, coef, trace, held_source, held_trace, inv, message, *refs):
    edges, (coefs, sems) = refs[:-2], refs[-2:]
    odd, side = index("gx") % 2, index("gz")
    rows_x, depth, width = source.shape
    cells = width // E
    copies = [
        pltpu.make_async_copy(coef, coefs, sems.at[0]),
        pltpu.make_async_copy(source, held_source, sems.at[1]),
        pltpu.make_async_copy(trace, held_trace, sems.at[2]),
    ]
    for copy in copies:
        copy.start()
    copies[0].wait()
    c = jnp.swapaxes(1.0 / (6.0 + coefs[...]), 1, 2)
    inv[...] = jnp.concatenate(
        [c, jnp.zeros((rows_x, depth, LANES - cells), jnp.float32)], axis=2
    )
    compact = jnp.zeros((rows_x, LANES), jnp.float32)
    for d in range(NEAR):
        plane = jnp.where(side == 0, inv[:, d, :], inv[:, depth - 1 - d, :])
        compact = compact + roll(plane, 32 * d, 1)
    for n in range(rows_x // ROWS):
        message[NEAR * rows_x :, n * LANES : (n + 1) * LANES] = compact[n * ROWS : (n + 1) * ROWS]
    copies[1].wait()
    for d in range(NEAR):
        plane = jnp.where(side == 0, held_source[:, d, :], held_source[:, depth - 1 - d, :])
        message[d * rows_x : (d + 1) * rows_x, :] = plane
    row_edges(odd, held_source, inv, edges)
    copies[2].wait()


def row_edges(odd, source, inv, messages):
    rows_x, depth, width = source.shape
    for number, message in enumerate(messages):
        packs = jnp.zeros((depth, LANES), jnp.float32)
        for k in range(HALO):
            last = rows_x - HALO + k
            message[k * depth : (k + 1) * depth, :] = choose(odd, source[k], source[last], number)
            packs = packs + roll(choose(odd, inv[k], inv[last], number), 32 * k, 1)
        for n in range(depth // ROWS):
            message[HALO * depth :, n * LANES : (n + 1) * LANES] = packs[n * ROWS : (n + 1) * ROWS]


def row_layers(message, depth):
    packs = jnp.concatenate(
        [message[HALO * depth :, n * LANES : (n + 1) * LANES] for n in range(depth // ROWS)], axis=0
    )
    planes = [message[k * depth : (k + 1) * depth] for k in range(HALO)]
    return planes, [jnp.where(lane_ids(packs) < 32, roll(packs, -32 * k, 1), 0.0) for k in range(HALO)]


def face_side_kernel(groups, own, other, s_out, i_out, i_own, *messages):
    odd = index("gx") % 2
    if groups == 2:
        first = index("gy") == 0
        parts = [jnp.where(first, own[...], other[...]), jnp.where(first, other[...], own[...])]
    else:
        parts = [other[n] for n in range(groups)]
    width = own.shape[1]
    cells = width // E
    rows_x = i_own.shape[0]

    def inverse(part):
        pieces = [
            part[NEAR * rows_x :, n * LANES : (n + 1) * LANES] for n in range(rows_x // ROWS)
        ]
        compact = jnp.concatenate(pieces, axis=0)
        planes = jnp.concatenate([roll(compact, -32 * d, 1) for d in range(NEAR)], axis=0)
        return spread(planes, width, cells)

    i_own[...] = inverse(own[...])[:rows_x]
    s_all = jnp.concatenate([part[: NEAR * rows_x] for part in parts], axis=1)
    i_all = jnp.concatenate([inverse(part) for part in parts], axis=1)
    for all_planes, out in ((s_all, s_out), (i_all, i_out)):
        for d in range(NEAR):
            out[d] = all_planes[d * rows_x : (d + 1) * rows_x]
    for number, message in enumerate(messages):
        for k, all_planes in enumerate((s_all, i_all)):
            for d in range(2):
                row = 4 * k + 2 * d
                top = d * rows_x
                message[row : row + 2, :] = choose(
                    odd, all_planes[top : top + 2], all_planes[top + rows_x - 2 : top + rows_x], number
                )


def face_trace_kernel(nx, s_in, i_in, order, *refs):
    odd = index("gx") % 2
    got = [r[:ROWS] for r in refs[:nx]]
    out, ext_s, ext_i = refs[nx:]
    _, rows_x, width = s_in.shape
    below, above = from_low(odd, got), from_high(odd, got)
    ext_s[...] = jnp.zeros(ext_s.shape, jnp.float32)
    ext_i[...] = jnp.zeros(ext_i.shape, jnp.float32)
    first, last = ROWS, ROWS + rows_x
    for ext, own, k in ((ext_s, s_in, 0), (ext_i, i_in, 1)):
        for d in range(2):
            row = 4 * k + 2 * d
            ext[d, first:last, :width] = own[d]
            ext[d, first - 2 : first, :width] = below[row : row + 2]
            ext[d, last : last + 2, :width] = above[row : row + 2]

    def around(u):
        return roll(u, 1, 0) + roll(u, -1, 0) + roll(u, E, 1) + roll(u, -E, 1)

    s0, i0, i1 = ext_s[0], ext_i[0], ext_i[1]
    u0, u1 = s0 * i0, ext_s[1] * i1
    deep = s_in[2] * i_in[2]
    v0 = (s0 + (around(u0) + u1)) * i0
    own = (around(u1) + u0)[first:last, :width]
    v1 = (s_in[1] + (own + deep)) * i_in[1]
    face = (s_in[0] + (around(v0)[first:last, :width] + v1)) * i_in[0]
    pieces = []
    for cell in range(width // E):
        start = cell * E // LANES * LANES
        pieces.append(roll(face[:, start : start + LANES], -(cell * E - start), 1))
    stacked = jnp.concatenate(pieces, axis=0)
    values = stacked.T[:E].astype(jnp.bfloat16)
    out[0] = jnp.dot(values, order[...], preferred_element_type=jnp.float32).astype(jnp.bfloat16)


def order_kernel(place, order):
    rows_x, _, cells_y = place.shape
    at = place[:, 0, :]
    trace = lax.broadcasted_iota(jnp.int32, (rows_x, order.shape[1]), 1)
    for y in range(cells_y):
        hit = at[:, y : y + 1] == trace
        order[y * rows_x : (y + 1) * rows_x, :] = jnp.where(hit, 1.0, 0.0).astype(jnp.bfloat16)


def spot_kernel(near_col, far_col, spot):
    at_x, at_z = index("gx"), index("gz")
    size_x = lax.axis_size("gx")
    for k in range(spot.shape[0]):
        block = near_col[0, 0, 0] if k == 0 else far_col[0, 0, 0, k - 1]
        apart = (block // 2) ^ at_x
        where = ((block % 2) ^ at_z) * size_x
        for n, step in enumerate(doubling(size_x)):
            where = where + jnp.where(apart & step > 0, 1 << n, 0)
        spot[k] = where


def join_kernel(one, two, out):
    count = one.shape[0]
    out[:count] = one[...]
    out[count:] = two[...]


ACROSS = (((1,), (1,)), ((), ()))


def row_order_kernel(order, near, far_u, near_out, far_out):
    size = 2 * LANES

    def step(n, _):
        columns = pl.ds(pl.multiple_of(n * size, size), size)
        rows = jnp.dot(order[...], near[:, columns], preferred_element_type=jnp.float32)
        near_out[:, columns] = rows.astype(jnp.bfloat16)
        return 0

    repeat(0, near.shape[1] // size, step, 4)
    rows = lax.dot_general(far_u[...], order[...], ACROSS, preferred_element_type=jnp.float32)
    far_out[...] = rows.astype(jnp.bfloat16)


def operator_kernel(halves, wanted, here, there, near, far_v, far_u, *outs):
    count = wanted.shape[0] - 1
    rank = far_v.shape[0] // count
    across = functools.partial(
        lax.dot_general, dimension_numbers=ACROSS, preferred_element_type=jnp.float32
    )
    size = here.shape[0]

    def traces(k):
        at = wanted[k] % size
        return jnp.where(wanted[k] < size, here[at], there[at])

    rows = across(traces(0), near[...])
    far = jnp.concatenate([traces(1 + k) for k in range(count)], axis=0)
    products = across(far, far_v[...])
    group = lax.broadcasted_iota(jnp.int32, (E, count * rank), 1) // rank
    weights = jnp.zeros((E, count * rank), jnp.float32)
    for k in range(count):
        weights = jnp.where(group == k, products[k * E : (k + 1) * E], weights)
    rows = rows + jnp.dot(
        weights.astype(jnp.bfloat16), far_u[...], preferred_element_type=jnp.float32
    )
    if halves:
        half = rows.shape[1] // 2
        first = index("gy") == 0
        outs[0][...] = jnp.where(first, rows[:, :half], rows[:, half:])
        outs[1][...] = jnp.where(first, rows[:, half:], rows[:, :half])
    else:
        outs[0][...] = rows


def finish_kernel(count, *refs):
    parts = refs[:count]
    inv, slab, tail, _, flux_out, out, held_flux, sems = refs[count:]
    side = index("gz")
    rows_x, _, width = slab.shape
    size, depth, _ = tail.shape
    columns = off_face(side, depth)
    tail_copy = pltpu.make_async_copy(
        tail.at[:, columns, :], out.at[rows_x - size :, columns, :], sems.at[2]
    )
    tail_copy.start()
    total = parts[0][...]
    if count == 2:
        total = total + parts[1][...]
    wide = jnp.concatenate([total, jnp.zeros((LANES - E, total.shape[1]), jnp.float32)], axis=0).T
    columns = []
    for start in range(0, width // E, LANES // E):
        column = wide[start * rows_x : (start + 1) * rows_x]
        for k in range(1, LANES // E):
            column = column + roll(wide[(start + k) * rows_x : (start + k + 1) * rows_x], k * E, 1)
        columns.append(column)
    flux = jnp.concatenate(columns, axis=1)
    held_flux[...] = flux[:, None, :]
    out_copy = pltpu.make_async_copy(held_flux, flux_out, sems.at[0])
    out_copy.start()
    added = (flux * inv[...])[:, None, :]
    row = lax.broadcasted_iota(jnp.int32, slab.shape, 1)
    slab[...] = slab[...] + jnp.where(row == side * (ROWS - 1), added, 0.0)
    top = pl.multiple_of(side * (out.shape[1] - ROWS), ROWS)
    copy = pltpu.make_async_copy(slab, out.at[:, pl.ds(top, ROWS), :], sems.at[1])
    copy.start()
    tail_copy.wait()
    out_copy.wait()
    copy.wait()


def put_side(cells, odd, messages, rows, first, last, c):
    halo = HALO * E
    lane = lane_ids(c)
    axis = c.ndim - 1
    low = jnp.where(lane < halo, first, roll(c, halo, axis))
    high = jnp.where(lane < halo, roll(last, halo, axis), roll(c, halo - (cells - HALO), axis))
    for number, message in enumerate(messages):
        message[rows] = choose(odd, low, high, number)


def side_edge_kernel(source, inv, *messages):
    rows_x, _, width = source.shape
    first, last = source[:, :, :LANES], source[:, :, width - LANES :]
    own = slice(HALO - 1, HALO - 1 + rows_x)
    put_side(width // E, index("gy") % 2, messages, own, first, last, inv[...])


def side_halo_kernel(nx, ny, depth, *refs):
    odd_x, odd_y = index("gx") % 2, index("gy") % 2
    got_x, messages = [r[...] for r in refs[:nx]], refs[nx + ny :]
    width = got_x[0].shape[1]
    rows_x = messages[0].shape[0] - 2 * (HALO - 1)
    for start, skip, edge in (
        (0, 1, from_low(odd_x, got_x)),
        (HALO - 1 + rows_x, 0, from_high(odd_x, got_x)),
    ):
        planes, compacts = row_layers(edge, depth)
        for k in range(HALO - 1):
            s, c = planes[k + skip], compacts[k + skip]
            first, last = s[:, :LANES], s[:, width - LANES :]
            put_side(width // E, odd_y, messages, start + k, first, last, c)


def widen(cells, ring, s, c, left, right):
    lane = lane_ids(right)
    width = HALO * E
    axis = right.ndim - 1
    zero = jnp.zeros_like(right)
    after = jnp.where(lane < width, right, zero)
    before = jnp.where(lane >= LANES - width, roll(left, LANES - width, axis), zero)
    pads = [after + before] if ring - cells == LANES // E else [after, before]
    own = jnp.where(lane < cells, c, zero)
    c_after = jnp.where((lane >= cells) & (lane < cells + HALO), roll(right, cells - width, axis), zero)
    c_before = jnp.where(
        (lane >= ring - HALO) & (lane < ring), roll(left, ring - HALO - width, axis), zero
    )
    return [s, *pads], own + c_after + c_before


def depth_edge_kernel(cells, ring, nx, ny, source, inv, *refs):
    odd_x, odd_y, side = index("gx") % 2, index("gy") % 2, index("gz")
    got_x, got_y, (two_out, one_out) = refs[:nx], refs[nx : nx + ny], refs[nx + ny :]
    rows_x, depth, width = source.shape
    wide = ring * E
    rows = two_out.shape[1]
    packs = jnp.zeros((rows, LANES), jnp.float32)

    def layer(message, z):
        lanes = message[HALO * depth + z % ROWS : HALO * depth + z % ROWS + 1, z // ROWS * LANES :]
        lanes = lanes[:, :LANES]
        lines = []
        for n in range(HALO):
            line = message[n * depth + z : n * depth + z + 1, :]
            compact = jnp.where(lane_ids(lanes) < 32, roll(lanes, -32 * n, 1), 0.0)
            lines.append(jnp.concatenate([line, compact], axis=1))
        return jnp.concatenate(lines, axis=0)

    for k in range(HALO):
        inner = lambda r: jnp.where(side == 0, r[:, depth - HALO + k, :], r[:, k, :])
        edges = [jnp.where(side == 0, layer(r, depth - HALO + k), layer(r, k)) for r in got_x]
        below, above = from_low(odd_x, edges), from_high(odd_x, edges)
        empty = jnp.zeros((rows - rows_x - 2 * HALO + 1, LANES), jnp.float32)
        beside = [jnp.concatenate([empty[:1], inner(r), empty], axis=0) for r in got_y]
        own = jnp.concatenate([inner(source), inner(inv)], axis=1)
        blank = jnp.zeros((rows - rows_x - 2 * HALO, width + LANES), jnp.float32)
        all_rows = jnp.concatenate([below, own, above, blank], axis=0)
        parts, compact = widen(
            cells, ring, all_rows[:, :width], all_rows[:, width:],
            from_low(odd_y, beside), from_high(odd_y, beside),
        )
        compact = jnp.where(lane_ids(compact) < ring, compact, 0.0)
        packs = packs + roll(compact, 32 * k, 1)
        out = jnp.concatenate(parts, axis=1)
        if k < 2:
            two_out[k] = out
        else:
            one_out[:, :wide] = out
    one_out[:, wide:] = packs


def assemble_kernel(cells, ring, nx, ny, source, inv, *refs):
    odd_x, odd_y = index("gx") % 2, index("gy") % 2
    got_x, got_y = refs[:nx], refs[nx : nx + ny]
    ext_s, ext_i, one, compacts, matrix = refs[nx + ny :]
    rows_x, depth, width = source.shape
    wide = ring * E
    all_z = depth + ROWS
    total = ext_s.shape[0]
    matrix[...] = spread_matrix(ring, wide)
    def place(x, s, c, got):
        parts, compact = widen(cells, ring, s, c, from_low(odd_y, got), from_high(odd_y, got))
        first = pl.ds(pl.multiple_of(x * all_z, ROWS), depth)
        compacts[first, :] = compact
        at = 0
        for part in parts:
            ext_s[first, at : at + part.shape[1]] = part
            at += part.shape[1]

    def own(x, _):
        place(x + HALO, source[x], inv[x], [r[x + HALO - 1] for r in got_y])
        return 0

    repeat(0, rows_x, own, 32)
    got = [r[...] for r in got_x]
    for base, skip, edge in ((0, 0, from_low(odd_x, got)), (rows_x + HALO, 2, from_high(odd_x, got))):
        planes, compact = row_layers(edge, depth)
        for k in range(HALO):
            if k == skip:
                beside = [jnp.zeros((depth, LANES), jnp.float32) for _ in got_y]
            else:
                beside = [r[base + k - 1] for r in got_y]
            place(base + k, planes[k], compact[k], beside)
    chunk = max(n for n in range(2 * ROWS, 321, 2 * ROWS) if total % n == 0)

    def expand(n, _):
        rows = pl.ds(pl.multiple_of(n * chunk, 2 * ROWS), chunk)
        some = packed(compacts[rows, :], ring)
        inverse = jnp.dot(some, matrix[...], preferred_element_type=jnp.float32)
        ext_i[rows, :] = inverse
        one[rows, :] = ext_s[rows, :] * inverse
        return 0

    repeat(0, total // chunk, expand, 5)


def depth_rows_kernel(ring, z_two, z_one, _s, _i, _o, ext_s, ext_i, one, compacts, inverses, matrix):
    all_x = compacts.shape[0] // ROWS
    all_z = ext_s.shape[0] // all_x
    depth, wide = all_z - ROWS, ring * E
    matrix[...] = spread_matrix(ring, wide)
    start = index("gz") * (ROWS - HALO)

    def rest(x):
        return pl.ds(pl.multiple_of(x * all_z + depth, ROWS), ROWS)

    def tile_of(x):
        return pl.ds(pl.multiple_of(x * ROWS, ROWS), ROWS)

    def spaced(rows):
        at = lax.broadcasted_iota(jnp.int32, (ROWS, rows[0].shape[1]), 0) - start
        tile = jnp.zeros(at.shape, jnp.float32)
        for k, value in enumerate(rows):
            tile = jnp.where(at == k, value, tile)
        return tile

    def zone(x, _):
        last = z_one[pl.ds(x, 1), :]
        ext_s[rest(x), :] = spaced(
            [z_two[0, pl.ds(x, 1), :], z_two[1, pl.ds(x, 1), :], last[:, :wide]]
        )
        packs = jnp.broadcast_to(last[:, wide:], (ROWS, LANES))
        compacts[tile_of(x), :] = spaced([roll(packs, -32 * k, 1) for k in range(HALO)])
        return 0

    def spread_out(x, _):
        i = inverses[tile_of(x), :]
        ext_i[rest(x), :] = i
        one[rest(x), :] = ext_s[rest(x), :] * i
        return 0

    repeat(0, all_x, zone, 38)
    some = packed(compacts[...], ring)
    inverses[...] = jnp.dot(some, matrix[...], preferred_element_type=jnp.float32)
    repeat(0, all_x, spread_out, 38)


def repeat(first, last, step, most):
    count = last - first
    unroll = max(n for n in range(1, most + 1) if count % n == 0)
    lax.fori_loop(first, last, step, 0, unroll=unroll)


def swept(ext_s, ext_i, old, x, all_z, depth, width, store):
    at = lambda x, rows: pl.ds(pl.multiple_of(x * all_z, ROWS), rows)
    tiles = old.shape[1] // LANES
    lane = lax.broadcasted_iota(jnp.int32, (depth, LANES), 1)
    known = {}

    def tile(j):
        j %= tiles
        if j not in known:
            u = old[at(x, all_z), j * LANES : (j + 1) * LANES]
            known[j] = (u, roll(u[:depth], E, 1), roll(u[:depth], -E, 1))
        return known[j]

    for j in range(width // LANES):
        columns = slice(j * LANES, (j + 1) * LANES)
        here = tile(j)
        beside = old[at(x - 1, depth), columns] + old[at(x + 1, depth), columns]
        up = roll(here[0], 1, 0) + roll(here[0], -1, 0)
        side = jnp.where(lane < E, tile(j - 1)[1], here[1])
        side = side + jnp.where(lane >= LANES - E, tile(j + 1)[2], here[2])
        beside = beside + (up[:depth] + side)
        new = (ext_s[at(x, depth), columns] + beside) * ext_i[at(x, depth), columns]
        store(columns, new)


def sweep_kernel(all_z, first, last, ext_s, ext_i, old, *refs):
    new = refs[-1]

    def step(x, _):
        def store(columns, value):
            new[pl.ds(pl.multiple_of(x * all_z, ROWS), all_z), columns] = value

        swept(ext_s, ext_i, old, x, all_z, all_z, old.shape[1], store)
        return 0

    repeat(first, last, step, 36)


def off_face(side, depth):
    return pl.ds(pl.multiple_of((1 - side) * ROWS, ROWS), depth - ROWS)


def last_sweep_kernel(pieces, ext_s, ext_i, old, out, slab, tail, done, sems):
    side = index("gz")
    rows_x, depth, width = out.shape
    all_z = depth + ROWS
    size = rows_x // pieces
    copies = []
    for n in range(pieces):
        target, shift = (tail, n * size) if n == pieces - 1 else (done, 0)

        def step(x, _, target=target, shift=shift):
            def store(columns, value):
                target[x - shift, :, columns] = value
                slab[x, :, columns] = jnp.where(side == 0, value[:ROWS], value[depth - ROWS :])

            swept(ext_s, ext_i, old, x + HALO, all_z, depth, width, store)
            return 0

        repeat(n * size, (n + 1) * size, step, 8)
        if n < pieces - 1:
            rows, columns = slice(n * size, (n + 1) * size), off_face(side, depth)
            copies.append(
                pltpu.make_async_copy(done.at[rows, columns, :], out.at[rows, columns, :], sems.at[n])
            )
            copies[-1].start()
    for copy in copies:
        copy.wait()


def body(source, coef, face_trace, near_col, far_col, near_tile, far_u, far_v):
    rows_x, depth, width = source.shape
    cells = coef.shape[2]
    groups = lax.axis_size("gy")
    size_x = lax.axis_size("gx")
    tile = near_tile.shape[3]
    count = far_u.shape[3]
    rank = far_u.shape[4]
    nx, ny = message_count("gx"), message_count("gy")
    bf16 = jnp.bfloat16
    both = [(0, 1), (1, 0)]
    pad = LANES if groups == 2 else 2 * LANES
    ring = (width + pad) // E
    wide = width + pad
    all_x, all_z = rows_x + 2 * HALO, depth + ROWS
    part = rows_x * cells
    halves = groups == 2
    coef = coef.transpose(0, 2, 1)

    held_source, held_trace, inv, near, *vol_x = call(
        face_start_kernel, (kept(source), kept(coef), kept(face_trace)),
        [vector(source.shape), vector(face_trace.shape, jnp.int32), vector((rows_x, depth, LANES)),
          vector((NEAR * rows_x + ROWS, width))]
        + [vector((HALO * depth + ROWS, width))] * nx,
        in_specs=[MAIN] * 3,
        scratch=(vector(coef.shape), pltpu.SemaphoreType.DMA((3,))),
    )
    if halves:
        other = held(lax.ppermute(near, "gy", both))
    else:
        other = held(lax.all_gather(near, "gy", axis=0, tiled=False))
    got_vol_x = swap(vol_x, "gx")
    full = vector((NEAR, rows_x, width * groups))
    s_face, i_face, i_own, *face_x = call(
        functools.partial(face_side_kernel, groups), (near, other),
        [full, full, vector((rows_x, width))]
        + [vector(((1 + n) * ROWS, width * groups)) for n in range(nx)], work=500,
    )
    got_x = swap(face_x, "gx")
    (order,) = call(order_kernel, (held_trace,), [vector((tile, tile), bf16)], after=(near,))
    sides = [vector((all_x - 2, depth, LANES))] * ny
    vol_y = call(side_edge_kernel, (held_source, inv), sides, after=(near,))
    vol_y = call(
        functools.partial(side_halo_kernel, nx, ny, depth), (*got_vol_x, *vol_y), sides,
        after=(order, *got_x), input_output_aliases={nx + n: n for n in range(ny)},
    )
    got_vol_y = swap(vol_y, "gy")

    ext = pltpu.VMEM((2, rows_x + 2 * ROWS, width * groups + LANES), jnp.float32)
    (traces,) = call(
        functools.partial(face_trace_kernel, nx), (s_face, i_face, order, *got_x),
        [vector((1, E, tile), bf16)], scratch=(ext, ext),
    )
    steps = doubling(size_x)
    for step in steps:
        other = held(lax.ppermute(traces, "gx", [(i, i ^ step) for i in range(size_x)]))
        twice = (2 * traces.shape[0], E, tile)
        before = ()
        if step == steps[0]:
            (spot,) = call(
                spot_kernel, (near_col, far_col), [pltpu.SMEM((count + 1,), jnp.int32)],
                in_specs=[SCALAR, SCALAR], out_specs=[SCALAR], after=(traces,),
            )
            before = (spot,)
        if step == steps[-2]:
            near, far_rows = call(
                row_order_kernel,
                (order, held(near_tile.reshape(tile, tile)), held(far_u.reshape(count * rank, tile))),
                [vector((tile, tile), bf16), vector((count * rank, tile), bf16)], work=3000,
                after=(traces,),
            )
            before = (*before, near)
        if step == 1:
            rounded = -(-all_x // ROWS) * ROWS
            vol_z = call(
                functools.partial(depth_edge_kernel, cells, ring, nx, ny),
                (held_source, inv, *got_vol_x, *got_vol_y),
                [vector((2, rounded, wide)), vector((rounded, wide + LANES))], work=500,
                after=(traces,),
            )
            got_vol_z = [held(lax.ppermute(v, "gz", both)) for v in vol_z]
            ext = vector((all_x * all_z, wide))
            most = call(
                functools.partial(assemble_kernel, cells, ring, nx, ny),
                (held_source, inv, *got_vol_x, *got_vol_y), [ext, ext, ext],
                scratch=(vector((all_x * all_z, LANES)), vector((LANES, wide), bf16)),
                after=vol_z,
            )
            ext_s, ext_i, one = call(
                functools.partial(depth_rows_kernel, ring), (*got_vol_z, *most), [ext, ext, ext],
                scratch=(
                    vector((all_x * ROWS, LANES)), vector((all_x * ROWS, wide)),
                    vector((LANES, wide), bf16),
                ),
                input_output_aliases={2: 0, 3: 1, 4: 2},
            )
            (two,) = call(
                functools.partial(sweep_kernel, all_z, 1, all_x - 1), (ext_s, ext_i, one), [ext],
                work=2500,
            )
            before = (two,)
        (traces,) = call(
            join_kernel, (traces, other), [vector(twice, bf16)], work=300, after=before
        )
    other = held(lax.ppermute(traces, "gz", both))
    middle = 2 + (all_x - 4) * 2 // 3
    (three,) = call(
        functools.partial(sweep_kernel, all_z, 2, middle), (ext_s, ext_i, two), [ext], work=1400,
        after=(traces,),
    )

    rows = call(
        functools.partial(operator_kernel, halves),
        (spot, traces, other, near, held(far_v.reshape(count * rank, tile)), far_rows),
        [vector((E, part))] * 2 if halves else [plain((E, tile))],
        in_specs=[SCALAR] + [VECTOR] * 5, work=2500, after=(three,),
    )
    if halves:
        sums = (rows[0], held(lax.ppermute(rows[1], "gy", both)))
    else:
        sums = (held(lax.psum_scatter(rows[0], "gy", scatter_dimension=1, tiled=True)),)
    (three,) = call(
        functools.partial(sweep_kernel, all_z, middle, all_x - 2), (ext_s, ext_i, two, three), [ext],
        work=1400, input_output_aliases={3: 0}, after=rows,
    )
    pieces = 4
    size = rows_x // pieces
    field, slab, tail = call(
        functools.partial(last_sweep_kernel, pieces), (ext_s, ext_i, three),
        [plain(source.shape), vector((rows_x, ROWS, width)), vector((size, depth, width))],
        out_specs=[MAIN, VECTOR, VECTOR], work=2000,
        scratch=(vector((rows_x - size, depth, width)), pltpu.SemaphoreType.DMA((pieces - 1,))),
    )

    flux, result = call(
        functools.partial(finish_kernel, len(sums)), (*sums, i_own, slab, tail, field),
        [plain((rows_x, 1, width)), plain(source.shape)],
        in_specs=[VECTOR] * (len(sums) + 3) + [MAIN], out_specs=[MAIN, MAIN],
        scratch=(vector((rows_x, 1, width)), pltpu.SemaphoreType.DMA((3,))),
        input_output_aliases={len(sums) + 3: 1},
    )
    return (result, flux)


def solution(mesh):
    return jax.shard_map(
        body,
        mesh=mesh,
        in_specs=(
            P("gx", "gz", "gy"),
            P("gx", "gz", "gy"),
            P("gx", "gz", None),
            P("gx", "gz", "gy"),
            P("gx", "gz", "gy", None),
            P("gx", "gz", "gy", None, None),
            P("gx", "gz", "gy", None, None, None),
            P("gx", "gz", "gy", None, None, None),
        ),
        out_specs=(P("gx", "gz", "gy"), P("gx", "gz", "gy")),
        check_vma=False,
    )
```

```python
import functools
import math

import jax
import jax.numpy as jnp
from jax import lax
from jax.experimental import pallas as pl
from jax.experimental.pallas import tpu as pltpu
from jax.sharding import PartitionSpec as P

E = 32
LANES = 128
ROWS = 8
HALO = 3
NEAR = 3


def roll(value, shift, axis):
    return pltpu.roll(value, shift % value.shape[axis], axis)


def lane_ids(value):
    return lax.broadcasted_iota(jnp.int32, value.shape, value.ndim - 1)


def held(value):
    return pltpu.with_memory_space_constraint(value, pltpu.VMEM)


def kept(value):
    return pltpu.with_memory_space_constraint(value, pltpu.HBM)


VECTOR = pl.BlockSpec(memory_space=pltpu.VMEM)
SCALAR = pl.BlockSpec(memory_space=pltpu.SMEM)
PLACED = pl.BlockSpec(memory_space=pl.ANY)
MAIN = pl.BlockSpec(memory_space=pltpu.HBM)


def vector(shape, dtype=jnp.float32):
    return pltpu.VMEM(shape, dtype)


def plain(shape, dtype=jnp.float32):
    return jax.ShapeDtypeStruct(shape, dtype)


def size_of(a):
    return math.prod(a.shape) * jnp.dtype(a.dtype).itemsize


def call(kernel, operands, out_shape, in_specs=None, out_specs=None, scratch=(), room=8, work=1000, after=(), **kw):
    given, tokens = len(operands), len(after)

    def body(*refs):
        kernel(*refs[:given], *refs[given + tokens :])

    return pl.pallas_call(
        body,
        out_shape=out_shape,
        in_specs=(in_specs or [VECTOR] * given) + [PLACED] * tokens,
        out_specs=out_specs or [VECTOR] * len(out_shape),
        scratch_shapes=list(scratch),
        compiler_params=pltpu.CompilerParams(vmem_limit_bytes=room * 1024 * 1024),
        cost_estimate=pl.CostEstimate(flops=0, bytes_accessed=work * 3000, transcendentals=0),
        **kw,
    )(*operands, *after)


def index(axis):
    return lax.axis_index(axis).astype(jnp.int32)


def pairs(count):
    first = [(i, i ^ 1) for i in range(count)]
    second = [(i, i + 1) for i in range(1, count - 1, 2)]
    return first, second + [(b, a) for a, b in second]


def swap(messages, axis):
    count = lax.axis_size(axis)
    return [held(lax.ppermute(m, axis, p)) for m, p in zip(messages, pairs(count))]


def doubling(count):
    steps = []
    while count > 1:
        count //= 2
        steps.append(count)
    return steps


def message_count(axis):
    return 1 if lax.axis_size(axis) == 2 else 2


def choose(odd, low, high, number):
    return jnp.where(odd == number, high, low)


def from_low(odd, received):
    other = received[1] if len(received) == 2 else jnp.zeros_like(received[0])
    return jnp.where(odd == 1, received[0], other)


def from_high(odd, received):
    other = received[1] if len(received) == 2 else jnp.zeros_like(received[0])
    return jnp.where(odd == 1, other, received[0])


def spread_matrix(cells, width):
    k = lax.broadcasted_iota(jnp.int32, (LANES, width), 0)
    cell = lax.broadcasted_iota(jnp.int32, (LANES, width), 1) // E
    part = k // 32
    hit = (k - part * 32 == cell) & (part < 3) & (cell < cells)
    return jnp.where(hit, 1.0, 0.0).astype(jnp.bfloat16)


def packed(compact, cells):
    compact = jnp.where(lane_ids(compact) < cells, compact, 0.0)
    high = compact.astype(jnp.bfloat16).astype(jnp.float32)
    rest = compact - high
    middle = rest.astype(jnp.bfloat16).astype(jnp.float32)
    low = (rest - middle).astype(jnp.bfloat16).astype(jnp.float32)
    axis = compact.ndim - 1
    return (high + roll(middle, 32, axis) + roll(low, 64, axis)).astype(jnp.bfloat16)


def spread(compact, width, cells):
    return jnp.dot(
        packed(compact, cells), spread_matrix(cells, width), preferred_element_type=jnp.float32
    )


def face_start_kernel(source, coef, trace, held_source, held_trace, inv, message, *refs):
    edges, (coefs, sems) = refs[:-2], refs[-2:]
    odd, side = index("gx") % 2, index("gz")
    rows_x, depth, width = source.shape
    cells = width // E
    copies = [
        pltpu.make_async_copy(coef, coefs, sems.at[0]),
        pltpu.make_async_copy(source, held_source, sems.at[1]),
        pltpu.make_async_copy(trace, held_trace, sems.at[2]),
    ]
    for copy in copies:
        copy.start()
    copies[0].wait()
    c = jnp.swapaxes(1.0 / (6.0 + coefs[...]), 1, 2)
    inv[...] = jnp.concatenate(
        [c, jnp.zeros((rows_x, depth, LANES - cells), jnp.float32)], axis=2
    )
    compact = jnp.zeros((rows_x, LANES), jnp.float32)
    for d in range(NEAR):
        plane = jnp.where(side == 0, inv[:, d, :], inv[:, depth - 1 - d, :])
        compact = compact + roll(plane, 32 * d, 1)
    for n in range(rows_x // ROWS):
        message[NEAR * rows_x :, n * LANES : (n + 1) * LANES] = compact[n * ROWS : (n + 1) * ROWS]
    copies[1].wait()
    for d in range(NEAR):
        plane = jnp.where(side == 0, held_source[:, d, :], held_source[:, depth - 1 - d, :])
        message[d * rows_x : (d + 1) * rows_x, :] = plane
    row_edges(odd, held_source, inv, edges)
    copies[2].wait()


def row_edges(odd, source, inv, messages):
    rows_x, depth, width = source.shape
    for number, message in enumerate(messages):
        packs = jnp.zeros((depth, LANES), jnp.float32)
        for k in range(HALO):
            last = rows_x - HALO + k
            message[k * depth : (k + 1) * depth, :] = choose(odd, source[k], source[last], number)
            packs = packs + roll(choose(odd, inv[k], inv[last], number), 32 * k, 1)
        for n in range(depth // ROWS):
            message[HALO * depth :, n * LANES : (n + 1) * LANES] = packs[n * ROWS : (n + 1) * ROWS]


def row_layers(message, depth):
    packs = jnp.concatenate(
        [message[HALO * depth :, n * LANES : (n + 1) * LANES] for n in range(depth // ROWS)], axis=0
    )
    planes = [message[k * depth : (k + 1) * depth] for k in range(HALO)]
    return planes, [jnp.where(lane_ids(packs) < 32, roll(packs, -32 * k, 1), 0.0) for k in range(HALO)]


def face_side_kernel(groups, own, other, s_out, i_out, i_own, *messages):
    odd = index("gx") % 2
    if groups == 2:
        first = index("gy") == 0
        parts = [jnp.where(first, own[...], other[...]), jnp.where(first, other[...], own[...])]
    else:
        parts = [other[n] for n in range(groups)]
    width = own.shape[1]
    cells = width // E
    rows_x = i_own.shape[0]

    def inverse(part):
        pieces = [
            part[NEAR * rows_x :, n * LANES : (n + 1) * LANES] for n in range(rows_x // ROWS)
        ]
        compact = jnp.concatenate(pieces, axis=0)
        planes = jnp.concatenate([roll(compact, -32 * d, 1) for d in range(NEAR)], axis=0)
        return spread(planes, width, cells)

    i_own[...] = inverse(own[...])[:rows_x]
    s_all = jnp.concatenate([part[: NEAR * rows_x] for part in parts], axis=1)
    i_all = jnp.concatenate([inverse(part) for part in parts], axis=1)
    for all_planes, out in ((s_all, s_out), (i_all, i_out)):
        for d in range(NEAR):
            out[d] = all_planes[d * rows_x : (d + 1) * rows_x]
    for number, message in enumerate(messages):
        for k, all_planes in enumerate((s_all, i_all)):
            for d in range(2):
                row = 4 * k + 2 * d
                top = d * rows_x
                message[row : row + 2, :] = choose(
                    odd, all_planes[top : top + 2], all_planes[top + rows_x - 2 : top + rows_x], number
                )


def face_trace_kernel(nx, s_in, i_in, order, *refs):
    odd = index("gx") % 2
    got = [r[:ROWS] for r in refs[:nx]]
    out, ext_s, ext_i = refs[nx:]
    _, rows_x, width = s_in.shape
    below, above = from_low(odd, got), from_high(odd, got)
    ext_s[...] = jnp.zeros(ext_s.shape, jnp.float32)
    ext_i[...] = jnp.zeros(ext_i.shape, jnp.float32)
    first, last = ROWS, ROWS + rows_x
    for ext, own, k in ((ext_s, s_in, 0), (ext_i, i_in, 1)):
        for d in range(2):
            row = 4 * k + 2 * d
            ext[d, first:last, :width] = own[d]
            ext[d, first - 2 : first, :width] = below[row : row + 2]
            ext[d, last : last + 2, :width] = above[row : row + 2]

    def around(u):
        return roll(u, 1, 0) + roll(u, -1, 0) + roll(u, E, 1) + roll(u, -E, 1)

    s0, i0, i1 = ext_s[0], ext_i[0], ext_i[1]
    u0, u1 = s0 * i0, ext_s[1] * i1
    deep = s_in[2] * i_in[2]
    v0 = (s0 + (around(u0) + u1)) * i0
    own = (around(u1) + u0)[first:last, :width]
    v1 = (s_in[1] + (own + deep)) * i_in[1]
    face = (s_in[0] + (around(v0)[first:last, :width] + v1)) * i_in[0]
    pieces = []
    for cell in range(width // E):
        start = cell * E // LANES * LANES
        pieces.append(roll(face[:, start : start + LANES], -(cell * E - start), 1))
    stacked = jnp.concatenate(pieces, axis=0)
    values = stacked.T[:E].astype(jnp.bfloat16)
    out[0] = jnp.dot(values, order[...], preferred_element_type=jnp.float32).astype(jnp.bfloat16)


def order_kernel(place, order):
    rows_x, _, cells_y = place.shape
    at = place[:, 0, :]
    trace = lax.broadcasted_iota(jnp.int32, (rows_x, order.shape[1]), 1)
    for y in range(cells_y):
        hit = at[:, y : y + 1] == trace
        order[y * rows_x : (y + 1) * rows_x, :] = jnp.where(hit, 1.0, 0.0).astype(jnp.bfloat16)


def spot_kernel(near_col, far_col, spot):
    at_x, at_z = index("gx"), index("gz")
    size_x = lax.axis_size("gx")
    for k in range(spot.shape[0]):
        block = near_col[0, 0, 0] if k == 0 else far_col[0, 0, 0, k - 1]
        apart = (block // 2) ^ at_x
        where = ((block % 2) ^ at_z) * size_x
        for n, step in enumerate(doubling(size_x)):
            where = where + jnp.where(apart & step > 0, 1 << n, 0)
        spot[k] = where


def join_kernel(one, two, out):
    count = one.shape[0]
    out[:count] = one[...]
    out[count:] = two[...]


ACROSS = (((1,), (1,)), ((), ()))


def row_order_kernel(order, near, far_u, near_out, far_out):
    size = 2 * LANES

    def step(n, _):
        columns = pl.ds(pl.multiple_of(n * size, size), size)
        rows = jnp.dot(order[...], near[:, columns], preferred_element_type=jnp.float32)
        near_out[:, columns] = rows.astype(jnp.bfloat16)
        return 0

    repeat(0, near.shape[1] // size, step, 4)
    rows = lax.dot_general(far_u[...], order[...], ACROSS, preferred_element_type=jnp.float32)
    far_out[...] = rows.astype(jnp.bfloat16)


def operator_kernel(halves, wanted, here, there, near, far_v, far_u, *outs):
    count = wanted.shape[0] - 1
    rank = far_v.shape[0] // count
    across = functools.partial(
        lax.dot_general, dimension_numbers=ACROSS, preferred_element_type=jnp.float32
    )
    size = here.shape[0]

    def traces(k):
        at = wanted[k] % size
        return jnp.where(wanted[k] < size, here[at], there[at])

    rows = across(traces(0), near[...])
    far = jnp.concatenate([traces(1 + k) for k in range(count)], axis=0)
    products = across(far, far_v[...])
    group = lax.broadcasted_iota(jnp.int32, (E, count * rank), 1) // rank
    weights = jnp.zeros((E, count * rank), jnp.float32)
    for k in range(count):
        weights = jnp.where(group == k, products[k * E : (k + 1) * E], weights)
    rows = rows + jnp.dot(
        weights.astype(jnp.bfloat16), far_u[...], preferred_element_type=jnp.float32
    )
    if halves:
        half = rows.shape[1] // 2
        first = index("gy") == 0
        outs[0][...] = jnp.where(first, rows[:, :half], rows[:, half:])
        outs[1][...] = jnp.where(first, rows[:, half:], rows[:, :half])
    else:
        outs[0][...] = rows


def finish_kernel(count, *refs):
    parts = refs[:count]
    inv, slab, tail, _, flux_out, out, held_flux, sems = refs[count:]
    side = index("gz")
    rows_x, _, width = slab.shape
    size, depth, _ = tail.shape
    columns = off_face(side, depth)
    tail_copy = pltpu.make_async_copy(
        tail.at[:, columns, :], out.at[rows_x - size :, columns, :], sems.at[2]
    )
    tail_copy.start()
    total = parts[0][...]
    if count == 2:
        total = total + parts[1][...]
    wide = jnp.concatenate([total, jnp.zeros((LANES - E, total.shape[1]), jnp.float32)], axis=0).T
    columns = []
    for start in range(0, width // E, LANES // E):
        column = wide[start * rows_x : (start + 1) * rows_x]
        for k in range(1, LANES // E):
            column = column + roll(wide[(start + k) * rows_x : (start + k + 1) * rows_x], k * E, 1)
        columns.append(column)
    flux = jnp.concatenate(columns, axis=1)
    held_flux[...] = flux[:, None, :]
    out_copy = pltpu.make_async_copy(held_flux, flux_out, sems.at[0])
    out_copy.start()
    added = (flux * inv[...])[:, None, :]
    row = lax.broadcasted_iota(jnp.int32, slab.shape, 1)
    slab[...] = slab[...] + jnp.where(row == side * (ROWS - 1), added, 0.0)
    top = pl.multiple_of(side * (out.shape[1] - ROWS), ROWS)
    copy = pltpu.make_async_copy(slab, out.at[:, pl.ds(top, ROWS), :], sems.at[1])
    copy.start()
    tail_copy.wait()
    out_copy.wait()
    copy.wait()


def put_side(cells, odd, messages, rows, first, last, c):
    halo = HALO * E
    lane = lane_ids(c)
    axis = c.ndim - 1
    low = jnp.where(lane < halo, first, roll(c, halo, axis))
    high = jnp.where(lane < halo, roll(last, halo, axis), roll(c, halo - (cells - HALO), axis))
    for number, message in enumerate(messages):
        message[rows] = choose(odd, low, high, number)


def side_edge_kernel(source, inv, *messages):
    rows_x, _, width = source.shape
    first, last = source[:, :, :LANES], source[:, :, width - LANES :]
    own = slice(HALO - 1, HALO - 1 + rows_x)
    put_side(width // E, index("gy") % 2, messages, own, first, last, inv[...])


def side_halo_kernel(nx, ny, depth, *refs):
    odd_x, odd_y = index("gx") % 2, index("gy") % 2
    got_x, messages = [r[...] for r in refs[:nx]], refs[nx + ny :]
    width = got_x[0].shape[1]
    rows_x = messages[0].shape[0] - 2 * (HALO - 1)
    for start, skip, edge in (
        (0, 1, from_low(odd_x, got_x)),
        (HALO - 1 + rows_x, 0, from_high(odd_x, got_x)),
    ):
        planes, compacts = row_layers(edge, depth)
        for k in range(HALO - 1):
            s, c = planes[k + skip], compacts[k + skip]
            first, last = s[:, :LANES], s[:, width - LANES :]
            put_side(width // E, odd_y, messages, start + k, first, last, c)


def widen(cells, ring, s, c, left, right):
    lane = lane_ids(right)
    width = HALO * E
    axis = right.ndim - 1
    zero = jnp.zeros_like(right)
    after = jnp.where(lane < width, right, zero)
    before = jnp.where(lane >= LANES - width, roll(left, LANES - width, axis), zero)
    pads = [after + before] if ring - cells == LANES // E else [after, before]
    own = jnp.where(lane < cells, c, zero)
    c_after = jnp.where((lane >= cells) & (lane < cells + HALO), roll(right, cells - width, axis), zero)
    c_before = jnp.where(
        (lane >= ring - HALO) & (lane < ring), roll(left, ring - HALO - width, axis), zero
    )
    return [s, *pads], own + c_after + c_before


def depth_edge_kernel(cells, ring, nx, ny, source, inv, *refs):
    odd_x, odd_y, side = index("gx") % 2, index("gy") % 2, index("gz")
    got_x, got_y, (two_out, one_out) = refs[:nx], refs[nx : nx + ny], refs[nx + ny :]
    rows_x, depth, width = source.shape
    wide = ring * E
    rows = two_out.shape[1]
    packs = jnp.zeros((rows, LANES), jnp.float32)

    def layer(message, z):
        lanes = message[HALO * depth + z % ROWS : HALO * depth + z % ROWS + 1, z // ROWS * LANES :]
        lanes = lanes[:, :LANES]
        lines = []
        for n in range(HALO):
            line = message[n * depth + z : n * depth + z + 1, :]
            compact = jnp.where(lane_ids(lanes) < 32, roll(lanes, -32 * n, 1), 0.0)
            lines.append(jnp.concatenate([line, compact], axis=1))
        return jnp.concatenate(lines, axis=0)

    for k in range(HALO):
        inner = lambda r: jnp.where(side == 0, r[:, depth - HALO + k, :], r[:, k, :])
        edges = [jnp.where(side == 0, layer(r, depth - HALO + k), layer(r, k)) for r in got_x]
        below, above = from_low(odd_x, edges), from_high(odd_x, edges)
        empty = jnp.zeros((rows - rows_x - 2 * HALO + 1, LANES), jnp.float32)
        beside = [jnp.concatenate([empty[:1], inner(r), empty], axis=0) for r in got_y]
        own = jnp.concatenate([inner(source), inner(inv)], axis=1)
        blank = jnp.zeros((rows - rows_x - 2 * HALO, width + LANES), jnp.float32)
        all_rows = jnp.concatenate([below, own, above, blank], axis=0)
        parts, compact = widen(
            cells, ring, all_rows[:, :width], all_rows[:, width:],
            from_low(odd_y, beside), from_high(odd_y, beside),
        )
        compact = jnp.where(lane_ids(compact) < ring, compact, 0.0)
        packs = packs + roll(compact, 32 * k, 1)
        out = jnp.concatenate(parts, axis=1)
        if k < 2:
            two_out[k] = out
        else:
            one_out[:, :wide] = out
    one_out[:, wide:] = packs


def assemble_kernel(cells, ring, nx, ny, source, inv, *refs):
    odd_x, odd_y = index("gx") % 2, index("gy") % 2
    got_x, got_y = refs[:nx], refs[nx : nx + ny]
    ext_s, ext_i, one, compacts, matrix = refs[nx + ny :]
    rows_x, depth, width = source.shape
    wide = ring * E
    all_z = depth + ROWS
    total = ext_s.shape[0]
    matrix[...] = spread_matrix(ring, wide)
    def place(x, s, c, got):
        parts, compact = widen(cells, ring, s, c, from_low(odd_y, got), from_high(odd_y, got))
        first = pl.ds(pl.multiple_of(x * all_z, ROWS), depth)
        compacts[first, :] = compact
        at = 0
        for part in parts:
            ext_s[first, at : at + part.shape[1]] = part
            at += part.shape[1]

    def own(x, _):
        place(x + HALO, source[x], inv[x], [r[x + HALO - 1] for r in got_y])
        return 0

    repeat(0, rows_x, own, 32)
    got = [r[...] for r in got_x]
    for base, skip, edge in ((0, 0, from_low(odd_x, got)), (rows_x + HALO, 2, from_high(odd_x, got))):
        planes, compact = row_layers(edge, depth)
        for k in range(HALO):
            if k == skip:
                beside = [jnp.zeros((depth, LANES), jnp.float32) for _ in got_y]
            else:
                beside = [r[base + k - 1] for r in got_y]
            place(base + k, planes[k], compact[k], beside)
    chunk = max(n for n in range(2 * ROWS, 321, 2 * ROWS) if total % n == 0)

    def expand(n, _):
        rows = pl.ds(pl.multiple_of(n * chunk, 2 * ROWS), chunk)
        some = packed(compacts[rows, :], ring)
        inverse = jnp.dot(some, matrix[...], preferred_element_type=jnp.float32)
        ext_i[rows, :] = inverse
        one[rows, :] = ext_s[rows, :] * inverse
        return 0

    repeat(0, total // chunk, expand, 5)


def depth_rows_kernel(ring, z_two, z_one, _s, _i, _o, ext_s, ext_i, one, compacts, inverses, matrix):
    all_x = compacts.shape[0] // ROWS
    all_z = ext_s.shape[0] // all_x
    depth, wide = all_z - ROWS, ring * E
    matrix[...] = spread_matrix(ring, wide)
    start = index("gz") * (ROWS - HALO)

    def rest(x):
        return pl.ds(pl.multiple_of(x * all_z + depth, ROWS), ROWS)

    def tile_of(x):
        return pl.ds(pl.multiple_of(x * ROWS, ROWS), ROWS)

    def spaced(rows):
        at = lax.broadcasted_iota(jnp.int32, (ROWS, rows[0].shape[1]), 0) - start
        tile = jnp.zeros(at.shape, jnp.float32)
        for k, value in enumerate(rows):
            tile = jnp.where(at == k, value, tile)
        return tile

    def zone(x, _):
        last = z_one[pl.ds(x, 1), :]
        ext_s[rest(x), :] = spaced(
            [z_two[0, pl.ds(x, 1), :], z_two[1, pl.ds(x, 1), :], last[:, :wide]]
        )
        packs = jnp.broadcast_to(last[:, wide:], (ROWS, LANES))
        compacts[tile_of(x), :] = spaced([roll(packs, -32 * k, 1) for k in range(HALO)])
        return 0

    def spread_out(x, _):
        i = inverses[tile_of(x), :]
        ext_i[rest(x), :] = i
        one[rest(x), :] = ext_s[rest(x), :] * i
        return 0

    repeat(0, all_x, zone, 38)
    some = packed(compacts[...], ring)
    inverses[...] = jnp.dot(some, matrix[...], preferred_element_type=jnp.float32)
    repeat(0, all_x, spread_out, 38)


def repeat(first, last, step, most):
    count = last - first
    unroll = max(n for n in range(1, most + 1) if count % n == 0)
    lax.fori_loop(first, last, step, 0, unroll=unroll)


def swept(ext_s, ext_i, old, x, all_z, depth, width, store):
    at = lambda x, rows: pl.ds(pl.multiple_of(x * all_z, ROWS), rows)
    tiles = old.shape[1] // LANES
    lane = lax.broadcasted_iota(jnp.int32, (depth, LANES), 1)
    known = {}

    def tile(j):
        j %= tiles
        if j not in known:
            u = old[at(x, all_z), j * LANES : (j + 1) * LANES]
            known[j] = (u, roll(u[:depth], E, 1), roll(u[:depth], -E, 1))
        return known[j]

    for j in range(width // LANES):
        columns = slice(j * LANES, (j + 1) * LANES)
        here = tile(j)
        beside = old[at(x - 1, depth), columns] + old[at(x + 1, depth), columns]
        up = roll(here[0], 1, 0) + roll(here[0], -1, 0)
        side = jnp.where(lane < E, tile(j - 1)[1], here[1])
        side = side + jnp.where(lane >= LANES - E, tile(j + 1)[2], here[2])
        beside = beside + (up[:depth] + side)
        new = (ext_s[at(x, depth), columns] + beside) * ext_i[at(x, depth), columns]
        store(columns, new)


def sweep_kernel(all_z, first, last, ext_s, ext_i, old, *refs):
    new = refs[-1]

    def step(x, _):
        def store(columns, value):
            new[pl.ds(pl.multiple_of(x * all_z, ROWS), all_z), columns] = value

        swept(ext_s, ext_i, old, x, all_z, all_z, old.shape[1], store)
        return 0

    repeat(first, last, step, 36)


def off_face(side, depth):
    return pl.ds(pl.multiple_of((1 - side) * ROWS, ROWS), depth - ROWS)


def last_sweep_kernel(pieces, ext_s, ext_i, old, out, slab, tail, done, sems):
    side = index("gz")
    rows_x, depth, width = out.shape
    all_z = depth + ROWS
    size = rows_x // pieces
    copies = []
    for n in range(pieces):
        target, shift = (tail, n * size) if n == pieces - 1 else (done, 0)

        def step(x, _, target=target, shift=shift):
            def store(columns, value):
                target[x - shift, :, columns] = value
                slab[x, :, columns] = jnp.where(side == 0, value[:ROWS], value[depth - ROWS :])

            swept(ext_s, ext_i, old, x + HALO, all_z, depth, width, store)
            return 0

        repeat(n * size, (n + 1) * size, step, 8)
        if n < pieces - 1:
            rows, columns = slice(n * size, (n + 1) * size), off_face(side, depth)
            copies.append(
                pltpu.make_async_copy(done.at[rows, columns, :], out.at[rows, columns, :], sems.at[n])
            )
            copies[-1].start()
    for copy in copies:
        copy.wait()


def body(source, coef, face_trace, near_col, far_col, near_tile, far_u, far_v):
    rows_x, depth, width = source.shape
    cells = coef.shape[2]
    groups = lax.axis_size("gy")
    size_x = lax.axis_size("gx")
    tile = near_tile.shape[3]
    count = far_u.shape[3]
    rank = far_u.shape[4]
    nx, ny = message_count("gx"), message_count("gy")
    bf16 = jnp.bfloat16
    both = [(0, 1), (1, 0)]
    pad = LANES if groups == 2 else 2 * LANES
    ring = (width + pad) // E
    wide = width + pad
    all_x, all_z = rows_x + 2 * HALO, depth + ROWS
    part = rows_x * cells
    halves = groups == 2
    coef = coef.transpose(0, 2, 1)

    held_source, held_trace, inv, near, *vol_x = call(
        face_start_kernel, (kept(source), kept(coef), kept(face_trace)),
        [vector(source.shape), vector(face_trace.shape, jnp.int32), vector((rows_x, depth, LANES)),
          vector((NEAR * rows_x + ROWS, width))]
        + [vector((HALO * depth + ROWS, width))] * nx,
        in_specs=[MAIN] * 3,
        scratch=(vector(coef.shape), pltpu.SemaphoreType.DMA((3,))),
    )
    if halves:
        other = held(lax.ppermute(near, "gy", both))
    else:
        other = held(lax.all_gather(near, "gy", axis=0, tiled=False))
    got_vol_x = swap(vol_x, "gx")
    full = vector((NEAR, rows_x, width * groups))
    s_face, i_face, i_own, *face_x = call(
        functools.partial(face_side_kernel, groups), (near, other),
        [full, full, vector((rows_x, width))]
        + [vector((ROWS, width * groups))] * nx, work=500,
    )
    got_x = swap(face_x, "gx")
    (order,) = call(order_kernel, (held_trace,), [vector((tile, tile), bf16)], after=(near,))
    sides = [vector((all_x - 2, depth, LANES))] * ny
    vol_y = call(side_edge_kernel, (held_source, inv), sides, after=(near,))
    vol_y = call(
        functools.partial(side_halo_kernel, nx, ny, depth), (*got_vol_x, *vol_y), sides,
        after=(order, *got_x), input_output_aliases={nx + n: n for n in range(ny)},
    )
    got_vol_y = swap(vol_y, "gy")

    ext = pltpu.VMEM((2, rows_x + 2 * ROWS, width * groups + LANES), jnp.float32)
    (traces,) = call(
        functools.partial(face_trace_kernel, nx), (s_face, i_face, order, *got_x),
        [vector((1, E, tile), bf16)], scratch=(ext, ext),
    )
    steps = doubling(size_x)
    for step in steps:
        other = held(lax.ppermute(traces, "gx", [(i, i ^ step) for i in range(size_x)]))
        twice = (2 * traces.shape[0], E, tile)
        before = ()
        if step == steps[0]:
            (spot,) = call(
                spot_kernel, (near_col, far_col), [pltpu.SMEM((count + 1,), jnp.int32)],
                in_specs=[SCALAR, SCALAR], out_specs=[SCALAR], after=(traces,),
            )
            before = (spot,)
        if step == steps[-2]:
            near, far_rows = call(
                row_order_kernel,
                (order, held(near_tile.reshape(tile, tile)), held(far_u.reshape(count * rank, tile))),
                [vector((tile, tile), bf16), vector((count * rank, tile), bf16)], work=3000,
                after=(traces,),
            )
            before = (*before, near)
        if step == 1:
            rounded = -(-all_x // ROWS) * ROWS
            vol_z = call(
                functools.partial(depth_edge_kernel, cells, ring, nx, ny),
                (held_source, inv, *got_vol_x, *got_vol_y),
                [vector((2, rounded, wide)), vector((rounded, wide + LANES))], work=500,
                after=(traces,),
            )
            got_vol_z = [held(lax.ppermute(v, "gz", both)) for v in vol_z]
            ext = vector((all_x * all_z, wide))
            most = call(
                functools.partial(assemble_kernel, cells, ring, nx, ny),
                (held_source, inv, *got_vol_x, *got_vol_y), [ext, ext, ext],
                scratch=(vector((all_x * all_z, LANES)), vector((LANES, wide), bf16)),
                after=vol_z,
            )
            ext_s, ext_i, one = call(
                functools.partial(depth_rows_kernel, ring), (*got_vol_z, *most), [ext, ext, ext],
                scratch=(
                    vector((all_x * ROWS, LANES)), vector((all_x * ROWS, wide)),
                    vector((LANES, wide), bf16),
                ),
                input_output_aliases={2: 0, 3: 1, 4: 2},
            )
            (two,) = call(
                functools.partial(sweep_kernel, all_z, 1, all_x - 1), (ext_s, ext_i, one), [ext],
                work=2500,
            )
            before = (two,)
        (traces,) = call(
            join_kernel, (traces, other), [vector(twice, bf16)], work=300, after=before
        )
    other = held(lax.ppermute(traces, "gz", both))
    middle = 2 + (all_x - 4) * 2 // 3
    (three,) = call(
        functools.partial(sweep_kernel, all_z, 2, middle), (ext_s, ext_i, two), [ext], work=1400,
        after=(traces,),
    )

    rows = call(
        functools.partial(operator_kernel, halves),
        (spot, traces, other, near, held(far_v.reshape(count * rank, tile)), far_rows),
        [vector((E, part))] * 2 if halves else [plain((E, tile))],
        in_specs=[SCALAR] + [VECTOR] * 5, work=2500, after=(three,),
    )
    if halves:
        sums = (rows[0], held(lax.ppermute(rows[1], "gy", both)))
    else:
        sums = (held(lax.psum_scatter(rows[0], "gy", scatter_dimension=1, tiled=True)),)
    (three,) = call(
        functools.partial(sweep_kernel, all_z, middle, all_x - 2), (ext_s, ext_i, two, three), [ext],
        work=1400, input_output_aliases={3: 0}, after=rows,
    )
    pieces = 4
    size = rows_x // pieces
    field, slab, tail = call(
        functools.partial(last_sweep_kernel, pieces), (ext_s, ext_i, three),
        [plain(source.shape), vector((rows_x, ROWS, width)), vector((size, depth, width))],
        out_specs=[MAIN, VECTOR, VECTOR], work=2000,
        scratch=(vector((rows_x - size, depth, width)), pltpu.SemaphoreType.DMA((pieces - 1,))),
    )

    flux, result = call(
        functools.partial(finish_kernel, len(sums)), (*sums, i_own, slab, tail, field),
        [plain((rows_x, 1, width)), plain(source.shape)],
        in_specs=[VECTOR] * (len(sums) + 3) + [MAIN], out_specs=[MAIN, MAIN],
        scratch=(vector((rows_x, 1, width)), pltpu.SemaphoreType.DMA((3,))),
        input_output_aliases={len(sums) + 3: 1},
    )
    return (result, flux)


def solution(mesh):
    return jax.shard_map(
        body,
        mesh=mesh,
        in_specs=(
            P("gx", "gz", "gy"),
            P("gx", "gz", "gy"),
            P("gx", "gz", None),
            P("gx", "gz", "gy"),
            P("gx", "gz", "gy", None),
            P("gx", "gz", "gy", None, None),
            P("gx", "gz", "gy", None, None, None),
            P("gx", "gz", "gy", None, None, None),
        ),
        out_specs=(P("gx", "gz", "gy"), P("gx", "gz", "gy")),
        check_vma=False,
    )
```
